32 devices in a mesh: gx: 8 (over z, y), gy: 4 (over x, core).
Axes of the slice: x: 2, y: 2, z: 4, core: 2. Of those that a mesh axis runs over, the one named last changes fastest.
Arguments:
- layer_input: bfloat16 [8192, 2560], P('gx'), may hold values from -6 to 6
- norm_gain: float32 [2560], replicated, may hold values from 0.5 to 1.5
- gate_weight: bfloat16 [2560, 5120], P('gx', 'gy'), may hold values from -0.125 to 0.125
- value_weight: bfloat16 [2560, 5120], P('gx', 'gy'), may hold values from -0.125 to 0.125
- state_weight: bfloat16 [2560, 256], P('gx'), may hold values from -0.125 to 0.125
- step_weight: bfloat16 [2560, 80], P('gx', 'gy'), may hold values from -0.125 to 0.125
- conv_value: float32 [4, 5120], P(None, 'gy'), may hold values from -3 to 3
- conv_value_bias: float32 [5120], P('gy'), may hold values from -1.5 to 1.5
- conv_state: float32 [4, 256], replicated, may hold values from -3 to 3
- conv_state_bias: float32 [256], replicated, may hold values from -1.5 to 1.5
- step_bias: float32 [80], P('gy'), may hold values from -6.5 to -2
- decay_log: float32 [80], P('gy'), may hold values from 0 to 2.7
- skip_scale: float32 [80], P('gy'), may hold values from 0.5 to 1.5
- gated_gain: float32 [5120], P('gy'), may hold values from 0.5 to 1.5
- out_weight: bfloat16 [5120, 2560], P('gy', 'gx'), may hold values from -0.125 to 0.125
- segment_ids: int32 [8192], P('gx'), may hold values from 0 to 20, as said below
- cotangent: bfloat16 [8192, 2560], P('gx', 'gy'), may hold values from -6 to 6
Outputs:
- layer_output: bfloat16 [8192, 2560], P('gx', 'gy')
- grad_input: float32 [8192, 2560], P('gx', 'gy')
- grad_norm_gain: float32 [2560], P('gy')
- grad_gate_weight: float32 [2560, 5120], P('gx', 'gy')
- grad_value_weight: float32 [2560, 5120], P('gx', 'gy')
- grad_state_weight: float32 [2560, 256], P('gx')
- grad_step_weight: float32 [2560, 80], P('gx', 'gy')
- grad_conv_value: float32 [4, 5120], P(None, 'gy')
- grad_conv_value_bias: float32 [5120], P('gy')
- grad_conv_state: float32 [4, 256], replicated
- grad_conv_state_bias: float32 [256], replicated
- grad_step_bias: float32 [80], P('gy')
- grad_decay_log: float32 [80], P('gy')
- grad_skip_scale: float32 [80], P('gy')
- grad_gated_gain: float32 [5120], P('gy')
- grad_out_weight: float32 [5120, 2560], P('gy', 'gx')
The draws below stay inside these ranges and needn't reach their ends.
Inputs may be any that keep to these rules, and one draw needn't show every extreme that they name: `segment_ids`: within each packed row of 1024 tokens the ids count documents from 0 upward and never fall; every document holds 51 to 512 tokens, except that the last one of a row may be shorter.
All inputs are finite; a program needn't handle non-finite values.
Results may differ from the reference program's by a relative error of at most 0.011.
Values may be sent and summed in bfloat16 or wider, within the bound.
No kernel may reach another device: no remote copies, remote signals or barrier semaphores. Data moves between devices by JAX's collectives and lax.ppermute only.
A program may use at most 256 MiB of HBM per device.

```python
import jax
import jax.numpy as jnp
from jax import lax

D = 2560
HEADS = 80
STATE = 128
KCONV = 4
GROUP = 256
SEQ = 1024
INNER = 5120
TOKENS = 8192


def draw_segment_ids(key, part):
    key = jax.random.fold_in(key, 7)
    length_key, row_key = jax.random.split(key)
    row_count = TOKENS // SEQ
    shortest = SEQ // 20
    doc_slots = SEQ // shortest + 1
    lengths = jax.random.randint(length_key, (row_count, doc_slots), shortest, SEQ // 2 + 1)
    chosen = jax.random.randint(row_key, (), 0, row_count)
    row_numbers = jnp.arange(row_count, dtype=jnp.int32)
    lengths = jnp.where((row_numbers == chosen)[:, None], shortest, lengths)
    doc_ends = jnp.cumsum(lengths, axis=1)
    positions = jnp.arange(SEQ, dtype=jnp.int32)
    doc_ids = jnp.sum((positions[None, :, None] >= doc_ends[:, None, :]).astype(jnp.int32), axis=2)
    return doc_ids.reshape(TOKENS).astype(jnp.int32)


def raised(values, stream_key, source, target, blocks, factor):
    owner, partner = [(jnp.arange(values.shape[position]) // (values.shape[position] // blocks)).reshape([-1 if axis == position else 1 for axis in range(values.ndim)]) for position in (source, target)]
    chosen = jax.random.permutation(stream_key, blocks)[partner]
    strong = (owner == chosen) | (owner == (partner + blocks // 2) % blocks)
    return jnp.where(strong, factor * values, values)


def block_levels(key, dims, pieces, least, top_value):
    gain = 1.0
    for position, blocks in pieces:
        heights = jax.random.uniform(jax.random.fold_in(jax.random.fold_in(key, 6), position), (blocks,), jnp.float32, least / len(pieces), top_value / len(pieces))
        gain = gain * jnp.repeat(jnp.exp(heights), dims[position] // blocks).reshape((-1,) + (1,) * (len(dims) - 1 - position))
    return gain


def noise(stream_key, extent, spread, reach, shards=(), held_as=jnp.bfloat16):
    entries = spread * jax.random.normal(stream_key, extent, jnp.float32)
    if shards:
        entries = entries * block_levels(stream_key, extent, shards, -0.22, 0.18)
    return jnp.clip(entries, -reach, reach).astype(held_as)


def heavy_noise(stream_key, shape, width, bound, cuts, heavy, kind=jnp.bfloat16):
    values = width * jax.random.normal(stream_key, shape, jnp.float32)
    if cuts:
        values = values * block_levels(stream_key, shape, cuts, -0.22, 0.18)
    return jnp.clip(raised(values, jax.random.fold_in(stream_key, 3), *heavy), -bound, bound).astype(kind)


def setup_inputs(seed: int = 0) -> dict:
    splits = jax.random.split(jax.random.key(seed), 18)
    return {
        "layer_input": noise(splits[0], (TOKENS, D), 1.0, 6.0, ((0, 8),)),
        "norm_gain": jnp.clip(1.0 + 0.1 * jax.random.normal(splits[1], (D,), jnp.float32), 0.5, 1.5),
        "gate_weight": noise(splits[2], (D, INNER), D ** -0.5, 0.125, ((0, 8), (1, 4))),
        "value_weight": noise(splits[3], (D, INNER), D ** -0.5, 0.125, ((0, 8), (1, 4))),
        "state_weight": noise(splits[4], (D, 2 * STATE), D ** -0.5, 0.125, ((0, 8),)),
        "step_weight": noise(splits[5], (D, HEADS), D ** -0.5, 0.125, ((0, 8), (1, 4))),
        "conv_value": noise(splits[6], (KCONV, INNER), KCONV ** -0.5, 3.0, ((1, 4),), jnp.float32),
        "conv_value_bias": noise(splits[7], (INNER,), 0.3, 1.5, ((0, 4),), jnp.float32),
        "conv_state": noise(splits[8], (KCONV, 2 * STATE), KCONV ** -0.5, 3.0, (), jnp.float32),
        "conv_state_bias": noise(splits[9], (2 * STATE,), 0.3, 1.5, (), jnp.float32),
        "step_bias": jnp.clip(-6.5 + 4.5 * jax.random.uniform(splits[10], (HEADS,), jnp.float32) ** block_levels(splits[10], (HEADS,), ((0, 4),), -0.2, 0.2), -6.5, -2.0),
        "decay_log": jnp.clip(2.7 * jax.random.uniform(splits[11], (HEADS,), jnp.float32) ** block_levels(splits[11], (HEADS,), ((0, 4),), -0.2, 0.2), 0.0, 2.7),
        "skip_scale": jnp.clip(0.5 + 1.0 * jax.random.uniform(splits[12], (HEADS,), jnp.float32) ** block_levels(splits[12], (HEADS,), ((0, 4),), -0.2, 0.2), 0.5, 1.5),
        "gated_gain": jnp.clip(1.0 + 0.1 * jax.random.normal(splits[13], (INNER,), jnp.float32), 0.5, 1.5),
        "out_weight": heavy_noise(splits[14], (INNER, D), INNER ** -0.5, 0.125, ((0, 4), (1, 8)), (0, 1, 8, 2.0)),
        "segment_ids": draw_segment_ids(jax.random.fold_in(splits[17], 71), 0),
        "cotangent": noise(splits[16], (TOKENS, D), 1.0, 6.0, ((0, 8), (1, 4))),
    }


epsilon = 1e-05
highest = lax.Precision.HIGHEST

@jax.custom_vjp
def low(v):
    return lax.optimization_barrier(v.astype(jnp.bfloat16)).astype(jnp.float32)

@jax.custom_vjp
def low_back(v):
    return v

def low_keep(v):
    return (low(v), None)

def low_pass(kept, grad):
    return (grad,)

def back_keep(v):
    return (v, None)

def back_low(kept, grad):
    return (low(grad),)
low.defvjp(low_keep, low_pass)
low_back.defvjp(back_keep, back_low)

def product_high(left, right):
    return jnp.dot(left, right, precision=highest)

def causal_conv(values, kernel, offset_bias, segments):
    seq_len = values.shape[0]
    total = offset_bias + kernel[0] * values
    for offset in range(1, kernel.shape[0]):
        moved = jnp.concatenate([jnp.zeros((offset, values.shape[1]), values.dtype), values[:seq_len - offset]], 0)
        moved_seg = jnp.concatenate([jnp.full((offset,), -1, jnp.int32), segments[:seq_len - offset]], 0)
        same_doc = (moved_seg == segments).astype(values.dtype)
        total = total + kernel[offset] * moved * same_doc[:, None]
    return total

def group_step(running, inputs):
    memory, previous = running
    x_block, b_block, c_block, decay_rate, step_size, seg_block = inputs
    block_len = seg_block.shape[0]
    cumulative = jnp.cumsum(decay_rate, axis=0)
    row_index = lax.broadcasted_iota(jnp.int32, (block_len, block_len), 0)
    col_index = lax.broadcasted_iota(jnp.int32, (block_len, block_len), 1)
    visible = (row_index >= col_index) & (seg_block[:, None] == seg_block[None, :])
    log_decay = cumulative.T[:, :, None] - cumulative.T[:, None, :]
    decay_mask = jnp.where(visible[None], jnp.exp(jnp.where(visible[None], log_decay, 0.0)), 0.0)
    intersection = product_high(c_block, b_block.T)
    mixing = decay_mask * intersection[None] * step_size.T[:, None, :]
    within = jnp.einsum('hts,shp->thp', mixing, x_block, precision=highest)
    carried = (seg_block == previous).astype(memory.dtype)
    from_state = jnp.einsum('tn,hpn->thp', c_block, memory, precision=highest)
    from_state = from_state * (jnp.exp(cumulative) * carried[:, None])[:, :, None]
    last_seg = seg_block[block_len - 1]
    tail_weight = (seg_block == last_seg).astype(memory.dtype)[:, None] * jnp.exp(cumulative[block_len - 1][None, :] - cumulative) * step_size
    fresh_state = jnp.einsum('sh,shp,sn->hpn', tail_weight, x_block, b_block, precision=highest)
    survives = (last_seg == previous).astype(memory.dtype)
    memory = survives * jnp.exp(cumulative[block_len - 1])[:, None, None] * memory + fresh_state
    return ((memory, last_seg), within + from_state)

def ssm_mixer(projected, conv_value, conv_value_bias, conv_state, conv_state_bias, step_bias, decay_log, skip_scale, segments):
    inner_width = conv_value.shape[1]
    head_count = step_bias.shape[0]
    head_dim = inner_width // head_count
    states = conv_state.shape[1] // 2
    seq_len = projected.shape[0]
    blocks = seq_len // GROUP
    gate_in = projected[:, :inner_width]
    value_in = projected[:, inner_width:2 * inner_width]
    state_in = projected[:, 2 * inner_width:2 * inner_width + 2 * states]
    step_in = projected[:, 2 * inner_width + 2 * states:]
    values = jax.nn.silu(causal_conv(value_in, conv_value, conv_value_bias, segments))
    state_act = jax.nn.silu(causal_conv(state_in, conv_state, conv_state_bias, segments))
    step_size = jax.nn.softplus(step_in + step_bias)
    decay_rate = -jnp.exp(decay_log) * step_size
    inputs = (values.reshape(blocks, GROUP, head_count, head_dim), state_act[:, :states].reshape(blocks, GROUP, states), state_act[:, states:].reshape(blocks, GROUP, states), decay_rate.reshape(blocks, GROUP, head_count), step_size.reshape(blocks, GROUP, head_count), segments.reshape(blocks, GROUP))
    initial = (jnp.zeros((head_count, head_dim, states), projected.dtype), jnp.array(-1, jnp.int32))
    finished, outputs = lax.scan(jax.checkpoint(group_step), initial, inputs)
    combined = outputs.reshape(seq_len, head_count, head_dim) + skip_scale[None, :, None] * values.reshape(seq_len, head_count, head_dim)
    return combined.reshape(seq_len, inner_width) * jax.nn.silu(gate_in)

def forward(params, tokens, segments):
    norm_gain, gate_weight, value_weight, state_weight, step_weight, conv_value, conv_value_bias, conv_state, conv_state_bias, step_bias, decay_log, skip_scale, gated_gain, out_weight = params
    scale_in = lax.rsqrt(lax.optimization_barrier(jnp.mean(tokens * tokens, axis=1, keepdims=True)) + epsilon)
    normed = low(tokens * scale_in * norm_gain)
    projected = low_back(product_high(normed, jnp.concatenate([gate_weight, value_weight, state_weight, step_weight], 1)))
    gated = ssm_mixer(projected, conv_value, conv_value_bias, conv_state, conv_state_bias, step_bias, decay_log, skip_scale, segments)
    scale_out = lax.rsqrt(lax.optimization_barrier(jnp.mean(gated * gated, axis=1, keepdims=True)) + epsilon)
    scaled = low(gated * gated_gain)
    return tokens + scale_out * low_back(product_high(scaled, out_weight))

def reference(layer_input, norm_gain, gate_weight, value_weight, state_weight, step_weight, conv_value, conv_value_bias, conv_state, conv_state_bias, step_bias, decay_log, skip_scale, gated_gain, out_weight, segment_ids, cotangent):
    params = tuple((argument.astype(jnp.float32) for argument in (norm_gain, gate_weight, value_weight, state_weight, step_weight, conv_value, conv_value_bias, conv_state, conv_state_bias, step_bias, decay_log, skip_scale, gated_gain, out_weight)))
    row_count = TOKENS // SEQ
    inputs = (layer_input.astype(jnp.float32).reshape(row_count, SEQ, D), segment_ids.reshape(row_count, SEQ).astype(jnp.int32), cotangent.astype(jnp.float32).reshape(row_count, SEQ, D))
    totals = jax.tree.map(jnp.zeros_like, params)

    def one_row(running, row_data):
        tokens, segments, upstream = row_data
        result, pullback = jax.vjp(lambda weights, values: forward(weights, values, segments), params, tokens)
        weight_grads, grad_tokens = pullback(upstream)
        return (jax.tree.map(jnp.add, running, weight_grads), (result, grad_tokens))
    summed, (results, grad_rows) = lax.scan(one_row, totals, inputs)
    return (results.reshape(TOKENS, D).astype(jnp.bfloat16), grad_rows.reshape(TOKENS, D), summed[0], summed[1], summed[2], summed[3], summed[4], summed[5], summed[6], summed[7], summed[8], summed[9], summed[10], summed[11], summed[12], summed[13])
```

```python
import jax
import jax.numpy as jnp
from jax import lax
from jax.sharding import PartitionSpec as P

GROUP = 256
INNER = 5120


epsilon = 1e-05
highest = lax.Precision.HIGHEST


def causal_conv(values, kernel, offset_bias, segments):
    seq_len = values.shape[0]
    total = offset_bias + kernel[0] * values
    for offset in range(1, kernel.shape[0]):
        moved = jnp.concatenate(
            [jnp.zeros((offset, values.shape[1]), values.dtype), values[: seq_len - offset]], 0
        )
        moved_seg = jnp.concatenate(
            [jnp.full((offset,), -1, jnp.int32), segments[: seq_len - offset]], 0
        )
        same_doc = (moved_seg == segments).astype(values.dtype)
        total = total + kernel[offset] * moved * same_doc[:, None]
    return total


def group_step(running, inputs):
    memory, previous = running
    x_block, b_block, c_block, decay_rate, step_size, seg_block = inputs
    block_len = seg_block.shape[0]
    cumulative = jnp.cumsum(decay_rate, axis=0)
    row_index = lax.broadcasted_iota(jnp.int32, (block_len, block_len), 0)
    col_index = lax.broadcasted_iota(jnp.int32, (block_len, block_len), 1)
    visible = (row_index >= col_index) & (seg_block[:, None] == seg_block[None, :])
    log_decay = cumulative.T[:, :, None] - cumulative.T[:, None, :]
    decay_mask = jnp.where(visible[None], jnp.exp(jnp.where(visible[None], log_decay, 0.0)), 0.0)
    intersection = jnp.dot(c_block, b_block.T, precision=highest)
    mixing = decay_mask * intersection[None] * step_size.T[:, None, :]
    within = jnp.einsum("hts,shp->thp", mixing, x_block, precision=highest)
    carried = (seg_block == previous).astype(memory.dtype)
    from_state = jnp.einsum("tn,hpn->thp", c_block, memory, precision=highest)
    from_state = from_state * (jnp.exp(cumulative) * carried[:, None])[:, :, None]
    last_seg = seg_block[block_len - 1]
    tail_weight = (
        (seg_block == last_seg).astype(memory.dtype)[:, None]
        * jnp.exp(cumulative[block_len - 1][None, :] - cumulative)
        * step_size
    )
    fresh_state = jnp.einsum("sh,shp,sn->hpn", tail_weight, x_block, b_block, precision=highest)
    survives = (last_seg == previous).astype(memory.dtype)
    memory = survives * jnp.exp(cumulative[block_len - 1])[:, None, None] * memory + fresh_state
    return ((memory, last_seg), within + from_state)


def ssm_mixer(
    value_in,
    state_in,
    step_in,
    conv_value,
    conv_value_bias,
    conv_state,
    conv_state_bias,
    step_bias,
    decay_log,
    skip_scale,
    segments,
):
    inner_width = conv_value.shape[1]
    head_count = step_bias.shape[0]
    head_dim = inner_width // head_count
    states = conv_state.shape[1] // 2
    seq_len = value_in.shape[0]
    blocks = seq_len // GROUP
    values = jax.nn.silu(causal_conv(value_in, conv_value, conv_value_bias, segments))
    state_act = jax.nn.silu(causal_conv(state_in, conv_state, conv_state_bias, segments))
    step_size = jax.nn.softplus(step_in + step_bias)
    decay_rate = -jnp.exp(decay_log) * step_size
    inputs = (
        values.reshape(blocks, GROUP, head_count, head_dim),
        state_act[:, :states].reshape(blocks, GROUP, states),
        state_act[:, states:].reshape(blocks, GROUP, states),
        decay_rate.reshape(blocks, GROUP, head_count),
        step_size.reshape(blocks, GROUP, head_count),
        segments.reshape(blocks, GROUP),
    )
    initial = (jnp.zeros((head_count, head_dim, states), value_in.dtype), jnp.array(-1, jnp.int32))
    finished, outputs = lax.scan(jax.checkpoint(group_step), initial, inputs)
    combined = outputs.reshape(seq_len, head_count, head_dim) + skip_scale[
        None, :, None
    ] * values.reshape(seq_len, head_count, head_dim)
    return combined.reshape(seq_len, inner_width)


def contract_rows(left, right):
    return lax.dot_general(
        left, right, (((0,), (0,)), ((), ())), preferred_element_type=jnp.float32
    )


def contract_cols(left, right):
    return lax.dot_general(
        left, right, (((1,), (1,)), ((), ())), preferred_element_type=jnp.float32
    )


def scatter_rows(partial):
    return lax.psum_scatter(
        partial.astype(jnp.bfloat16), "gx", scatter_dimension=0, tiled=True
    ).astype(jnp.float32)


def on_device(
    layer_input,
    norm_gain,
    gate_weight,
    value_weight,
    state_weight,
    step_weight,
    conv_value,
    conv_value_bias,
    conv_state,
    conv_state_bias,
    step_bias,
    decay_log,
    skip_scale,
    gated_gain,
    out_weight,
    segment_ids,
    cotangent,
):
    model_width = layer_input.shape[1]
    col_width = cotangent.shape[1]
    state_cols = state_weight.shape[1]
    col_start = lax.axis_index("gy") * col_width

    full_value = lax.all_gather(value_weight, "gx", axis=0, tiled=True)
    full_state = lax.all_gather(
        jnp.concatenate([state_weight, step_weight], 1), "gx", axis=0, tiled=True
    )
    gate_weight, full_value = lax.optimization_barrier((gate_weight, full_value))
    full_gate = lax.all_gather(gate_weight, "gx", axis=0, tiled=True)
    out_rows, full_gate = lax.optimization_barrier((out_weight.T, full_gate))
    full_out = lax.all_gather(out_rows, "gx", axis=0, tiled=True)
    upstream = lax.all_gather(cotangent, "gy", axis=1, tiled=True)

    tokens = layer_input.astype(jnp.float32)
    scale_in = lax.rsqrt(jnp.mean(tokens * tokens, axis=1, keepdims=True) + epsilon)
    normed = (tokens * scale_in * norm_gain).astype(jnp.bfloat16)

    value_in = jnp.dot(normed, full_value, preferred_element_type=jnp.float32)
    state_step = jnp.dot(normed, full_state, preferred_element_type=jnp.float32)
    mixed, mixer_pull = jax.vjp(
        lambda *operands: ssm_mixer(*operands, segment_ids),
        value_in,
        state_step[:, :state_cols],
        state_step[:, state_cols:],
        conv_value,
        conv_value_bias,
        conv_state,
        conv_state_bias,
        step_bias,
        decay_log,
        skip_scale,
    )
    gate_in = jnp.dot(normed, full_gate, preferred_element_type=jnp.float32)
    gate_open = jax.nn.sigmoid(gate_in)
    gate_act = gate_in * gate_open
    gated = mixed * gate_act
    squares = lax.psum(jnp.sum(gated * gated, axis=1), "gy")
    scale_out = lax.rsqrt(squares / INNER + epsilon)[:, None]
    scaled = (gated * gated_gain).astype(jnp.bfloat16)

    scaled_out = (gated * gated_gain * scale_out).astype(jnp.bfloat16)
    grad_out = scatter_rows(contract_rows(upstream, scaled_out))

    up_back = jnp.dot(upstream, full_out, preferred_element_type=jnp.float32)
    grad_scale = lax.psum(jnp.sum(gated * gated_gain * up_back, axis=1), "gy")[:, None]
    grad_scaled = scale_out * up_back
    grad_gated = grad_scaled * gated_gain - grad_scale * scale_out**3 * gated / INNER
    gate_gain_part = jnp.sum(grad_scaled * gated, axis=0)
    grad_gate_in = (
        grad_gated * mixed * gate_open * (1.0 + gate_in * (1.0 - gate_open))
    ).astype(jnp.bfloat16)
    grad_gate = scatter_rows(contract_rows(normed, grad_gate_in))

    pulled = mixer_pull(grad_gated * gate_act)
    grad_value_in = pulled[0].astype(jnp.bfloat16)
    grad_state_in = jnp.concatenate([pulled[1], pulled[2]], 1).astype(jnp.bfloat16)
    grad_state_step = scatter_rows(contract_rows(normed, grad_state_in))
    grad_value = scatter_rows(contract_rows(normed, grad_value_in))

    product = lax.psum_scatter(
        (contract_cols(scaled, full_out) * scale_out).astype(jnp.bfloat16),
        "gy",
        scatter_dimension=1,
        tiled=True,
    )
    token_cols = lax.dynamic_slice_in_dim(layer_input, col_start, col_width, 1).astype(jnp.float32)
    layer_output = (token_cols + product.astype(jnp.float32)).astype(jnp.bfloat16)

    grad_normed_part = (
        contract_cols(grad_gate_in, full_gate)
        + contract_cols(grad_value_in, full_value)
        + contract_cols(grad_state_in, full_state)
    )
    grad_normed = lax.psum_scatter(
        grad_normed_part.astype(jnp.bfloat16), "gy", scatter_dimension=1, tiled=True
    ).astype(jnp.float32)
    gain_cols = lax.dynamic_slice_in_dim(norm_gain, col_start, col_width, 0)
    weighted = grad_normed * gain_cols
    inner_dot = lax.psum(jnp.sum(weighted * token_cols, axis=1), "gy")[:, None]
    grad_input = (
        cotangent.astype(jnp.float32)
        + scale_in * weighted
        - token_cols * scale_in**3 * inner_dot / model_width
    )
    norm_gain_part = jnp.sum(grad_normed * token_cols * scale_in, axis=0)
    conv_state_sum, conv_bias_sum = lax.psum((pulled[5], pulled[6]), ("gx", "gy"))
    grad_state = lax.psum(grad_state_step[:, :state_cols], "gy")
    small_sums = lax.psum(
        (norm_gain_part, gate_gain_part, pulled[3], pulled[4], pulled[7], pulled[8], pulled[9]),
        "gx",
    )
    return (
        layer_output,
        grad_input,
        small_sums[0],
        grad_gate,
        grad_value,
        grad_state,
        grad_state_step[:, state_cols:],
        small_sums[2],
        small_sums[3],
        conv_state_sum,
        conv_bias_sum,
        small_sums[4],
        small_sums[5],
        small_sums[6],
        small_sums[1],
        grad_out.T,
    )


def solution(mesh):
    return jax.shard_map(
        on_device,
        mesh=mesh,
        in_specs=(
            P("gx", None),
            P(),
            P("gx", "gy"),
            P("gx", "gy"),
            P("gx", None),
            P("gx", "gy"),
            P(None, "gy"),
            P("gy"),
            P(),
            P(),
            P("gy"),
            P("gy"),
            P("gy"),
            P("gy"),
            P("gy", "gx"),
            P("gx"),
            P("gx", "gy"),
        ),
        out_specs=(
            P("gx", "gy"),
            P("gx", "gy"),
            P("gy"),
            P("gx", "gy"),
            P("gx", "gy"),
            P("gx", None),
            P("gx", "gy"),
            P(None, "gy"),
            P("gy"),
            P(),
            P(),
            P("gy"),
            P("gy"),
            P("gy"),
            P("gy"),
            P("gy", "gx"),
        ),
        check_vma=False,
    )
```

```python
import functools

import jax
import jax.numpy as jnp
from jax import lax
from jax.experimental import pallas as pl
from jax.experimental.pallas import tpu as pltpu
from jax.sharding import PartitionSpec as P

INNER = 5120
SPAN = 128
LANES = 128
HALF = 64
LOG2E = 1.4426950408889634
VMEM_BYTES = 56 * 1024 * 1024

epsilon = 1e-05
highest = lax.Precision.HIGHEST
low = jnp.bfloat16
wide = jnp.float32


def dot(left, right, precision=None):
    return jnp.dot(left, right, preferred_element_type=wide, precision=precision)


def contract_rows(left, right, precision=None):
    return lax.dot_general(
        left, right, (((0,), (0,)), ((), ())), preferred_element_type=wide, precision=precision
    )


def contract_cols(left, right, precision=None):
    return lax.dot_general(
        left, right, (((1,), (1,)), ((), ())), preferred_element_type=wide, precision=precision
    )


def sigmoid(v):
    return 1.0 / (1.0 + jnp.exp(-v))


def softplus(v):
    return jnp.maximum(v, 0.0) + jnp.log1p(jnp.exp(-jnp.abs(v)))


def conv_in(v, taps, bias, masks):
    total = bias + taps[0:1] * v
    for k in range(1, 4):
        total = total + taps[k : k + 1] * (pltpu.roll(v, k, 0) * masks[k - 1])
    return total


def conv_back(grad, v, taps, masks):
    rows = grad.shape[0]
    back = taps[0:1] * grad
    sums = [jnp.sum(grad * v, axis=0, keepdims=True)]
    for k in range(1, 4):
        kept = grad * masks[k - 1]
        sums.append(jnp.sum(kept * pltpu.roll(v, k, 0), axis=0, keepdims=True))
        back = back + taps[k : k + 1] * pltpu.roll(kept, rows - k, 0)
    sums.append(jnp.sum(grad, axis=0, keepdims=True))
    return back, sums


def visible_block(seg_col, seg_row, row_is_query):
    shape = (SPAN, SPAN)
    first = lax.broadcasted_iota(jnp.int32, shape, 0)
    second = lax.broadcasted_iota(jnp.int32, shape, 1)
    ordered = (first >= second) if row_is_query else (first <= second)
    return ordered & (seg_col == seg_row)


def lower_triangle():
    shape = (SPAN, SPAN)
    return (
        lax.broadcasted_iota(jnp.int32, shape, 0) >= lax.broadcasted_iota(jnp.int32, shape, 1)
    ).astype(wide)


def prep_kernel(
    state_ref, step_ref, taps_ref, bias_ref, step_bias_ref, rate_ref, masks_ref, seg_col_ref,
    seg_row_ref, b_ref, c_ref, bt_ref, ct_ref, g_ref, gt_ref, dtx_ref, cumx_ref, cumt_ref,
):
    rows, states = b_ref.shape
    masks = [masks_ref[k] for k in range(3)]
    for part, (out, out_t) in enumerate(((b_ref, bt_ref), (c_ref, ct_ref))):
        cols = slice(part * states, (part + 1) * states)
        pre = conv_in(state_ref[:, cols], taps_ref[:, cols], bias_ref[:, cols], masks)
        act = pre * sigmoid(pre)
        out[...] = act.astype(low)
        out_t[...] = act.T.astype(low)
    step = softplus(step_ref[...] + step_bias_ref[...])
    triangle = lower_triangle()
    heads = lax.broadcasted_iota(jnp.int32, (LANES, dtx_ref.shape[1]), 0)
    channels = lax.broadcasted_iota(jnp.int32, (LANES, dtx_ref.shape[1]), 1)
    expand = (channels // HALF == heads).astype(wide)
    rate = step * (rate_ref[...] * LOG2E)
    for c in range(rows // SPAN):
        at = slice(c * SPAN, (c + 1) * SPAN)
        grams = dot(c_ref[at], bt_ref[:, at])
        g_ref[at] = jnp.where(visible_block(seg_col_ref[at], seg_row_ref[:, at], True), grams, 0.0)
        grams_t = dot(b_ref[at], ct_ref[:, at])
        gt_ref[at] = jnp.where(
            visible_block(seg_col_ref[at], seg_row_ref[:, at], False), grams_t, 0.0
        )
        total = dot(triangle, rate[at], highest)
        cumx_ref[at] = dot(total, expand, highest)
        dtx_ref[at] = dot(step[at], expand, highest)
        cumt_ref[:, at] = total.T


def decays(cumx_ref, cumt_ref, at, head, row_is_query):
    lane = head * HALF
    column = cumx_ref[at, lane : lane + 1]
    row = cumt_ref[0, head : head + 1, at]
    gap = (column - row) if row_is_query else (row - column)
    return jnp.exp2(jnp.minimum(gap, 0.0))


def split_heads(block):
    left = lax.broadcasted_iota(jnp.int32, block.shape, 1) < HALF
    zero = jnp.zeros_like(block)
    return jnp.concatenate([jnp.where(left, block, zero), jnp.where(left, zero, block)], 0)


def fwd_kernel(
    value_ref, taps_ref, bias_ref, skip_ref, dtx_ref, cumx_ref, cumt_ref, masks_ref, c_ref, bt_ref,
    g_ref, out_ref, x_scr,
):
    rows = value_ref.shape[0]
    masks = [masks_ref[k] for k in range(3)]
    pre = conv_in(value_ref[...], taps_ref[...], bias_ref[...], masks)
    x_scr[...] = pre * sigmoid(pre)
    state = jnp.zeros((c_ref.shape[1], LANES), wide)
    for c in range(rows // SPAN):
        at = slice(c * SPAN, (c + 1) * SPAN)
        x = x_scr[at]
        cum = cumx_ref[at]
        stepped = x * dtx_ref[at]
        mixing = jnp.concatenate(
            [decays(cumx_ref, cumt_ref, at, head, True) * g_ref[at] for head in (0, 1)], 1
        ).astype(low)
        y = dot(mixing, split_heads(stepped.astype(low)))
        if c > 0:
            y = y + dot(c_ref[at], state.astype(low)) * (jnp.exp2(cum) * masks_ref[3, at])
        out_ref[at] = y + skip_ref[...] * x
        if c + 1 < rows // SPAN:
            end = slice((c + 1) * SPAN - 1, (c + 1) * SPAN)
            last = cum[SPAN - 1 : SPAN]
            tail = jnp.exp2(last - cum) * masks_ref[4, at]
            fresh = dot(bt_ref[:, at], (stepped.astype(low) * tail).astype(low))
            state = (masks_ref[3, end] * jnp.exp2(last)) * state + fresh


def bwd_kernel(
    value_ref, mixed_ref, grad_ref, taps_ref, bias_ref, skip_ref, dtx_ref, cumx_ref, cumt_ref,
    masks_ref, b_ref, c_ref, bt_ref, ct_ref, gt_ref,
    value_out, sums_out, db_ref, dc_ref, dg_ref, z_ref, dt_ref,
    pre_scr, x_scr, dpre_scr, state_scr,
):
    rows = value_ref.shape[0]
    blocks = rows // SPAN
    pair = pl.program_id(0)
    masks = [masks_ref[k] for k in range(3)]

    @pl.when(pair == 0)
    def _():
        for ref in (db_ref, dc_ref, dg_ref, z_ref, dt_ref):
            ref[...] = jnp.zeros_like(ref)

    pre = conv_in(value_ref[...], taps_ref[...], bias_ref[...], masks)
    pre_scr[...] = pre
    x_scr[...] = pre * sigmoid(pre)
    state = jnp.zeros((c_ref.shape[1], LANES), wide)
    for c in range(blocks):
        at = slice(c * SPAN, (c + 1) * SPAN)
        state_scr[c] = state
        if c + 1 < blocks:
            end = slice((c + 1) * SPAN - 1, (c + 1) * SPAN)
            cum = cumx_ref[at]
            last = cum[SPAN - 1 : SPAN]
            tail = jnp.exp2(last - cum) * masks_ref[4, at]
            stepped = (x_scr[at] * dtx_ref[at]).astype(low)
            fresh = dot(bt_ref[:, at], (stepped * tail).astype(low))
            state = (masks_ref[3, end] * jnp.exp2(last)) * state + fresh

    lanes = lax.broadcasted_iota(jnp.int32, (LANES, LANES), 0)
    heads = lax.broadcasted_iota(jnp.int32, (LANES, LANES), 1)
    gather = (lanes // HALF + 2 * pair == heads).astype(low)
    row_number = lax.broadcasted_iota(jnp.int32, (SPAN, LANES), 0)
    grad_skip = jnp.zeros((1, LANES), wide)
    grad_state = jnp.zeros((c_ref.shape[1], LANES), wide)
    for c in reversed(range(blocks)):
        at = slice(c * SPAN, (c + 1) * SPAN)
        end = slice((c + 1) * SPAN - 1, (c + 1) * SPAN)
        x = x_scr[at]
        dtx = dtx_ref[at]
        cum = cumx_ref[at]
        grad = grad_ref[at]
        grad_low = grad.astype(low)
        stepped = (x * dtx).astype(low)
        y = mixed_ref[at] - skip_ref[...] * x
        grad_mix = contract_cols(split_heads(stepped), grad_low)
        mixing = []
        grams = dg_ref[at]
        for head in (0, 1):
            decay = decays(cumx_ref, cumt_ref, at, head, False)
            mixing.append((decay * gt_ref[at]).astype(low))
            grams = grams + decay * grad_mix[head * SPAN : (head + 1) * SPAN]
        dg_ref[at] = grams
        grad_stepped = dot(jnp.concatenate(mixing, 1), split_heads(grad_low))
        last = cum[SPAN - 1 : SPAN]
        at_end = jnp.zeros((1, LANES), wide)
        carry = masks_ref[3, end] * jnp.exp2(last)
        if c + 1 < blocks:
            tail = jnp.exp2(last - cum) * masks_ref[4, at]
            grad_state_low = grad_state.astype(low)
            from_tail = dot(b_ref[at], grad_state_low) * tail
            grad_stepped = grad_stepped + from_tail
            db_ref[at] += contract_cols((stepped * tail).astype(low), grad_state_low)
            at_end = jnp.sum(stepped.astype(wide) * from_tail, axis=0, keepdims=True)
            at_end = at_end + carry * jnp.sum(state_scr[c] * grad_state, axis=0, keepdims=True)
        if c > 0:
            reach = (grad * (jnp.exp2(cum) * masks_ref[3, at])).astype(low)
            dc_ref[at] += contract_cols(reach, state_scr[c].astype(low))
            grad_state = carry * grad_state + dot(ct_ref[:, at], reach)
        z = grad_low.astype(wide) * y - stepped.astype(wide) * grad_stepped
        z = z + jnp.where(row_number == SPAN - 1, at_end, 0.0)
        z_high = z.astype(low)
        z_low = (z - z_high.astype(wide)).astype(low)
        z_ref[at] += dot(z_high, gather) + dot(z_low, gather)
        dt_ref[at] += dot((x * grad_stepped).astype(low), gather)
        grad_skip = grad_skip + jnp.sum(grad * x, axis=0, keepdims=True)
        pre_c = pre_scr[at]
        opened = sigmoid(pre_c)
        grad_x = grad_stepped * dtx + skip_ref[...] * grad
        dpre_scr[at] = grad_x * opened * (1.0 + pre_c * (1.0 - opened))

    back, sums = conv_back(dpre_scr[...], value_ref[...], taps_ref[...], masks)
    value_out[...] = back.astype(low)
    sums_out[...] = jnp.concatenate(sums + [grad_skip, jnp.zeros((2, LANES), wide)], 0)


def post_kernel(
    state_ref, step_ref, taps_ref, bias_ref, step_bias_ref, rate_ref, masks_ref, seg_col_ref,
    seg_row_ref, b_ref, c_ref, db_ref, dc_ref, dg_ref, z_ref, dt_ref,
    state_out, step_out, state_sums, step_sums, act_scr,
):
    rows, states = b_ref.shape
    masks = [masks_ref[k] for k in range(3)]
    triangle = lower_triangle()
    for c in range(rows // SPAN):
        at = slice(c * SPAN, (c + 1) * SPAN)
        seen = visible_block(seg_col_ref[at], seg_row_ref[:, at], False)
        grams = jnp.where(seen, dg_ref[at], 0.0)
        act_scr[0, at] = db_ref[at] + dot(grams.astype(low), c_ref[at])
        act_scr[1, at] = dc_ref[at] + dot(grams.T.astype(low), b_ref[at])
    for part in (0, 1):
        cols = slice(part * states, (part + 1) * states)
        v = state_ref[:, cols]
        pre = conv_in(v, taps_ref[:, cols], bias_ref[:, cols], masks)
        opened = sigmoid(pre)
        grad = act_scr[part] * opened * (1.0 + pre * (1.0 - opened))
        back, sums = conv_back(grad, v, taps_ref[:, cols], masks)
        state_out[:, cols] = back.astype(low)
        state_sums[:, cols] = jnp.concatenate(sums + [jnp.zeros((3, states), wide)], 0)
    pre = step_ref[...] + step_bias_ref[...]
    step = softplus(pre)
    rate_sum = jnp.zeros((1, LANES), wide)
    bias_sum = jnp.zeros((1, LANES), wide)
    for c in range(rows // SPAN):
        at = slice(c * SPAN, (c + 1) * SPAN)
        grad_rate = contract_rows(triangle, z_ref[at], highest)
        grad_step = (dt_ref[at] + rate_ref[...] * grad_rate) * sigmoid(pre[at])
        step_out[at] = grad_step.astype(low)
        rate_sum = rate_sum + jnp.sum(
            grad_rate * (rate_ref[...] * step[at]), axis=0, keepdims=True
        )
        bias_sum = bias_sum + jnp.sum(grad_step, axis=0, keepdims=True)
    step_sums[...] = jnp.concatenate([bias_sum, rate_sum, jnp.zeros((6, LANES), wide)], 0)


def call(kernel, outs, operands, grid=None, in_specs=None, out_specs=None, scratch=(), flops=0):
    shapes = tuple(jax.ShapeDtypeStruct(shape, kind) for shape, kind in outs)
    moved = sum(a.size * a.dtype.itemsize for a in operands)
    moved += sum(s.size * s.dtype.itemsize for s in shapes)
    extra = {} if grid is None else dict(grid=grid, in_specs=in_specs, out_specs=out_specs)
    return pl.pallas_call(
        kernel,
        out_shape=shapes,
        scratch_shapes=list(scratch),
        compiler_params=pltpu.CompilerParams(vmem_limit_bytes=VMEM_BYTES),
        cost_estimate=pl.CostEstimate(flops=flops, bytes_accessed=moved, transcendentals=0),
        **extra,
    )(*operands)


def column_block(rows):
    return pl.BlockSpec((rows, LANES), lambda i: (0, i))


def whole_block(shape):
    return pl.BlockSpec(shape, lambda i: (0,) * len(shape))


def lane_pad(v):
    return jnp.pad(v, ((0, 0), (0, LANES - v.shape[1])))


class Mixer:
    def __init__(
        self, state_in, step_in, conv_state, conv_state_bias, step_bias, decay_log, segments
    ):
        rows = state_in.shape[0]
        self.rows = rows
        self.head_count = step_bias.shape[0]
        self.pairs = (self.head_count + 1) // 2
        self.width = self.pairs * LANES
        self.states = conv_state.shape[1] // 2
        self.blocks = rows // SPAN
        before = [
            jnp.concatenate([jnp.full((k,), -1, jnp.int32), segments[: rows - k]]) == segments
            for k in (1, 2, 3)
        ]
        ends = segments.reshape(self.blocks, SPAN)[:, SPAN - 1]
        previous = jnp.concatenate([jnp.full((1,), -1, jnp.int32), ends[:-1]])
        carried = jnp.repeat(previous, SPAN) == segments
        tail = jnp.repeat(ends, SPAN) == segments
        flags = jnp.stack(before + [carried, tail]).astype(wide)
        self.masks = jnp.broadcast_to(flags[:, :, None], (5, rows, LANES))
        self.shared = (
            state_in,
            lane_pad(step_in),
            conv_state,
            conv_state_bias[None],
            lane_pad(step_bias[None]),
            lane_pad(-jnp.exp(decay_log)[None]),
            self.masks,
            segments[:, None],
            segments[None],
        )
        (
            self.b, self.c, self.bt, self.ct, self.g, self.gt, self.dtx, self.cumx, cumt,
        ) = call(
            prep_kernel,
            [((rows, self.states), low)] * 2
            + [((self.states, rows), low)] * 2
            + [((rows, SPAN), wide)] * 2
            + [((rows, self.width), wide)] * 2
            + [((LANES, rows), wide)],
            self.shared,
            flops=12 * rows * LANES * self.width,
        )
        self.cumt = cumt[: 2 * self.pairs].reshape(self.pairs, 2, rows)

    def widen(self, v):
        return jnp.pad(v, ((0, 0), (0, self.width - v.shape[1])))

    def forward(self, value_in, conv_value, conv_value_bias, skip_scale):
        rows, states = self.rows, self.states
        self.inner = value_in.shape[1]
        self.value = (
            self.widen(value_in),
            self.widen(conv_value),
            self.widen(conv_value_bias[None]),
            self.widen(jnp.repeat(skip_scale, HALF)[None]),
        )
        (mixed,) = call(
            fwd_kernel,
            [((rows, self.width), wide)],
            self.value + (self.dtx, self.cumx, self.cumt, self.masks, self.c, self.bt, self.g),
            grid=(self.pairs,),
            in_specs=[
                column_block(rows),
                column_block(4),
                column_block(1),
                column_block(1),
                column_block(rows),
                column_block(rows),
                pl.BlockSpec((1, 2, rows), lambda i: (i, 0, 0)),
                whole_block((5, rows, LANES)),
                whole_block((rows, states)),
                whole_block((states, rows)),
                whole_block((rows, SPAN)),
            ],
            out_specs=[column_block(rows)],
            scratch=[pltpu.VMEM((rows, LANES), wide)],
            flops=20 * rows * LANES * self.width,
        )
        self.mixed = mixed
        return mixed[:, : self.inner]

    def backward(self, grad_mixed):
        rows, states = self.rows, self.states
        value_grad, sums, db, dc, dg, z, dt = call(
            bwd_kernel,
            [((rows, self.width), low), ((8, self.width), wide)]
            + [((rows, LANES), wide)] * 5,
            (self.value[0], self.mixed, self.widen(grad_mixed))
            + self.value[1:]
            + (self.dtx, self.cumx, self.cumt, self.masks, self.b, self.c, self.bt, self.ct)
            + (self.gt,),
            grid=(self.pairs,),
            in_specs=[
                column_block(rows),
                column_block(rows),
                column_block(rows),
                column_block(4),
                column_block(1),
                column_block(1),
                column_block(rows),
                column_block(rows),
                pl.BlockSpec((1, 2, rows), lambda i: (i, 0, 0)),
                whole_block((5, rows, LANES)),
                whole_block((rows, states)),
                whole_block((rows, states)),
                whole_block((states, rows)),
                whole_block((states, rows)),
                whole_block((rows, SPAN)),
            ],
            out_specs=[column_block(rows), column_block(8)] + [whole_block((rows, LANES))] * 5,
            scratch=[pltpu.VMEM((rows, LANES), wide)] * 3
            + [pltpu.VMEM((self.blocks, states, LANES), wide)],
            flops=60 * rows * LANES * self.width,
        )
        state_grad, step_grad, state_sums, step_sums = call(
            post_kernel,
            [
                ((rows, 2 * states), low),
                ((rows, LANES), low),
                ((8, 2 * states), wide),
                ((8, LANES), wide),
            ],
            self.shared + (self.b, self.c, db, dc, dg, z, dt),
            scratch=[pltpu.VMEM((2, rows, states), wide)],
            flops=12 * rows * LANES * self.width,
        )
        heads = self.head_count
        skip_grad = sums[5, : self.inner].reshape(heads, HALF).sum(axis=1)
        return (
            value_grad[:, : self.inner],
            state_grad,
            step_grad[:, :heads],
            sums[:4, : self.inner],
            sums[4, : self.inner],
            state_sums[:4],
            state_sums[4],
            step_sums[0, :heads],
            step_sums[1, :heads],
            skip_grad,
        )


def scatter_rows(partial):
    return lax.psum_scatter(
        partial.astype(jnp.bfloat16), "gx", scatter_dimension=0, tiled=True
    ).astype(jnp.float32)


def on_device(
    layer_input,
    norm_gain,
    gate_weight,
    value_weight,
    state_weight,
    step_weight,
    conv_value,
    conv_value_bias,
    conv_state,
    conv_state_bias,
    step_bias,
    decay_log,
    skip_scale,
    gated_gain,
    out_weight,
    segment_ids,
    cotangent,
):
    model_width = layer_input.shape[1]
    col_width = cotangent.shape[1]
    state_cols = state_weight.shape[1]
    col_start = lax.axis_index("gy") * col_width

    full_value = lax.all_gather(value_weight, "gx", axis=0, tiled=True)
    full_state = lax.all_gather(
        jnp.concatenate([state_weight, step_weight], 1), "gx", axis=0, tiled=True
    )
    gate_weight, full_value = lax.optimization_barrier((gate_weight, full_value))
    full_gate = lax.all_gather(gate_weight, "gx", axis=0, tiled=True)
    out_rows, full_gate = lax.optimization_barrier((out_weight.T, full_gate))
    full_out = lax.all_gather(out_rows, "gx", axis=0, tiled=True)
    upstream = lax.all_gather(cotangent, "gy", axis=1, tiled=True)

    tokens = layer_input.astype(jnp.float32)
    scale_in = lax.rsqrt(jnp.mean(tokens * tokens, axis=1, keepdims=True) + epsilon)
    normed = (tokens * scale_in * norm_gain).astype(jnp.bfloat16)

    value_in = jnp.dot(normed, full_value, preferred_element_type=jnp.float32)
    state_step = jnp.dot(normed, full_state, preferred_element_type=jnp.float32)
    mixer = Mixer(
        state_step[:, :state_cols],
        state_step[:, state_cols:],
        conv_state,
        conv_state_bias,
        step_bias,
        decay_log,
        segment_ids,
    )
    mixed = mixer.forward(value_in, conv_value, conv_value_bias, skip_scale)
    gate_in = jnp.dot(normed, full_gate, preferred_element_type=jnp.float32)
    gate_open = jax.nn.sigmoid(gate_in)
    gate_act = gate_in * gate_open
    gated = mixed * gate_act
    squares = lax.psum(jnp.sum(gated * gated, axis=1), "gy")
    scale_out = lax.rsqrt(squares / INNER + epsilon)[:, None]
    scaled = (gated * gated_gain).astype(jnp.bfloat16)

    scaled_out = (gated * gated_gain * scale_out).astype(jnp.bfloat16)
    grad_out = scatter_rows(contract_rows(upstream, scaled_out))

    up_back = jnp.dot(upstream, full_out, preferred_element_type=jnp.float32)
    grad_scale = lax.psum(jnp.sum(gated * gated_gain * up_back, axis=1), "gy")[:, None]
    grad_scaled = scale_out * up_back
    grad_gated = grad_scaled * gated_gain - grad_scale * scale_out**3 * gated / INNER
    gate_gain_part = jnp.sum(grad_scaled * gated, axis=0)
    grad_gate_in = (
        grad_gated * mixed * gate_open * (1.0 + gate_in * (1.0 - gate_open))
    ).astype(jnp.bfloat16)
    grad_gate = scatter_rows(contract_rows(normed, grad_gate_in))

    pulled = mixer.backward(grad_gated * gate_act)
    grad_value_in = pulled[0]
    grad_state_in = jnp.concatenate([pulled[1], pulled[2]], 1)
    grad_state_step = scatter_rows(contract_rows(normed, grad_state_in))
    grad_value = scatter_rows(contract_rows(normed, grad_value_in))

    product = lax.psum_scatter(
        (contract_cols(scaled, full_out) * scale_out).astype(jnp.bfloat16),
        "gy",
        scatter_dimension=1,
        tiled=True,
    )
    token_cols = lax.dynamic_slice_in_dim(layer_input, col_start, col_width, 1).astype(jnp.float32)
    layer_output = (token_cols + product.astype(jnp.float32)).astype(jnp.bfloat16)

    grad_normed_part = (
        contract_cols(grad_gate_in, full_gate)
        + contract_cols(grad_value_in, full_value)
        + contract_cols(grad_state_in, full_state)
    )
    grad_normed = lax.psum_scatter(
        grad_normed_part.astype(jnp.bfloat16), "gy", scatter_dimension=1, tiled=True
    ).astype(jnp.float32)
    gain_cols = lax.dynamic_slice_in_dim(norm_gain, col_start, col_width, 0)
    weighted = grad_normed * gain_cols
    inner_dot = lax.psum(jnp.sum(weighted * token_cols, axis=1), "gy")[:, None]
    grad_input = (
        cotangent.astype(jnp.float32)
        + scale_in * weighted
        - token_cols * scale_in**3 * inner_dot / model_width
    )
    norm_gain_part = jnp.sum(grad_normed * token_cols * scale_in, axis=0)
    conv_state_sum, conv_bias_sum = lax.psum((pulled[5], pulled[6]), ("gx", "gy"))
    grad_state = lax.psum(grad_state_step[:, :state_cols], "gy")
    small_sums = lax.psum(
        (norm_gain_part, gate_gain_part, pulled[3], pulled[4], pulled[7], pulled[8], pulled[9]),
        "gx",
    )
    return (
        layer_output,
        grad_input,
        small_sums[0],
        grad_gate,
        grad_value,
        grad_state,
        grad_state_step[:, state_cols:],
        small_sums[2],
        small_sums[3],
        conv_state_sum,
        conv_bias_sum,
        small_sums[4],
        small_sums[5],
        small_sums[6],
        small_sums[1],
        grad_out.T,
    )


def solution(mesh):
    return jax.shard_map(
        on_device,
        mesh=mesh,
        in_specs=(
            P("gx", None),
            P(),
            P("gx", "gy"),
            P("gx", "gy"),
            P("gx", None),
            P("gx", "gy"),
            P(None, "gy"),
            P("gy"),
            P(),
            P(),
            P("gy"),
            P("gy"),
            P("gy"),
            P("gy"),
            P("gy", "gx"),
            P("gx"),
            P("gx", "gy"),
        ),
        out_specs=(
            P("gx", "gy"),
            P("gx", "gy"),
            P("gy"),
            P("gx", "gy"),
            P("gx", "gy"),
            P("gx", None),
            P("gx", "gy"),
            P(None, "gy"),
            P("gy"),
            P(),
            P(),
            P("gy"),
            P("gy"),
            P("gy"),
            P("gy"),
            P("gy", "gx"),
        ),
        check_vma=False,
    )
```

```python
import functools

import jax
import jax.numpy as jnp
from jax import lax
from jax.experimental import pallas as pl
from jax.experimental.pallas import tpu as pltpu
from jax.sharding import PartitionSpec as P

INNER = 5120
SPAN = 128
LANES = 128
HALF = 64
LOG2E = 1.4426950408889634
VMEM_BYTES = 56 * 1024 * 1024

epsilon = 1e-05
highest = lax.Precision.HIGHEST
low = jnp.bfloat16
wide = jnp.float32


def dot(left, right, precision=None):
    return jnp.dot(left, right, preferred_element_type=wide, precision=precision)


def contract_rows(left, right, precision=None):
    return lax.dot_general(
        left, right, (((0,), (0,)), ((), ())), preferred_element_type=wide, precision=precision
    )


def contract_cols(left, right, precision=None):
    return lax.dot_general(
        left, right, (((1,), (1,)), ((), ())), preferred_element_type=wide, precision=precision
    )


def sigmoid(v):
    return 1.0 / (1.0 + jnp.exp(-v))


def softplus(v):
    return jnp.maximum(v, 0.0) + jnp.log1p(jnp.exp(-jnp.abs(v)))


def conv_in(v, taps, bias, masks):
    total = bias + taps[0:1] * v
    for k in range(1, 4):
        total = total + taps[k : k + 1] * (pltpu.roll(v, k, 0) * masks[k - 1])
    return total


def conv_back(grad, v, taps, masks):
    rows = grad.shape[0]
    back = taps[0:1] * grad
    sums = [jnp.sum(grad * v, axis=0, keepdims=True)]
    for k in range(1, 4):
        kept = grad * masks[k - 1]
        sums.append(jnp.sum(kept * pltpu.roll(v, k, 0), axis=0, keepdims=True))
        back = back + taps[k : k + 1] * pltpu.roll(kept, rows - k, 0)
    sums.append(jnp.sum(grad, axis=0, keepdims=True))
    return back, sums


def visible_block(seg_col, seg_row, row_is_query):
    shape = (SPAN, SPAN)
    first = lax.broadcasted_iota(jnp.int32, shape, 0)
    second = lax.broadcasted_iota(jnp.int32, shape, 1)
    ordered = (first >= second) if row_is_query else (first <= second)
    return ordered & (seg_col == seg_row)


def lower_triangle():
    shape = (SPAN, SPAN)
    return (
        lax.broadcasted_iota(jnp.int32, shape, 0) >= lax.broadcasted_iota(jnp.int32, shape, 1)
    ).astype(wide)


def prep_kernel(
    state_ref, step_ref, taps_ref, bias_ref, step_bias_ref, rate_ref, masks_ref, seg_col_ref,
    seg_row_ref, b_ref, c_ref, bt_ref, ct_ref, g_ref, gt_ref, dtx_ref, cumx_ref, cumt_ref,
):
    rows, states = b_ref.shape
    masks = [masks_ref[k] for k in range(3)]
    for part, (out, out_t) in enumerate(((b_ref, bt_ref), (c_ref, ct_ref))):
        cols = slice(part * states, (part + 1) * states)
        pre = conv_in(state_ref[:, cols], taps_ref[:, cols], bias_ref[:, cols], masks)
        act = pre * sigmoid(pre)
        out[...] = act.astype(low)
        out_t[...] = act.T.astype(low)
    step = softplus(step_ref[...] + step_bias_ref[...])
    triangle = lower_triangle()
    heads = lax.broadcasted_iota(jnp.int32, (LANES, dtx_ref.shape[1]), 0)
    channels = lax.broadcasted_iota(jnp.int32, (LANES, dtx_ref.shape[1]), 1)
    expand = (channels // HALF == heads).astype(wide)
    rate = step * (rate_ref[...] * LOG2E)
    for c in range(rows // SPAN):
        at = slice(c * SPAN, (c + 1) * SPAN)
        grams = dot(c_ref[at], bt_ref[:, at])
        g_ref[at] = jnp.where(visible_block(seg_col_ref[at], seg_row_ref[:, at], True), grams, 0.0)
        grams_t = dot(b_ref[at], ct_ref[:, at])
        gt_ref[at] = jnp.where(
            visible_block(seg_col_ref[at], seg_row_ref[:, at], False), grams_t, 0.0
        )
        total = dot(triangle, rate[at], highest)
        cumx_ref[at] = dot(total, expand, highest)
        dtx_ref[at] = dot(step[at], expand, highest)
        cumt_ref[:, at] = total.T


def decays(cumx_ref, cumt_ref, at, head, row_is_query):
    lane = head * HALF
    column = cumx_ref[at, lane : lane + 1]
    row = cumt_ref[0, head : head + 1, at]
    gap = (column - row) if row_is_query else (row - column)
    return jnp.exp2(jnp.minimum(gap, 0.0))


def split_heads(block):
    left = lax.broadcasted_iota(jnp.int32, block.shape, 1) < HALF
    zero = jnp.zeros_like(block)
    return jnp.concatenate([jnp.where(left, block, zero), jnp.where(left, zero, block)], 0)


def fwd_kernel(
    value_ref, taps_ref, bias_ref, skip_ref, dtx_ref, cumx_ref, cumt_ref, masks_ref, c_ref, bt_ref,
    g_ref, out_ref, x_scr,
):
    rows = value_ref.shape[0]
    masks = [masks_ref[k] for k in range(3)]
    pre = conv_in(value_ref[...], taps_ref[...], bias_ref[...], masks)
    x_scr[...] = pre * sigmoid(pre)
    state = jnp.zeros((c_ref.shape[1], LANES), wide)
    for c in range(rows // SPAN):
        at = slice(c * SPAN, (c + 1) * SPAN)
        x = x_scr[at]
        cum = cumx_ref[at]
        stepped = x * dtx_ref[at]
        mixing = jnp.concatenate(
            [decays(cumx_ref, cumt_ref, at, head, True) * g_ref[at] for head in (0, 1)], 1
        ).astype(low)
        y = dot(mixing, split_heads(stepped.astype(low)))
        if c > 0:
            y = y + dot(c_ref[at], state.astype(low)) * (jnp.exp2(cum) * masks_ref[3, at])
        out_ref[at] = y + skip_ref[...] * x
        if c + 1 < rows // SPAN:
            end = slice((c + 1) * SPAN - 1, (c + 1) * SPAN)
            last = cum[SPAN - 1 : SPAN]
            tail = jnp.exp2(last - cum) * masks_ref[4, at]
            fresh = dot(bt_ref[:, at], (stepped.astype(low) * tail).astype(low))
            state = (masks_ref[3, end] * jnp.exp2(last)) * state + fresh


def bwd_kernel(
    value_ref, mixed_ref, grad_ref, taps_ref, bias_ref, skip_ref, dtx_ref, cumx_ref, cumt_ref,
    masks_ref, b_ref, c_ref, bt_ref, ct_ref, gt_ref,
    value_out, sums_out, db_ref, dc_ref, dg_ref, z_ref, dt_ref,
    pre_scr, x_scr, dpre_scr, state_scr,
):
    rows = value_ref.shape[0]
    blocks = rows // SPAN
    pair = pl.program_id(0)
    masks = [masks_ref[k] for k in range(3)]

    @pl.when(pair == 0)
    def _():
        for ref in (db_ref, dc_ref, dg_ref, z_ref, dt_ref):
            ref[...] = jnp.zeros_like(ref)

    pre = conv_in(value_ref[...], taps_ref[...], bias_ref[...], masks)
    pre_scr[...] = pre
    x_scr[...] = pre * sigmoid(pre)
    state = jnp.zeros((c_ref.shape[1], LANES), wide)
    for c in range(blocks):
        at = slice(c * SPAN, (c + 1) * SPAN)
        state_scr[c] = state
        if c + 1 < blocks:
            end = slice((c + 1) * SPAN - 1, (c + 1) * SPAN)
            cum = cumx_ref[at]
            last = cum[SPAN - 1 : SPAN]
            tail = jnp.exp2(last - cum) * masks_ref[4, at]
            stepped = (x_scr[at] * dtx_ref[at]).astype(low)
            fresh = dot(bt_ref[:, at], (stepped * tail).astype(low))
            state = (masks_ref[3, end] * jnp.exp2(last)) * state + fresh

    lanes = lax.broadcasted_iota(jnp.int32, (LANES, LANES), 0)
    heads = lax.broadcasted_iota(jnp.int32, (LANES, LANES), 1)
    gather = (lanes // HALF + 2 * pair == heads).astype(low)
    row_number = lax.broadcasted_iota(jnp.int32, (SPAN, LANES), 0)
    grad_skip = jnp.zeros((1, LANES), wide)
    grad_state = jnp.zeros((c_ref.shape[1], LANES), wide)
    for c in reversed(range(blocks)):
        at = slice(c * SPAN, (c + 1) * SPAN)
        end = slice((c + 1) * SPAN - 1, (c + 1) * SPAN)
        x = x_scr[at]
        dtx = dtx_ref[at]
        cum = cumx_ref[at]
        grad = grad_ref[at]
        grad_low = grad.astype(low)
        stepped = (x * dtx).astype(low)
        y = mixed_ref[at] - skip_ref[...] * x
        grad_mix = contract_cols(split_heads(stepped), grad_low)
        mixing = []
        grams = dg_ref[at]
        for head in (0, 1):
            decay = decays(cumx_ref, cumt_ref, at, head, False)
            mixing.append((decay * gt_ref[at]).astype(low))
            grams = grams + decay * grad_mix[head * SPAN : (head + 1) * SPAN]
        dg_ref[at] = grams
        grad_stepped = dot(jnp.concatenate(mixing, 1), split_heads(grad_low))
        last = cum[SPAN - 1 : SPAN]
        at_end = jnp.zeros((1, LANES), wide)
        carry = masks_ref[3, end] * jnp.exp2(last)
        if c + 1 < blocks:
            tail = jnp.exp2(last - cum) * masks_ref[4, at]
            grad_state_low = grad_state.astype(low)
            from_tail = dot(b_ref[at], grad_state_low) * tail
            grad_stepped = grad_stepped + from_tail
            db_ref[at] += contract_cols((stepped * tail).astype(low), grad_state_low)
            at_end = jnp.sum(stepped.astype(wide) * from_tail, axis=0, keepdims=True)
            at_end = at_end + carry * jnp.sum(state_scr[c] * grad_state, axis=0, keepdims=True)
        if c > 0:
            reach = (grad * (jnp.exp2(cum) * masks_ref[3, at])).astype(low)
            dc_ref[at] += contract_cols(reach, state_scr[c].astype(low))
            grad_state = carry * grad_state + dot(ct_ref[:, at], reach)
        z = grad_low.astype(wide) * y - stepped.astype(wide) * grad_stepped
        z = z + jnp.where(row_number == SPAN - 1, at_end, 0.0)
        z_high = z.astype(low)
        z_low = (z - z_high.astype(wide)).astype(low)
        z_ref[at] += dot(z_high, gather) + dot(z_low, gather)
        dt_ref[at] += dot((x * grad_stepped).astype(low), gather)
        grad_skip = grad_skip + jnp.sum(grad * x, axis=0, keepdims=True)
        pre_c = pre_scr[at]
        opened = sigmoid(pre_c)
        grad_x = grad_stepped * dtx + skip_ref[...] * grad
        dpre_scr[at] = grad_x * opened * (1.0 + pre_c * (1.0 - opened))

    back, sums = conv_back(dpre_scr[...], value_ref[...], taps_ref[...], masks)
    value_out[...] = back.astype(low)
    sums_out[...] = jnp.concatenate(sums + [grad_skip, jnp.zeros((2, LANES), wide)], 0)


def post_kernel(
    state_ref, step_ref, taps_ref, bias_ref, step_bias_ref, rate_ref, masks_ref, seg_col_ref,
    seg_row_ref, b_ref, c_ref, db_ref, dc_ref, dg_ref, z_ref, dt_ref,
    state_out, step_out, state_sums, step_sums, act_scr,
):
    rows, states = b_ref.shape
    masks = [masks_ref[k] for k in range(3)]
    triangle = lower_triangle()
    for c in range(rows // SPAN):
        at = slice(c * SPAN, (c + 1) * SPAN)
        seen = visible_block(seg_col_ref[at], seg_row_ref[:, at], False)
        grams = jnp.where(seen, dg_ref[at], 0.0)
        act_scr[0, at] = db_ref[at] + dot(grams.astype(low), c_ref[at])
        act_scr[1, at] = dc_ref[at] + dot(grams.T.astype(low), b_ref[at])
    for part in (0, 1):
        cols = slice(part * states, (part + 1) * states)
        v = state_ref[:, cols]
        pre = conv_in(v, taps_ref[:, cols], bias_ref[:, cols], masks)
        opened = sigmoid(pre)
        grad = act_scr[part] * opened * (1.0 + pre * (1.0 - opened))
        back, sums = conv_back(grad, v, taps_ref[:, cols], masks)
        state_out[:, cols] = back.astype(low)
        state_sums[:, cols] = jnp.concatenate(sums + [jnp.zeros((3, states), wide)], 0)
    pre = step_ref[...] + step_bias_ref[...]
    step = softplus(pre)
    rate_sum = jnp.zeros((1, LANES), wide)
    bias_sum = jnp.zeros((1, LANES), wide)
    for c in range(rows // SPAN):
        at = slice(c * SPAN, (c + 1) * SPAN)
        grad_rate = contract_rows(triangle, z_ref[at], highest)
        grad_step = (dt_ref[at] + rate_ref[...] * grad_rate) * sigmoid(pre[at])
        step_out[at] = grad_step.astype(low)
        rate_sum = rate_sum + jnp.sum(
            grad_rate * (rate_ref[...] * step[at]), axis=0, keepdims=True
        )
        bias_sum = bias_sum + jnp.sum(grad_step, axis=0, keepdims=True)
    step_sums[...] = jnp.concatenate([bias_sum, rate_sum, jnp.zeros((6, LANES), wide)], 0)


def call(kernel, outs, operands, grid=None, in_specs=None, out_specs=None, scratch=(), flops=0):
    shapes = tuple(jax.ShapeDtypeStruct(shape, kind) for shape, kind in outs)
    moved = sum(a.size * a.dtype.itemsize for a in operands)
    moved += sum(s.size * s.dtype.itemsize for s in shapes)
    extra = {} if grid is None else dict(grid=grid, in_specs=in_specs, out_specs=out_specs)
    return pl.pallas_call(
        kernel,
        out_shape=shapes,
        scratch_shapes=list(scratch),
        compiler_params=pltpu.CompilerParams(vmem_limit_bytes=VMEM_BYTES),
        cost_estimate=pl.CostEstimate(flops=flops, bytes_accessed=moved, transcendentals=0),
        **extra,
    )(*operands)


def column_block(rows):
    return pl.BlockSpec((rows, LANES), lambda i: (0, i))


def whole_block(shape):
    return pl.BlockSpec(shape, lambda i: (0,) * len(shape))


def lane_pad(v):
    return jnp.pad(v, ((0, 0), (0, LANES - v.shape[1])))


class Mixer:
    def __init__(
        self, state_in, step_in, conv_state, conv_state_bias, step_bias, decay_log, segments
    ):
        rows = state_in.shape[0]
        self.rows = rows
        self.head_count = step_bias.shape[0]
        self.pairs = (self.head_count + 1) // 2
        self.width = self.pairs * LANES
        self.states = conv_state.shape[1] // 2
        self.blocks = rows // SPAN
        before = [
            jnp.concatenate([jnp.full((k,), -1, jnp.int32), segments[: rows - k]]) == segments
            for k in (1, 2, 3)
        ]
        ends = segments.reshape(self.blocks, SPAN)[:, SPAN - 1]
        previous = jnp.concatenate([jnp.full((1,), -1, jnp.int32), ends[:-1]])
        carried = jnp.repeat(previous, SPAN) == segments
        tail = jnp.repeat(ends, SPAN) == segments
        flags = jnp.stack(before + [carried, tail]).astype(wide)
        self.masks = jnp.broadcast_to(flags[:, :, None], (5, rows, LANES))
        self.shared = (
            state_in,
            lane_pad(step_in),
            conv_state,
            conv_state_bias[None],
            lane_pad(step_bias[None]),
            lane_pad(-jnp.exp(decay_log)[None]),
            self.masks,
            segments[:, None],
            segments[None],
        )
        (
            self.b, self.c, self.bt, self.ct, self.g, self.gt, self.dtx, self.cumx, cumt,
        ) = call(
            prep_kernel,
            [((rows, self.states), low)] * 2
            + [((self.states, rows), low)] * 2
            + [((rows, SPAN), wide)] * 2
            + [((rows, self.width), wide)] * 2
            + [((LANES, rows), wide)],
            self.shared,
            flops=12 * rows * LANES * self.width,
        )
        self.cumt = cumt[: 2 * self.pairs].reshape(self.pairs, 2, rows)

    def widen(self, v):
        return jnp.pad(v, ((0, 0), (0, self.width - v.shape[1])))

    def forward(self, value_in, conv_value, conv_value_bias, skip_scale):
        rows, states = self.rows, self.states
        self.inner = value_in.shape[1]
        self.value = (
            self.widen(value_in),
            self.widen(conv_value),
            self.widen(conv_value_bias[None]),
            self.widen(jnp.repeat(skip_scale, HALF)[None]),
        )
        (mixed,) = call(
            fwd_kernel,
            [((rows, self.width), wide)],
            self.value + (self.dtx, self.cumx, self.cumt, self.masks, self.c, self.bt, self.g),
            grid=(self.pairs,),
            in_specs=[
                column_block(rows),
                column_block(4),
                column_block(1),
                column_block(1),
                column_block(rows),
                column_block(rows),
                pl.BlockSpec((1, 2, rows), lambda i: (i, 0, 0)),
                whole_block((5, rows, LANES)),
                whole_block((rows, states)),
                whole_block((states, rows)),
                whole_block((rows, SPAN)),
            ],
            out_specs=[column_block(rows)],
            scratch=[pltpu.VMEM((rows, LANES), wide)],
            flops=20 * rows * LANES * self.width,
        )
        self.mixed = mixed
        return mixed[:, : self.inner]

    def backward(self, grad_mixed):
        rows, states = self.rows, self.states
        value_grad, sums, db, dc, dg, z, dt = call(
            bwd_kernel,
            [((rows, self.width), low), ((8, self.width), wide)]
            + [((rows, LANES), wide)] * 5,
            (self.value[0], self.mixed, self.widen(grad_mixed))
            + self.value[1:]
            + (self.dtx, self.cumx, self.cumt, self.masks, self.b, self.c, self.bt, self.ct)
            + (self.gt,),
            grid=(self.pairs,),
            in_specs=[
                column_block(rows),
                column_block(rows),
                column_block(rows),
                column_block(4),
                column_block(1),
                column_block(1),
                column_block(rows),
                column_block(rows),
                pl.BlockSpec((1, 2, rows), lambda i: (i, 0, 0)),
                whole_block((5, rows, LANES)),
                whole_block((rows, states)),
                whole_block((rows, states)),
                whole_block((states, rows)),
                whole_block((states, rows)),
                whole_block((rows, SPAN)),
            ],
            out_specs=[column_block(rows), column_block(8)] + [whole_block((rows, LANES))] * 5,
            scratch=[pltpu.VMEM((rows, LANES), wide)] * 3
            + [pltpu.VMEM((self.blocks, states, LANES), wide)],
            flops=60 * rows * LANES * self.width,
        )
        state_grad, step_grad, state_sums, step_sums = call(
            post_kernel,
            [
                ((rows, 2 * states), low),
                ((rows, LANES), low),
                ((8, 2 * states), wide),
                ((8, LANES), wide),
            ],
            self.shared + (self.b, self.c, db, dc, dg, z, dt),
            scratch=[pltpu.VMEM((2, rows, states), wide)],
            flops=12 * rows * LANES * self.width,
        )
        heads = self.head_count
        skip_grad = sums[5, : self.inner].reshape(heads, HALF).sum(axis=1)
        return (
            value_grad[:, : self.inner],
            state_grad,
            step_grad[:, :heads],
            sums[:4, : self.inner],
            sums[4, : self.inner],
            state_sums[:4],
            state_sums[4],
            step_sums[0, :heads],
            step_sums[1, :heads],
            skip_grad,
        )


def ring_place(index, count):
    return jnp.where(index % 2 == 0, index // 2, count - 1 - index // 2)


def ring_index(place, count):
    place = place % count
    return jnp.where(place < (count + 1) // 2, 2 * place, 2 * (count - 1 - place) + 1)


def ring_moves(count):
    order = list(range(0, count, 2)) + list(range(1, count, 2))[::-1]
    ahead = [(order[k], order[(k + 1) % count]) for k in range(count)]
    return ahead, [(target, source) for source, target in ahead]


def ring_gather(shard, splits):
    count = lax.axis_size("gx")
    ahead, behind = ring_moves(count)
    me = lax.axis_index("gx")
    place = ring_place(me, count)
    rows, width = shard.shape
    half = rows // 2
    edges = [0] + splits + [width]
    fulls = [jnp.zeros((count * rows, hi - lo), shard.dtype) for lo, hi in zip(edges, edges[1:])]

    def put(fulls, piece, start):
        return [
            lax.dynamic_update_slice(full, piece[:, lo:hi], (start, 0))
            for full, lo, hi in zip(fulls, edges, edges[1:])
        ]

    fulls = put(fulls, shard, me * rows)
    up, down = shard[:half], shard[half:]
    for step in range(1, count):
        up = lax.ppermute(up, "gx", ahead)
        down = lax.ppermute(down, "gx", behind)
        fulls = put(fulls, up, ring_index(place - step, count) * rows)
        fulls = put(fulls, down, ring_index(place + step, count) * rows + half)
    return fulls, (up, down)


def ring_scatter(partial):
    count = lax.axis_size("gx")
    ahead, behind = ring_moves(count)
    place = ring_place(lax.axis_index("gx"), count)
    rows = partial.shape[0] // count
    half = rows // 2

    def part(target, offset):
        start = ring_index(target, count) * rows + offset
        return lax.dynamic_slice_in_dim(partial, start, half, 0)

    up, down = part(place - 1, 0), part(place + 1, half)
    for step in range(1, count):
        up = lax.ppermute(up, "gx", ahead).astype(wide)
        down = lax.ppermute(down, "gx", behind).astype(wide)
        up = up + part(place - 1 - step, 0).astype(wide)
        down = down + part(place + 1 + step, half).astype(wide)
        if step < count - 1:
            up, down = up.astype(low), down.astype(low)
    return jnp.concatenate([up, down], 0)


def after(value, *others):
    return lax.optimization_barrier((value,) + others)[0]


def on_device(
    layer_input,
    norm_gain,
    gate_weight,
    value_weight,
    state_weight,
    step_weight,
    conv_value,
    conv_value_bias,
    conv_state,
    conv_state_bias,
    step_bias,
    decay_log,
    skip_scale,
    gated_gain,
    out_weight,
    segment_ids,
    cotangent,
):
    model_width = layer_input.shape[1]
    col_width = cotangent.shape[1]
    state_cols = state_weight.shape[1]
    col_start = lax.axis_index("gy") * col_width

    state_step_weight = jnp.concatenate([state_weight, step_weight], 1)
    (full_state,), moved = ring_gather(state_step_weight, [])
    (full_value,), moved = ring_gather(after(value_weight, *moved), [])
    (full_gate,), moved = ring_gather(after(gate_weight, *moved), [])
    (full_out,), moved = ring_gather(after(out_weight.T, *moved), [])
    upstream = lax.all_gather(cotangent, "gy", axis=1, tiled=True)

    tokens = layer_input.astype(wide)
    scale_in = lax.rsqrt(jnp.mean(tokens * tokens, axis=1, keepdims=True) + epsilon)
    normed = (tokens * scale_in * norm_gain).astype(low)

    state_step = dot(normed, full_state)
    mixer = Mixer(
        state_step[:, :state_cols],
        state_step[:, state_cols:],
        conv_state,
        conv_state_bias,
        step_bias,
        decay_log,
        segment_ids,
    )
    value_in = dot(normed, full_value)
    mixed = mixer.forward(value_in, conv_value, conv_value_bias, skip_scale)
    gate_in = dot(normed, full_gate)
    gate_open = jax.nn.sigmoid(gate_in)
    gate_act = gate_in * gate_open
    gated = mixed * gate_act
    squares = lax.psum(jnp.sum(gated * gated, axis=1), "gy")
    scale_out = lax.rsqrt(squares / INNER + epsilon)[:, None]
    scaled = (gated * gated_gain).astype(low)

    scaled_out = (gated * gated_gain * scale_out).astype(low)
    grad_out = ring_scatter(contract_rows(upstream, scaled_out).astype(low))

    up_back = dot(upstream, full_out)
    grad_scale = lax.psum(jnp.sum(gated * gated_gain * up_back, axis=1), "gy")[:, None]
    grad_scaled = scale_out * up_back
    grad_gated = grad_scaled * gated_gain - grad_scale * scale_out**3 * gated / INNER
    gate_gain_part = jnp.sum(grad_scaled * gated, axis=0)
    grad_gate_in = (
        grad_gated * mixed * gate_open * (1.0 + gate_in * (1.0 - gate_open))
    ).astype(low)
    grad_gate = ring_scatter(contract_rows(normed, grad_gate_in).astype(low))

    pulled = mixer.backward(grad_gated * gate_act)
    grad_value_in = pulled[0]
    grad_state_in = jnp.concatenate([pulled[1], pulled[2]], 1)
    grad_state_step = ring_scatter(contract_rows(normed, grad_state_in).astype(low))
    grad_value = ring_scatter(contract_rows(normed, grad_value_in).astype(low))

    product = lax.psum_scatter(
        (contract_cols(full_out, scaled) * scale_out[:, 0]).astype(low),
        "gy",
        scatter_dimension=0,
        tiled=True,
    ).T
    token_cols = lax.dynamic_slice_in_dim(layer_input, col_start, col_width, 1).astype(wide)
    layer_output = (token_cols + product.astype(wide)).astype(low)

    grad_normed_part = (
        contract_cols(full_gate, grad_gate_in)
        + contract_cols(full_value, grad_value_in)
        + contract_cols(full_state, grad_state_in)
    )
    grad_normed = lax.psum_scatter(
        grad_normed_part.astype(low), "gy", scatter_dimension=0, tiled=True
    ).T.astype(wide)
    gain_cols = lax.dynamic_slice_in_dim(norm_gain, col_start, col_width, 0)
    weighted = grad_normed * gain_cols
    inner_dot = lax.psum(jnp.sum(weighted * token_cols, axis=1), "gy")[:, None]
    grad_input = (
        cotangent.astype(wide)
        + scale_in * weighted
        - token_cols * scale_in**3 * inner_dot / model_width
    )
    grad_norm_gain = lax.psum(jnp.sum(grad_normed * token_cols * scale_in, axis=0), "gx")

    small = (gate_gain_part,) + pulled[3:]
    packed = lax.psum(jnp.concatenate([v.reshape(-1) for v in small]), "gx")
    sums, start = [], 0
    for v in small:
        sums.append(packed[start : start + v.size].reshape(v.shape))
        start += v.size
    state_sums = lax.psum(
        jnp.concatenate([grad_state_step[:, :state_cols], sums[3], sums[4][None]], 0), "gy"
    )
    state_rows = state_weight.shape[0]
    return (
        layer_output,
        grad_input,
        grad_norm_gain,
        grad_gate,
        grad_value,
        state_sums[:state_rows],
        grad_state_step[:, state_cols:],
        sums[1],
        sums[2],
        state_sums[state_rows:-1],
        state_sums[-1],
        sums[5],
        sums[6],
        sums[7],
        sums[0],
        grad_out.T,
    )


def solution(mesh):
    return jax.shard_map(
        on_device,
        mesh=mesh,
        in_specs=(
            P("gx", None),
            P(),
            P("gx", "gy"),
            P("gx", "gy"),
            P("gx", None),
            P("gx", "gy"),
            P(None, "gy"),
            P("gy"),
            P(),
            P(),
            P("gy"),
            P("gy"),
            P("gy"),
            P("gy"),
            P("gy", "gx"),
            P("gx"),
            P("gx", "gy"),
        ),
        out_specs=(
            P("gx", "gy"),
            P("gx", "gy"),
            P("gy"),
            P("gx", "gy"),
            P("gx", "gy"),
            P("gx", None),
            P("gx", "gy"),
            P(None, "gy"),
            P("gy"),
            P(),
            P(),
            P("gy"),
            P("gy"),
            P("gy"),
            P("gy"),
            P("gy", "gx"),
        ),
        check_vma=False,
    )
```

```python
import functools

import jax
import jax.numpy as jnp
from jax import lax
from jax.experimental import pallas as pl
from jax.experimental.layout import Layout, with_layout_constraint
from jax.experimental.pallas import tpu as pltpu
from jax.sharding import PartitionSpec as P

INNER = 5120
SPAN = 128
LANES = 128
HALF = 64
LOG2E = 1.4426950408889634
VMEM_BYTES = 56 * 1024 * 1024

epsilon = 1e-05
highest = lax.Precision.HIGHEST
low = jnp.bfloat16
wide = jnp.float32


def dot(left, right, precision=None):
    return jnp.dot(left, right, preferred_element_type=wide, precision=precision)


def contract_rows(left, right, precision=None):
    return lax.dot_general(
        left, right, (((0,), (0,)), ((), ())), preferred_element_type=wide, precision=precision
    )


def contract_cols(left, right, precision=None):
    return lax.dot_general(
        left, right, (((1,), (1,)), ((), ())), preferred_element_type=wide, precision=precision
    )


def sigmoid(v):
    return 1.0 / (1.0 + jnp.exp(-v))


def softplus(v):
    return jnp.maximum(v, 0.0) + jnp.log1p(jnp.exp(-jnp.abs(v)))


def conv_in(v, taps, bias, masks):
    total = bias + taps[0:1] * v
    for k in range(1, 4):
        total = total + taps[k : k + 1] * (pltpu.roll(v, k, 0) * masks[k - 1])
    return total


def conv_back(grad, v, taps, masks):
    rows = grad.shape[0]
    back = taps[0:1] * grad
    sums = [jnp.sum(grad * v, axis=0, keepdims=True)]
    for k in range(1, 4):
        kept = grad * masks[k - 1]
        sums.append(jnp.sum(kept * pltpu.roll(v, k, 0), axis=0, keepdims=True))
        back = back + taps[k : k + 1] * pltpu.roll(kept, rows - k, 0)
    sums.append(jnp.sum(grad, axis=0, keepdims=True))
    return back, sums


def visible_block(seg_col, seg_row, row_is_query):
    shape = (SPAN, SPAN)
    first = lax.broadcasted_iota(jnp.int32, shape, 0)
    second = lax.broadcasted_iota(jnp.int32, shape, 1)
    ordered = (first >= second) if row_is_query else (first <= second)
    return ordered & (seg_col == seg_row)


def lower_triangle():
    shape = (SPAN, SPAN)
    return (
        lax.broadcasted_iota(jnp.int32, shape, 0) >= lax.broadcasted_iota(jnp.int32, shape, 1)
    ).astype(wide)


def prep_kernel(
    state_ref, step_ref, taps_ref, bias_ref, step_bias_ref, rate_ref, masks_ref, seg_col_ref,
    seg_row_ref, b_ref, c_ref, bt_ref, ct_ref, g_ref, gt_ref, dtx_ref, cumx_ref, cumt_ref,
):
    rows, states = b_ref.shape
    masks = [masks_ref[k] for k in range(3)]
    for part, (out, out_t) in enumerate(((b_ref, bt_ref), (c_ref, ct_ref))):
        cols = slice(part * states, (part + 1) * states)
        pre = conv_in(state_ref[:, cols], taps_ref[:, cols], bias_ref[:, cols], masks)
        act = pre * sigmoid(pre)
        out[...] = act.astype(low)
        out_t[...] = act.T.astype(low)
    step = softplus(step_ref[...] + step_bias_ref[...])
    triangle = lower_triangle()
    heads = lax.broadcasted_iota(jnp.int32, (LANES, dtx_ref.shape[1]), 0)
    channels = lax.broadcasted_iota(jnp.int32, (LANES, dtx_ref.shape[1]), 1)
    expand = (channels // HALF == heads).astype(wide)
    rate = step * (rate_ref[...] * LOG2E)
    for c in range(rows // SPAN):
        at = slice(c * SPAN, (c + 1) * SPAN)
        grams = dot(c_ref[at], bt_ref[:, at])
        g_ref[at] = jnp.where(visible_block(seg_col_ref[at], seg_row_ref[:, at], True), grams, 0.0)
        grams_t = dot(b_ref[at], ct_ref[:, at])
        gt_ref[at] = jnp.where(
            visible_block(seg_col_ref[at], seg_row_ref[:, at], False), grams_t, 0.0
        )
        total = dot(triangle, rate[at], highest)
        cumx_ref[at] = dot(total, expand, highest)
        dtx_ref[at] = dot(step[at], expand, highest)
        cumt_ref[:, at] = total.T


def decays(cumx_ref, cumt_ref, at, head, row_is_query):
    lane = head * HALF
    column = cumx_ref[at, lane : lane + 1]
    row = cumt_ref[0, head : head + 1, at]
    gap = (column - row) if row_is_query else (row - column)
    return jnp.exp2(jnp.minimum(gap, 0.0))


def split_heads(block):
    left = lax.broadcasted_iota(jnp.int32, block.shape, 1) < HALF
    zero = jnp.zeros_like(block)
    return jnp.concatenate([jnp.where(left, block, zero), jnp.where(left, zero, block)], 0)


def fwd_kernel(
    value_ref, taps_ref, bias_ref, skip_ref, dtx_ref, cumx_ref, cumt_ref, masks_ref, c_ref, bt_ref,
    g_ref, out_ref, x_scr,
):
    rows = value_ref.shape[0]
    masks = [masks_ref[k] for k in range(3)]
    pre = conv_in(value_ref[...], taps_ref[...], bias_ref[...], masks)
    x_scr[...] = pre * sigmoid(pre)
    state = jnp.zeros((c_ref.shape[1], LANES), wide)
    for c in range(rows // SPAN):
        at = slice(c * SPAN, (c + 1) * SPAN)
        x = x_scr[at]
        cum = cumx_ref[at]
        stepped = x * dtx_ref[at]
        mixing = jnp.concatenate(
            [decays(cumx_ref, cumt_ref, at, head, True) * g_ref[at] for head in (0, 1)], 1
        ).astype(low)
        y = dot(mixing, split_heads(stepped.astype(low)))
        if c > 0:
            y = y + dot(c_ref[at], state.astype(low)) * (jnp.exp2(cum) * masks_ref[3, at])
        out_ref[at] = y + skip_ref[...] * x
        if c + 1 < rows // SPAN:
            end = slice((c + 1) * SPAN - 1, (c + 1) * SPAN)
            last = cum[SPAN - 1 : SPAN]
            tail = jnp.exp2(last - cum) * masks_ref[4, at]
            fresh = dot(bt_ref[:, at], (stepped.astype(low) * tail).astype(low))
            state = (masks_ref[3, end] * jnp.exp2(last)) * state + fresh


def bwd_kernel(
    first, resumed, value_ref, mixed_ref, grad_ref, taps_ref, bias_ref, skip_ref, dtx_ref, cumx_ref, cumt_ref,
    masks_ref, b_ref, c_ref, bt_ref, ct_ref, gt_ref, *more,
):
    earlier, more = more[: 7 * resumed], more[7 * resumed :]
    value_out, sums_out, *totals, pre_scr, x_scr, dpre_scr, state_scr = more
    db_ref, dc_ref, dg_ref, z_ref, dt_ref = totals
    rows = value_ref.shape[0]
    blocks = rows // SPAN
    pair = pl.program_id(0) + first
    masks = [masks_ref[k] for k in range(3)]

    @pl.when(pl.program_id(0) == 0)
    def _():
        for place, ref in enumerate(totals):
            ref[...] = earlier[2 + place][...] if resumed else jnp.zeros_like(ref)

    pre = conv_in(value_ref[...], taps_ref[...], bias_ref[...], masks)
    pre_scr[...] = pre
    x_scr[...] = pre * sigmoid(pre)
    state = jnp.zeros((c_ref.shape[1], LANES), wide)
    for c in range(blocks):
        at = slice(c * SPAN, (c + 1) * SPAN)
        state_scr[c] = state
        if c + 1 < blocks:
            end = slice((c + 1) * SPAN - 1, (c + 1) * SPAN)
            cum = cumx_ref[at]
            last = cum[SPAN - 1 : SPAN]
            tail = jnp.exp2(last - cum) * masks_ref[4, at]
            stepped = (x_scr[at] * dtx_ref[at]).astype(low)
            fresh = dot(bt_ref[:, at], (stepped * tail).astype(low))
            state = (masks_ref[3, end] * jnp.exp2(last)) * state + fresh

    lanes = lax.broadcasted_iota(jnp.int32, (LANES, LANES), 0)
    heads = lax.broadcasted_iota(jnp.int32, (LANES, LANES), 1)
    gather = (lanes // HALF + 2 * pair == heads).astype(low)
    row_number = lax.broadcasted_iota(jnp.int32, (SPAN, LANES), 0)
    grad_skip = jnp.zeros((1, LANES), wide)
    grad_state = jnp.zeros((c_ref.shape[1], LANES), wide)
    for c in reversed(range(blocks)):
        at = slice(c * SPAN, (c + 1) * SPAN)
        end = slice((c + 1) * SPAN - 1, (c + 1) * SPAN)
        x = x_scr[at]
        dtx = dtx_ref[at]
        cum = cumx_ref[at]
        grad = grad_ref[at]
        grad_low = grad.astype(low)
        stepped = (x * dtx).astype(low)
        y = mixed_ref[at] - skip_ref[...] * x
        grad_mix = contract_cols(split_heads(stepped), grad_low)
        mixing = []
        grams = dg_ref[at]
        for head in (0, 1):
            decay = decays(cumx_ref, cumt_ref, at, head, False)
            mixing.append((decay * gt_ref[at]).astype(low))
            grams = grams + decay * grad_mix[head * SPAN : (head + 1) * SPAN]
        dg_ref[at] = grams
        grad_stepped = dot(jnp.concatenate(mixing, 1), split_heads(grad_low))
        last = cum[SPAN - 1 : SPAN]
        at_end = jnp.zeros((1, LANES), wide)
        carry = masks_ref[3, end] * jnp.exp2(last)
        if c + 1 < blocks:
            tail = jnp.exp2(last - cum) * masks_ref[4, at]
            grad_state_low = grad_state.astype(low)
            from_tail = dot(b_ref[at], grad_state_low) * tail
            grad_stepped = grad_stepped + from_tail
            db_ref[at] += contract_cols((stepped * tail).astype(low), grad_state_low)
            at_end = jnp.sum(stepped.astype(wide) * from_tail, axis=0, keepdims=True)
            at_end = at_end + carry * jnp.sum(state_scr[c] * grad_state, axis=0, keepdims=True)
        if c > 0:
            reach = (grad * (jnp.exp2(cum) * masks_ref[3, at])).astype(low)
            dc_ref[at] += contract_cols(reach, state_scr[c].astype(low))
            grad_state = carry * grad_state + dot(ct_ref[:, at], reach)
        z = grad_low.astype(wide) * y - stepped.astype(wide) * grad_stepped
        z = z + jnp.where(row_number == SPAN - 1, at_end, 0.0)
        z_high = z.astype(low)
        z_low = (z - z_high.astype(wide)).astype(low)
        z_ref[at] += dot(z_high, gather) + dot(z_low, gather)
        dt_ref[at] += dot((x * grad_stepped).astype(low), gather)
        grad_skip = grad_skip + jnp.sum(grad * x, axis=0, keepdims=True)
        pre_c = pre_scr[at]
        opened = sigmoid(pre_c)
        grad_x = grad_stepped * dtx + skip_ref[...] * grad
        dpre_scr[at] = grad_x * opened * (1.0 + pre_c * (1.0 - opened))

    back, sums = conv_back(dpre_scr[...], value_ref[...], taps_ref[...], masks)
    value_out[...] = back.astype(low)
    sums_out[...] = jnp.concatenate(sums + [grad_skip, jnp.zeros((2, LANES), wide)], 0)


def post_kernel(
    state_ref, step_ref, taps_ref, bias_ref, step_bias_ref, rate_ref, masks_ref, seg_col_ref,
    seg_row_ref, b_ref, c_ref, db_ref, dc_ref, dg_ref, z_ref, dt_ref,
    state_out, step_out, state_sums, step_sums, act_scr,
):
    rows, states = b_ref.shape
    masks = [masks_ref[k] for k in range(3)]
    triangle = lower_triangle()
    for c in range(rows // SPAN):
        at = slice(c * SPAN, (c + 1) * SPAN)
        seen = visible_block(seg_col_ref[at], seg_row_ref[:, at], False)
        grams = jnp.where(seen, dg_ref[at], 0.0)
        act_scr[0, at] = db_ref[at] + dot(grams.astype(low), c_ref[at])
        act_scr[1, at] = dc_ref[at] + dot(grams.T.astype(low), b_ref[at])
    for part in (0, 1):
        cols = slice(part * states, (part + 1) * states)
        v = state_ref[:, cols]
        pre = conv_in(v, taps_ref[:, cols], bias_ref[:, cols], masks)
        opened = sigmoid(pre)
        grad = act_scr[part] * opened * (1.0 + pre * (1.0 - opened))
        back, sums = conv_back(grad, v, taps_ref[:, cols], masks)
        state_out[:, cols] = back.astype(low)
        state_sums[:, cols] = jnp.concatenate(sums + [jnp.zeros((3, states), wide)], 0)
    pre = step_ref[...] + step_bias_ref[...]
    step = softplus(pre)
    rate_sum = jnp.zeros((1, LANES), wide)
    bias_sum = jnp.zeros((1, LANES), wide)
    for c in range(rows // SPAN):
        at = slice(c * SPAN, (c + 1) * SPAN)
        grad_rate = contract_rows(triangle, z_ref[at], highest)
        grad_step = (dt_ref[at] + rate_ref[...] * grad_rate) * sigmoid(pre[at])
        step_out[at] = grad_step.astype(low)
        rate_sum = rate_sum + jnp.sum(
            grad_rate * (rate_ref[...] * step[at]), axis=0, keepdims=True
        )
        bias_sum = bias_sum + jnp.sum(grad_step, axis=0, keepdims=True)
    step_sums[...] = jnp.concatenate([bias_sum, rate_sum, jnp.zeros((6, LANES), wide)], 0)


def call(
    kernel, outs, operands, grid=None, in_specs=None, out_specs=None, scratch=(), flops=0, aliases={}
):
    shapes = tuple(jax.ShapeDtypeStruct(shape, kind) for shape, kind in outs)
    moved = sum(a.size * a.dtype.itemsize for a in operands)
    moved += sum(s.size * s.dtype.itemsize for s in shapes)
    extra = {} if grid is None else dict(grid=grid, in_specs=in_specs, out_specs=out_specs)
    return pl.pallas_call(
        kernel,
        out_shape=shapes,
        scratch_shapes=list(scratch),
        compiler_params=pltpu.CompilerParams(vmem_limit_bytes=VMEM_BYTES),
        input_output_aliases=dict(aliases),
        cost_estimate=pl.CostEstimate(flops=flops, bytes_accessed=moved, transcendentals=0),
        **extra,
    )(*operands)


def column_block(rows, first=0):
    return pl.BlockSpec((rows, LANES), lambda i: (0, i + first))


def whole_block(shape):
    return pl.BlockSpec(shape, lambda i: (0,) * len(shape))


def lane_pad(v):
    return jnp.pad(v, ((0, 0), (0, LANES - v.shape[1])))


class Mixer:
    def __init__(
        self, state_in, step_in, conv_state, conv_state_bias, step_bias, decay_log, segments
    ):
        rows = state_in.shape[0]
        self.rows = rows
        self.head_count = step_bias.shape[0]
        self.pairs = (self.head_count + 1) // 2
        self.width = self.pairs * LANES
        self.states = conv_state.shape[1] // 2
        self.blocks = rows // SPAN
        before = [
            jnp.concatenate([jnp.full((k,), -1, jnp.int32), segments[: rows - k]]) == segments
            for k in (1, 2, 3)
        ]
        ends = segments.reshape(self.blocks, SPAN)[:, SPAN - 1]
        previous = jnp.concatenate([jnp.full((1,), -1, jnp.int32), ends[:-1]])
        carried = jnp.repeat(previous, SPAN) == segments
        tail = jnp.repeat(ends, SPAN) == segments
        flags = jnp.stack(before + [carried, tail]).astype(wide)
        self.masks = jnp.broadcast_to(flags[:, :, None], (5, rows, LANES))
        self.shared = (
            state_in,
            lane_pad(step_in),
            conv_state,
            conv_state_bias[None],
            lane_pad(step_bias[None]),
            lane_pad(-jnp.exp(decay_log)[None]),
            self.masks,
            segments[:, None],
            segments[None],
        )
        (
            self.b, self.c, self.bt, self.ct, self.g, self.gt, self.dtx, self.cumx, cumt,
        ) = call(
            prep_kernel,
            [((rows, self.states), low)] * 2
            + [((self.states, rows), low)] * 2
            + [((rows, SPAN), wide)] * 2
            + [((rows, self.width), wide)] * 2
            + [((LANES, rows), wide)],
            self.shared,
            flops=12 * rows * LANES * self.width,
        )
        self.cumt = cumt[: 2 * self.pairs].reshape(self.pairs, 2, rows)

    def widen(self, v):
        return jnp.pad(v, ((0, 0), (0, self.width - v.shape[1])))

    def forward(self, value_in, conv_value, conv_value_bias, skip_scale):
        rows, states = self.rows, self.states
        self.inner = value_in.shape[1]
        self.value = (
            self.widen(value_in),
            self.widen(conv_value),
            self.widen(conv_value_bias[None]),
            self.widen(jnp.repeat(skip_scale, HALF)[None]),
        )
        (mixed,) = call(
            fwd_kernel,
            [((rows, self.width), wide)],
            self.value + (self.dtx, self.cumx, self.cumt, self.masks, self.c, self.bt, self.g),
            grid=(self.pairs,),
            in_specs=[
                column_block(rows),
                column_block(4),
                column_block(1),
                column_block(1),
                column_block(rows),
                column_block(rows),
                pl.BlockSpec((1, 2, rows), lambda i: (i, 0, 0)),
                whole_block((5, rows, LANES)),
                whole_block((rows, states)),
                whole_block((states, rows)),
                whole_block((rows, SPAN)),
            ],
            out_specs=[column_block(rows)],
            scratch=[pltpu.VMEM((rows, LANES), wide)],
            flops=20 * rows * LANES * self.width,
        )
        self.mixed = mixed
        return mixed[:, : self.inner]

    def backward_part(self, grad_mixed, first, last, earlier=()):
        rows, states = self.rows, self.states
        operands = (
            (self.value[0], self.mixed, self.widen(grad_mixed))
            + self.value[1:]
            + (self.dtx, self.cumx, self.cumt, self.masks, self.b, self.c, self.bt, self.ct)
            + (self.gt,)
        )
        totals = [whole_block((rows, LANES))] * 5
        resumed = bool(earlier)
        return call(
            functools.partial(bwd_kernel, first, resumed),
            [((rows, self.width), low), ((8, self.width), wide)]
            + [((rows, LANES), wide)] * 5,
            operands + tuple(earlier),
            grid=(last - first,),
            in_specs=[
                column_block(rows, first),
                column_block(rows, first),
                column_block(rows, first),
                column_block(4, first),
                column_block(1, first),
                column_block(1, first),
                column_block(rows, first),
                column_block(rows, first),
                pl.BlockSpec((1, 2, rows), lambda i: (i + first, 0, 0)),
                whole_block((5, rows, LANES)),
                whole_block((rows, states)),
                whole_block((rows, states)),
                whole_block((states, rows)),
                whole_block((states, rows)),
                whole_block((rows, SPAN)),
            ]
            + ([pl.BlockSpec(memory_space=pl.ANY)] * 2 + totals if resumed else []),
            out_specs=[column_block(rows, first), column_block(8, first)] + totals,
            scratch=[pltpu.VMEM((rows, LANES), wide)] * 3
            + [pltpu.VMEM((self.blocks, states, LANES), wide)],
            flops=60 * rows * LANES * (last - first) * LANES,
            aliases={len(operands): 0, len(operands) + 1: 1} if resumed else {},
        )

    def backward_end(self, db, dc, dg, z, dt):
        rows, states = self.rows, self.states
        return call(
            post_kernel,
            [
                ((rows, 2 * states), low),
                ((rows, LANES), low),
                ((8, 2 * states), wide),
                ((8, LANES), wide),
            ],
            self.shared + (self.b, self.c, db, dc, dg, z, dt),
            scratch=[pltpu.VMEM((2, rows, states), wide)],
            flops=12 * rows * LANES * self.width,
        )

    def backward(self, grad_mixed):
        half = (self.pairs + 1) // 2
        part = self.backward_part(grad_mixed, 0, half)
        value_grad, sums, *totals = self.backward_part(grad_mixed, half, self.pairs, part)
        return self.gradients(value_grad, sums, *self.backward_end(*totals))

    def gradients(self, value_grad, sums, state_grad, step_grad, state_sums, step_sums):
        heads = self.head_count
        skip_grad = sums[5, : self.inner].reshape(heads, HALF).sum(axis=1)
        return (
            value_grad[:, : self.inner],
            state_grad,
            step_grad[:, :heads],
            sums[:4, : self.inner],
            sums[4, : self.inner],
            state_sums[:4],
            state_sums[4],
            step_sums[0, :heads],
            step_sums[1, :heads],
            skip_grad,
        )


def ring_place(index, count):
    return jnp.where(index % 2 == 0, index // 2, count - 1 - index // 2)


def ring_index(place, count):
    place = place % count
    return jnp.where(place < (count + 1) // 2, 2 * place, 2 * (count - 1 - place) + 1)


def ring_moves(count):
    order = list(range(0, count, 2)) + list(range(1, count, 2))[::-1]
    ahead = [(order[k], order[(k + 1) % count]) for k in range(count)]
    return ahead, [(target, source) for source, target in ahead]


def ring_gather(shard, splits):
    count = lax.axis_size("gx")
    ahead, behind = ring_moves(count)
    me = lax.axis_index("gx")
    place = ring_place(me, count)
    rows, width = shard.shape
    half = rows // 2
    edges = [0] + splits + [width]
    fulls = [jnp.zeros((count * rows, hi - lo), shard.dtype) for lo, hi in zip(edges, edges[1:])]

    def put(fulls, piece, start):
        return [
            lax.dynamic_update_slice(full, piece[:, lo:hi], (start, 0))
            for full, lo, hi in zip(fulls, edges, edges[1:])
        ]

    fulls = put(fulls, shard, me * rows)
    up, down = shard[:half], shard[half:]
    for step in range(1, count):
        up = lax.ppermute(up, "gx", ahead)
        down = lax.ppermute(down, "gx", behind)
        fulls = put(fulls, up, ring_index(place - step, count) * rows)
        fulls = put(fulls, down, ring_index(place + step, count) * rows + half)
    return fulls, (up, down)


class RingSum:
    def __init__(self, partial):
        self.count = lax.axis_size("gx")
        self.moves = ring_moves(self.count)
        self.place = ring_place(lax.axis_index("gx"), self.count)
        self.rows = partial.shape[0] // self.count
        self.half = self.rows // 2
        self.partial = partial
        self.taken = 0
        self.held = (self.part(-1, 0), self.part(1, self.half))

    def part(self, target, offset):
        start = ring_index(self.place + target, self.count) * self.rows + offset
        return lax.dynamic_slice_in_dim(self.partial, start, self.half, 0)

    def step(self, times=1):
        for _ in range(min(times, self.count - 1 - self.taken)):
            self.taken += 1
            up, down = (
                lax.ppermute(held, "gx", move).astype(wide)
                for held, move in zip(self.held, self.moves)
            )
            up = up + self.part(-1 - self.taken, 0).astype(wide)
            down = down + self.part(1 + self.taken, self.half).astype(wide)
            if self.taken < self.count - 1:
                up, down = up.astype(low), down.astype(low)
            self.held = (up, down)
        return self.held

    def finish(self):
        return jnp.concatenate(self.step(self.count), 0)


def flips(count, bit):
    return [(k, k ^ bit) for k in range(count)]


def halving_sum(partial, axis):
    count = lax.axis_size(axis)
    me = lax.axis_index(axis)
    held = partial.reshape(count, partial.shape[0] // count, partial.shape[1])
    bit = 1
    while bit < count:
        pairs = held.reshape(held.shape[0] // 2, 2, *held.shape[1:])
        mine = (me // bit) % 2
        kept = lax.dynamic_index_in_dim(pairs, mine, 1, keepdims=False)
        given = lax.dynamic_index_in_dim(pairs, 1 - mine, 1, keepdims=False)
        got = lax.ppermute(given, axis, flips(count, bit))
        held = (kept.astype(wide) + got.astype(wide)).astype(partial.dtype)
        bit *= 2
    return held[0]


def butterfly_sum(v, axis):
    count = lax.axis_size(axis)
    bit = 1
    while bit < count:
        v = v + lax.ppermute(v, axis, flips(count, bit))
        bit *= 2
    return v


def scatter_rows(partial):
    return lax.psum_scatter(partial, "gx", scatter_dimension=0, tiled=True)


def row_major(v):
    return with_layout_constraint(v, Layout((0, 1)))


def after(value, *others):
    return lax.optimization_barrier((value,) + others)[0]


def on_device(
    layer_input,
    norm_gain,
    gate_weight,
    value_weight,
    state_weight,
    step_weight,
    conv_value,
    conv_value_bias,
    conv_state,
    conv_state_bias,
    step_bias,
    decay_log,
    skip_scale,
    gated_gain,
    out_weight,
    segment_ids,
    cotangent,
):
    model_width = layer_input.shape[1]
    col_width = cotangent.shape[1]
    state_cols = state_weight.shape[1]
    col_start = lax.axis_index("gy") * col_width

    state_step_weight = jnp.concatenate([state_weight, step_weight], 1)
    full_state = lax.all_gather(state_step_weight, "gx", axis=0, tiled=True)
    upstream = lax.all_gather(cotangent, "gy", axis=1, tiled=True)
    full_out = lax.all_gather(out_weight.T, "gx", axis=0, tiled=True)
    (full_value,), moved = ring_gather(value_weight, [])
    (full_gate,), moved = ring_gather(after(gate_weight, *moved), [])

    tokens = layer_input.astype(wide)
    scale_in = lax.rsqrt(jnp.mean(tokens * tokens, axis=1, keepdims=True) + epsilon)
    normed = (tokens * scale_in * norm_gain).astype(low)

    state_step = dot(normed, full_state)
    mixer = Mixer(
        state_step[:, :state_cols],
        state_step[:, state_cols:],
        conv_state,
        conv_state_bias,
        step_bias,
        decay_log,
        segment_ids,
    )
    value_in = dot(normed, full_value)
    mixed = mixer.forward(value_in, conv_value, conv_value_bias, skip_scale)
    full_value_state = jnp.concatenate([full_value, full_state], 1)
    up_back = dot(upstream, full_out)
    gate_in = dot(normed, full_gate)
    gate_open = jax.nn.sigmoid(gate_in)
    gate_act = gate_in * gate_open
    gated = mixed * gate_act

    sums_out = lax.psum(
        jnp.stack(
            [jnp.sum(gated * gated, axis=1), jnp.sum(gated * gated_gain * up_back, axis=1)]
        ),
        "gy",
    )
    scale_out = lax.rsqrt(sums_out[0] / INNER + epsilon)[:, None]
    grad_scale = sums_out[1][:, None]
    scaled = (gated * gated_gain).astype(low)

    scaled_out = (gated * gated_gain * scale_out).astype(low)
    out_ring = RingSum(row_major(contract_rows(upstream, scaled_out).astype(low)))

    grad_scaled = scale_out * after(up_back, *out_ring.held)
    grad_gated = grad_scaled * gated_gain - grad_scale * scale_out**3 * gated / INNER
    gate_gain_part = jnp.sum(grad_scaled * gated, axis=0)
    grad_gate_in = (
        grad_gated * mixed * gate_open * (1.0 + gate_in * (1.0 - gate_open))
    ).astype(low)
    grad_mixed = grad_gated * gate_act
    gate_partial = contract_rows(after(normed, *out_ring.step()), grad_gate_in)
    gate_ring = RingSum(row_major(gate_partial.astype(low)))

    half = (mixer.pairs + 1) // 2
    part = mixer.backward_part(after(grad_mixed, *out_ring.step(), *gate_ring.held), 0, half)
    grad_mixed = after(grad_mixed, *out_ring.step(), *gate_ring.step(), part[0])
    value_grad, value_sums, *totals = mixer.backward_part(grad_mixed, half, mixer.pairs, part)
    grad_value_in = value_grad[:, : gate_weight.shape[1]]
    value_partial = contract_rows(
        after(normed, *out_ring.step(), *gate_ring.step()), grad_value_in
    )
    value_ring = RingSum(row_major(value_partial.astype(low)))
    ends = mixer.backward_end(
        after(totals[0], *out_ring.step(), *gate_ring.step(), *value_ring.held), *totals[1:]
    )
    pulled = mixer.gradients(value_grad, value_sums, *ends)
    grad_state_in = jnp.concatenate([pulled[1], pulled[2]], 1)
    state_partial = row_major(contract_rows(normed, grad_state_in).astype(low))
    grad_state_step = scatter_rows(state_partial).astype(wide)

    held = out_ring.step() + gate_ring.step() + value_ring.step()
    grad_normed_part = contract_cols(full_gate, after(grad_gate_in, state_partial, *held))
    grad_value_state_in = jnp.concatenate([grad_value_in, grad_state_in], 1)
    held = out_ring.step() + gate_ring.step() + value_ring.step()
    grad_value_state_in = after(grad_value_state_in, *held)
    grad_normed_part = grad_normed_part + contract_cols(full_value_state, grad_value_state_in)
    grad_normed_part = grad_normed_part.astype(low)
    held = gate_ring.step() + value_ring.step()
    product_part = contract_cols(full_out, after(scaled, grad_normed_part, *held))
    product_part = (product_part * scale_out[:, 0]).astype(low)
    grad_out = out_ring.finish()
    grad_gate = gate_ring.finish()
    grad_value = value_ring.finish()

    grad_normed = halving_sum(grad_normed_part, "gy").T.astype(wide)
    token_cols = lax.dynamic_slice_in_dim(layer_input, col_start, col_width, 1).astype(wide)
    gain_cols = lax.dynamic_slice_in_dim(norm_gain, col_start, col_width, 0)
    weighted = grad_normed * gain_cols
    inner_dot = lax.psum(jnp.sum(weighted * token_cols, axis=1), "gy")[:, None]
    grad_input = (
        cotangent.astype(wide)
        + scale_in * weighted
        - token_cols * scale_in**3 * inner_dot / model_width
    )
    grad_norm_gain = butterfly_sum(jnp.sum(grad_normed * token_cols * scale_in, axis=0), "gx")
    product = halving_sum(product_part, "gy").T
    layer_output = (token_cols + product.astype(wide)).astype(low)

    small = (gate_gain_part,) + pulled[3:]
    packed = jnp.concatenate([v.reshape(-1) for v in small])
    packed = butterfly_sum(after(packed, product_part), "gx")
    sums, start = [], 0
    for v in small:
        sums.append(packed[start : start + v.size].reshape(v.shape))
        start += v.size
    state_sums = butterfly_sum(
        jnp.concatenate([grad_state_step[:, :state_cols], sums[3], sums[4][None]], 0), "gy"
    )
    state_rows = state_weight.shape[0]
    return (
        layer_output,
        grad_input,
        grad_norm_gain,
        grad_gate,
        grad_value,
        state_sums[:state_rows],
        grad_state_step[:, state_cols:],
        sums[1],
        sums[2],
        state_sums[state_rows:-1],
        state_sums[-1],
        sums[5],
        sums[6],
        sums[7],
        sums[0],
        grad_out.T,
    )


def solution(mesh):
    return jax.shard_map(
        on_device,
        mesh=mesh,
        in_specs=(
            P("gx", None),
            P(),
            P("gx", "gy"),
            P("gx", "gy"),
            P("gx", None),
            P("gx", "gy"),
            P(None, "gy"),
            P("gy"),
            P(),
            P(),
            P("gy"),
            P("gy"),
            P("gy"),
            P("gy"),
            P("gy", "gx"),
            P("gx"),
            P("gx", "gy"),
        ),
        out_specs=(
            P("gx", "gy"),
            P("gx", "gy"),
            P("gy"),
            P("gx", "gy"),
            P("gx", "gy"),
            P("gx", None),
            P("gx", "gy"),
            P(None, "gy"),
            P("gy"),
            P(),
            P(),
            P("gy"),
            P("gy"),
            P("gy"),
            P("gy"),
            P("gy", "gx"),
        ),
        check_vma=False,
    )
```

```python
import functools

import jax
import jax.numpy as jnp
from jax import lax
from jax.experimental import pallas as pl
from jax.experimental.layout import Layout, with_layout_constraint
from jax.experimental.pallas import tpu as pltpu
from jax.sharding import PartitionSpec as P

INNER = 5120
SPAN = 128
LANES = 128
HALF = 64
LOG2E = 1.4426950408889634
VMEM_BYTES = 56 * 1024 * 1024

epsilon = 1e-05
highest = lax.Precision.HIGHEST
low = jnp.bfloat16
wide = jnp.float32


def dot(left, right, precision=None):
    return jnp.dot(left, right, preferred_element_type=wide, precision=precision)


def contract_rows(left, right, precision=None):
    return lax.dot_general(
        left, right, (((0,), (0,)), ((), ())), preferred_element_type=wide, precision=precision
    )


def contract_cols(left, right, precision=None):
    return lax.dot_general(
        left, right, (((1,), (1,)), ((), ())), preferred_element_type=wide, precision=precision
    )


def sigmoid(v):
    return 1.0 / (1.0 + jnp.exp(-v))


def softplus(v):
    return jnp.maximum(v, 0.0) + jnp.log1p(jnp.exp(-jnp.abs(v)))


def conv_in(v, taps, bias, masks):
    total = bias + taps[0:1] * v
    for k in range(1, 4):
        total = total + taps[k : k + 1] * (pltpu.roll(v, k, 0) * masks[k - 1])
    return total


def conv_back(grad, v, taps, masks):
    rows = grad.shape[0]
    back = taps[0:1] * grad
    sums = [jnp.sum(grad * v, axis=0, keepdims=True)]
    for k in range(1, 4):
        kept = grad * masks[k - 1]
        sums.append(jnp.sum(kept * pltpu.roll(v, k, 0), axis=0, keepdims=True))
        back = back + taps[k : k + 1] * pltpu.roll(kept, rows - k, 0)
    sums.append(jnp.sum(grad, axis=0, keepdims=True))
    return back, sums


def visible_block(seg_col, seg_row, row_is_query):
    shape = (SPAN, SPAN)
    first = lax.broadcasted_iota(jnp.int32, shape, 0)
    second = lax.broadcasted_iota(jnp.int32, shape, 1)
    ordered = (first >= second) if row_is_query else (first <= second)
    return ordered & (seg_col == seg_row)


def lower_triangle():
    shape = (SPAN, SPAN)
    return (
        lax.broadcasted_iota(jnp.int32, shape, 0) >= lax.broadcasted_iota(jnp.int32, shape, 1)
    ).astype(wide)


def prep_kernel(
    state_ref, step_ref, taps_ref, bias_ref, step_bias_ref, rate_ref, masks_ref, seg_col_ref,
    seg_row_ref, b_ref, c_ref, bt_ref, ct_ref, g_ref, gt_ref, dtx_ref, cumx_ref, cumt_ref,
):
    rows, states = b_ref.shape
    masks = [masks_ref[k] for k in range(3)]
    for part, (out, out_t) in enumerate(((b_ref, bt_ref), (c_ref, ct_ref))):
        cols = slice(part * states, (part + 1) * states)
        pre = conv_in(state_ref[:, cols], taps_ref[:, cols], bias_ref[:, cols], masks)
        act = pre * sigmoid(pre)
        out[...] = act.astype(low)
        out_t[...] = act.T.astype(low)
    step = softplus(step_ref[...] + step_bias_ref[...])
    triangle = lower_triangle()
    heads = lax.broadcasted_iota(jnp.int32, (LANES, dtx_ref.shape[1]), 0)
    channels = lax.broadcasted_iota(jnp.int32, (LANES, dtx_ref.shape[1]), 1)
    expand = (channels // HALF == heads).astype(wide)
    rate = step * (rate_ref[...] * LOG2E)
    for c in range(rows // SPAN):
        at = slice(c * SPAN, (c + 1) * SPAN)
        grams = dot(c_ref[at], bt_ref[:, at])
        g_ref[at] = jnp.where(visible_block(seg_col_ref[at], seg_row_ref[:, at], True), grams, 0.0)
        grams_t = dot(b_ref[at], ct_ref[:, at])
        gt_ref[at] = jnp.where(
            visible_block(seg_col_ref[at], seg_row_ref[:, at], False), grams_t, 0.0
        )
        total = dot(triangle, rate[at], highest)
        cumx_ref[at] = dot(total, expand, highest)
        dtx_ref[at] = dot(step[at], expand, highest)
        cumt_ref[:, at] = total.T


def decays(cumx_ref, cumt_ref, at, head, row_is_query):
    lane = head * HALF
    column = cumx_ref[at, lane : lane + 1]
    row = cumt_ref[0, head : head + 1, at]
    gap = (column - row) if row_is_query else (row - column)
    return jnp.exp2(jnp.minimum(gap, 0.0))


def split_heads(block):
    left = lax.broadcasted_iota(jnp.int32, block.shape, 1) < HALF
    zero = jnp.zeros_like(block)
    return jnp.concatenate([jnp.where(left, block, zero), jnp.where(left, zero, block)], 0)


def fwd_kernel(
    value_ref, taps_ref, bias_ref, skip_ref, dtx_ref, cumx_ref, cumt_ref, masks_ref, c_ref, bt_ref,
    g_ref, out_ref, x_scr,
):
    rows = value_ref.shape[0]
    masks = [masks_ref[k] for k in range(3)]
    pre = conv_in(value_ref[...], taps_ref[...], bias_ref[...], masks)
    x_scr[...] = pre * sigmoid(pre)
    state = jnp.zeros((c_ref.shape[1], LANES), wide)
    for c in range(rows // SPAN):
        at = slice(c * SPAN, (c + 1) * SPAN)
        x = x_scr[at]
        cum = cumx_ref[at]
        stepped = x * dtx_ref[at]
        mixing = jnp.concatenate(
            [decays(cumx_ref, cumt_ref, at, head, True) * g_ref[at] for head in (0, 1)], 1
        ).astype(low)
        y = dot(mixing, split_heads(stepped.astype(low)))
        if c > 0:
            y = y + dot(c_ref[at], state.astype(low)) * (jnp.exp2(cum) * masks_ref[3, at])
        out_ref[at] = y + skip_ref[...] * x
        if c + 1 < rows // SPAN:
            end = slice((c + 1) * SPAN - 1, (c + 1) * SPAN)
            last = cum[SPAN - 1 : SPAN]
            tail = jnp.exp2(last - cum) * masks_ref[4, at]
            fresh = dot(bt_ref[:, at], (stepped.astype(low) * tail).astype(low))
            state = (masks_ref[3, end] * jnp.exp2(last)) * state + fresh


def bwd_kernel(
    first, resumed, value_ref, mixed_ref, grad_ref, taps_ref, bias_ref, skip_ref, dtx_ref, cumx_ref, cumt_ref,
    masks_ref, b_ref, c_ref, bt_ref, ct_ref, gt_ref, *more,
):
    earlier, more = more[: 7 * resumed], more[7 * resumed :]
    value_out, sums_out, *totals, pre_scr, x_scr, dpre_scr, state_scr = more
    db_ref, dc_ref, dg_ref, z_ref, dt_ref = totals
    rows = value_ref.shape[0]
    blocks = rows // SPAN
    pair = pl.program_id(0) + first
    masks = [masks_ref[k] for k in range(3)]

    @pl.when(pl.program_id(0) == 0)
    def _():
        for place, ref in enumerate(totals):
            ref[...] = earlier[2 + place][...] if resumed else jnp.zeros_like(ref)

    pre = conv_in(value_ref[...], taps_ref[...], bias_ref[...], masks)
    pre_scr[...] = pre
    x_scr[...] = pre * sigmoid(pre)
    state = jnp.zeros((c_ref.shape[1], LANES), wide)
    for c in range(blocks):
        at = slice(c * SPAN, (c + 1) * SPAN)
        state_scr[c] = state
        if c + 1 < blocks:
            end = slice((c + 1) * SPAN - 1, (c + 1) * SPAN)
            cum = cumx_ref[at]
            last = cum[SPAN - 1 : SPAN]
            tail = jnp.exp2(last - cum) * masks_ref[4, at]
            stepped = (x_scr[at] * dtx_ref[at]).astype(low)
            fresh = dot(bt_ref[:, at], (stepped * tail).astype(low))
            state = (masks_ref[3, end] * jnp.exp2(last)) * state + fresh

    lanes = lax.broadcasted_iota(jnp.int32, (LANES, LANES), 0)
    heads = lax.broadcasted_iota(jnp.int32, (LANES, LANES), 1)
    gather = (lanes // HALF + 2 * pair == heads).astype(low)
    row_number = lax.broadcasted_iota(jnp.int32, (SPAN, LANES), 0)
    grad_skip = jnp.zeros((1, LANES), wide)
    grad_state = jnp.zeros((c_ref.shape[1], LANES), wide)
    for c in reversed(range(blocks)):
        at = slice(c * SPAN, (c + 1) * SPAN)
        end = slice((c + 1) * SPAN - 1, (c + 1) * SPAN)
        x = x_scr[at]
        dtx = dtx_ref[at]
        cum = cumx_ref[at]
        grad = grad_ref[at]
        grad_low = grad.astype(low)
        stepped = (x * dtx).astype(low)
        y = mixed_ref[at] - skip_ref[...] * x
        grad_mix = contract_cols(split_heads(stepped), grad_low)
        mixing = []
        grams = dg_ref[at]
        for head in (0, 1):
            decay = decays(cumx_ref, cumt_ref, at, head, False)
            mixing.append((decay * gt_ref[at]).astype(low))
            grams = grams + decay * grad_mix[head * SPAN : (head + 1) * SPAN]
        dg_ref[at] = grams
        grad_stepped = dot(jnp.concatenate(mixing, 1), split_heads(grad_low))
        last = cum[SPAN - 1 : SPAN]
        at_end = jnp.zeros((1, LANES), wide)
        carry = masks_ref[3, end] * jnp.exp2(last)
        if c + 1 < blocks:
            tail = jnp.exp2(last - cum) * masks_ref[4, at]
            grad_state_low = grad_state.astype(low)
            from_tail = dot(b_ref[at], grad_state_low) * tail
            grad_stepped = grad_stepped + from_tail
            db_ref[at] += contract_cols((stepped * tail).astype(low), grad_state_low)
            at_end = jnp.sum(stepped.astype(wide) * from_tail, axis=0, keepdims=True)
            at_end = at_end + carry * jnp.sum(state_scr[c] * grad_state, axis=0, keepdims=True)
        if c > 0:
            reach = (grad * (jnp.exp2(cum) * masks_ref[3, at])).astype(low)
            dc_ref[at] += contract_cols(reach, state_scr[c].astype(low))
            grad_state = carry * grad_state + dot(ct_ref[:, at], reach)
        z = grad_low.astype(wide) * y - stepped.astype(wide) * grad_stepped
        z = z + jnp.where(row_number == SPAN - 1, at_end, 0.0)
        z_high = z.astype(low)
        z_low = (z - z_high.astype(wide)).astype(low)
        z_ref[at] += dot(z_high, gather) + dot(z_low, gather)
        dt_ref[at] += dot((x * grad_stepped).astype(low), gather)
        grad_skip = grad_skip + jnp.sum(grad * x, axis=0, keepdims=True)
        pre_c = pre_scr[at]
        opened = sigmoid(pre_c)
        grad_x = grad_stepped * dtx + skip_ref[...] * grad
        dpre_scr[at] = grad_x * opened * (1.0 + pre_c * (1.0 - opened))

    back, sums = conv_back(dpre_scr[...], value_ref[...], taps_ref[...], masks)
    value_out[...] = back.astype(low)
    sums_out[...] = jnp.concatenate(sums + [grad_skip, jnp.zeros((2, LANES), wide)], 0)


def post_kernel(
    state_ref, step_ref, taps_ref, bias_ref, step_bias_ref, rate_ref, masks_ref, seg_col_ref,
    seg_row_ref, b_ref, c_ref, db_ref, dc_ref, dg_ref, z_ref, dt_ref,
    state_out, step_out, state_sums, step_sums, act_scr,
):
    rows, states = b_ref.shape
    masks = [masks_ref[k] for k in range(3)]
    triangle = lower_triangle()
    for c in range(rows // SPAN):
        at = slice(c * SPAN, (c + 1) * SPAN)
        seen = visible_block(seg_col_ref[at], seg_row_ref[:, at], False)
        grams = jnp.where(seen, dg_ref[at], 0.0)
        act_scr[0, at] = db_ref[at] + dot(grams.astype(low), c_ref[at])
        act_scr[1, at] = dc_ref[at] + dot(grams.T.astype(low), b_ref[at])
    for part in (0, 1):
        cols = slice(part * states, (part + 1) * states)
        v = state_ref[:, cols]
        pre = conv_in(v, taps_ref[:, cols], bias_ref[:, cols], masks)
        opened = sigmoid(pre)
        grad = act_scr[part] * opened * (1.0 + pre * (1.0 - opened))
        back, sums = conv_back(grad, v, taps_ref[:, cols], masks)
        state_out[:, cols] = back.astype(low)
        state_sums[:, cols] = jnp.concatenate(sums + [jnp.zeros((3, states), wide)], 0)
    pre = step_ref[...] + step_bias_ref[...]
    step = softplus(pre)
    rate_sum = jnp.zeros((1, LANES), wide)
    bias_sum = jnp.zeros((1, LANES), wide)
    for c in range(rows // SPAN):
        at = slice(c * SPAN, (c + 1) * SPAN)
        grad_rate = contract_rows(triangle, z_ref[at], highest)
        grad_step = (dt_ref[at] + rate_ref[...] * grad_rate) * sigmoid(pre[at])
        step_out[at] = grad_step.astype(low)
        rate_sum = rate_sum + jnp.sum(
            grad_rate * (rate_ref[...] * step[at]), axis=0, keepdims=True
        )
        bias_sum = bias_sum + jnp.sum(grad_step, axis=0, keepdims=True)
    step_sums[...] = jnp.concatenate([bias_sum, rate_sum, jnp.zeros((6, LANES), wide)], 0)


def call(
    kernel, outs, operands, grid=None, in_specs=None, out_specs=None, scratch=(), flops=0, aliases={}
):
    shapes = tuple(jax.ShapeDtypeStruct(shape, kind) for shape, kind in outs)
    moved = sum(a.size * a.dtype.itemsize for a in operands)
    moved += sum(s.size * s.dtype.itemsize for s in shapes)
    extra = {} if grid is None else dict(grid=grid, in_specs=in_specs, out_specs=out_specs)
    return pl.pallas_call(
        kernel,
        out_shape=shapes,
        scratch_shapes=list(scratch),
        compiler_params=pltpu.CompilerParams(vmem_limit_bytes=VMEM_BYTES),
        input_output_aliases=dict(aliases),
        cost_estimate=pl.CostEstimate(flops=flops, bytes_accessed=moved, transcendentals=0),
        **extra,
    )(*operands)


def column_block(rows, first=0):
    return pl.BlockSpec((rows, LANES), lambda i: (0, i + first))


def whole_block(shape):
    return pl.BlockSpec(shape, lambda i: (0,) * len(shape))


def lane_pad(v):
    return jnp.pad(v, ((0, 0), (0, LANES - v.shape[1])))


class Mixer:
    def __init__(
        self, state_in, step_in, conv_state, conv_state_bias, step_bias, decay_log, segments
    ):
        rows = state_in.shape[0]
        self.rows = rows
        self.head_count = step_bias.shape[0]
        self.pairs = (self.head_count + 1) // 2
        self.width = self.pairs * LANES
        self.states = conv_state.shape[1] // 2
        self.blocks = rows // SPAN
        before = [
            jnp.concatenate([jnp.full((k,), -1, jnp.int32), segments[: rows - k]]) == segments
            for k in (1, 2, 3)
        ]
        ends = segments.reshape(self.blocks, SPAN)[:, SPAN - 1]
        previous = jnp.concatenate([jnp.full((1,), -1, jnp.int32), ends[:-1]])
        carried = jnp.repeat(previous, SPAN) == segments
        tail = jnp.repeat(ends, SPAN) == segments
        flags = jnp.stack(before + [carried, tail]).astype(wide)
        self.masks = jnp.broadcast_to(flags[:, :, None], (5, rows, LANES))
        self.shared = (
            state_in,
            lane_pad(step_in),
            conv_state,
            conv_state_bias[None],
            lane_pad(step_bias[None]),
            lane_pad(-jnp.exp(decay_log)[None]),
            self.masks,
            segments[:, None],
            segments[None],
        )
        (
            self.b, self.c, self.bt, self.ct, self.g, self.gt, self.dtx, self.cumx, cumt,
        ) = call(
            prep_kernel,
            [((rows, self.states), low)] * 2
            + [((self.states, rows), low)] * 2
            + [((rows, SPAN), wide)] * 2
            + [((rows, self.width), wide)] * 2
            + [((LANES, rows), wide)],
            self.shared,
            flops=12 * rows * LANES * self.width,
        )
        self.cumt = cumt[: 2 * self.pairs].reshape(self.pairs, 2, rows)

    def widen(self, v):
        return jnp.pad(v, ((0, 0), (0, self.width - v.shape[1])))

    def forward(self, value_in, conv_value, conv_value_bias, skip_scale):
        rows, states = self.rows, self.states
        self.inner = value_in.shape[1]
        self.value = (
            self.widen(value_in),
            self.widen(conv_value),
            self.widen(conv_value_bias[None]),
            self.widen(jnp.repeat(skip_scale, HALF)[None]),
        )
        (mixed,) = call(
            fwd_kernel,
            [((rows, self.width), wide)],
            self.value + (self.dtx, self.cumx, self.cumt, self.masks, self.c, self.bt, self.g),
            grid=(self.pairs,),
            in_specs=[
                column_block(rows),
                column_block(4),
                column_block(1),
                column_block(1),
                column_block(rows),
                column_block(rows),
                pl.BlockSpec((1, 2, rows), lambda i: (i, 0, 0)),
                whole_block((5, rows, LANES)),
                whole_block((rows, states)),
                whole_block((states, rows)),
                whole_block((rows, SPAN)),
            ],
            out_specs=[column_block(rows)],
            scratch=[pltpu.VMEM((rows, LANES), wide)],
            flops=20 * rows * LANES * self.width,
        )
        self.mixed = mixed
        return mixed[:, : self.inner]

    def backward_part(self, grad_mixed, first, last, earlier=()):
        rows, states = self.rows, self.states
        operands = (
            (self.value[0], self.mixed, self.widen(grad_mixed))
            + self.value[1:]
            + (self.dtx, self.cumx, self.cumt, self.masks, self.b, self.c, self.bt, self.ct)
            + (self.gt,)
        )
        totals = [whole_block((rows, LANES))] * 5
        resumed = bool(earlier)
        return call(
            functools.partial(bwd_kernel, first, resumed),
            [((rows, self.width), low), ((8, self.width), wide)]
            + [((rows, LANES), wide)] * 5,
            operands + tuple(earlier),
            grid=(last - first,),
            in_specs=[
                column_block(rows, first),
                column_block(rows, first),
                column_block(rows, first),
                column_block(4, first),
                column_block(1, first),
                column_block(1, first),
                column_block(rows, first),
                column_block(rows, first),
                pl.BlockSpec((1, 2, rows), lambda i: (i + first, 0, 0)),
                whole_block((5, rows, LANES)),
                whole_block((rows, states)),
                whole_block((rows, states)),
                whole_block((states, rows)),
                whole_block((states, rows)),
                whole_block((rows, SPAN)),
            ]
            + ([pl.BlockSpec(memory_space=pl.ANY)] * 2 + totals if resumed else []),
            out_specs=[column_block(rows, first), column_block(8, first)] + totals,
            scratch=[pltpu.VMEM((rows, LANES), wide)] * 3
            + [pltpu.VMEM((self.blocks, states, LANES), wide)],
            flops=60 * rows * LANES * (last - first) * LANES,
            aliases={len(operands): 0, len(operands) + 1: 1} if resumed else {},
        )

    def backward_end(self, db, dc, dg, z, dt):
        rows, states = self.rows, self.states
        return call(
            post_kernel,
            [
                ((rows, 2 * states), low),
                ((rows, LANES), low),
                ((8, 2 * states), wide),
                ((8, LANES), wide),
            ],
            self.shared + (self.b, self.c, db, dc, dg, z, dt),
            scratch=[pltpu.VMEM((2, rows, states), wide)],
            flops=12 * rows * LANES * self.width,
        )

    def backward(self, grad_mixed):
        half = (self.pairs + 1) // 2
        part = self.backward_part(grad_mixed, 0, half)
        value_grad, sums, *totals = self.backward_part(grad_mixed, half, self.pairs, part)
        return self.gradients(value_grad, sums, *self.backward_end(*totals))

    def gradients(self, value_grad, sums, state_grad, step_grad, state_sums, step_sums):
        heads = self.head_count
        skip_grad = sums[5, : self.inner].reshape(heads, HALF).sum(axis=1)
        return (
            value_grad[:, : self.inner],
            state_grad,
            step_grad[:, :heads],
            sums[:4, : self.inner],
            sums[4, : self.inner],
            state_sums[:4],
            state_sums[4],
            step_sums[0, :heads],
            step_sums[1, :heads],
            skip_grad,
        )


def ring_place(index, count):
    return jnp.where(index % 2 == 0, index // 2, count - 1 - index // 2)


def ring_index(place, count):
    place = place % count
    return jnp.where(place < (count + 1) // 2, 2 * place, 2 * (count - 1 - place) + 1)


def ring_moves(count):
    order = list(range(0, count, 2)) + list(range(1, count, 2))[::-1]
    ahead = [(order[k], order[(k + 1) % count]) for k in range(count)]
    return ahead, [(target, source) for source, target in ahead]


class RingGather:
    def __init__(self, shard):
        self.count = lax.axis_size("gx")
        self.moves = ring_moves(self.count)
        me = lax.axis_index("gx")
        self.place = ring_place(me, self.count)
        self.rows, width = shard.shape
        self.half = self.rows // 2
        self.taken = 0
        self.held = (shard[: self.half], shard[self.half :])
        full = jnp.zeros((self.count * self.rows, width), shard.dtype)
        self.full = lax.dynamic_update_slice(full, shard, (me * self.rows, 0))

    def step(self, times=1):
        for _ in range(min(times, self.count - 1 - self.taken)):
            self.taken += 1
            self.held = tuple(
                lax.ppermute(held, "gx", move) for held, move in zip(self.held, self.moves)
            )
            for piece, sign, offset in zip(self.held, (-1, 1), (0, self.half)):
                owner = ring_index(self.place + sign * self.taken, self.count)
                start = owner * self.rows + offset
                self.full = lax.dynamic_update_slice(self.full, piece, (start, 0))
        return self.held

    def wait_for(self, *others):
        self.held = (after(self.held[0], *others), self.held[1])

    def finish(self):
        self.step(self.count)
        return self.full


class RingSum:
    def __init__(self, partial):
        self.count = lax.axis_size("gx")
        self.moves = ring_moves(self.count)
        self.place = ring_place(lax.axis_index("gx"), self.count)
        self.rows = partial.shape[0] // self.count
        self.half = self.rows // 2
        self.partial = partial
        self.taken = 0
        self.held = (self.part(-1, 0), self.part(1, self.half))

    def part(self, target, offset):
        start = ring_index(self.place + target, self.count) * self.rows + offset
        return lax.dynamic_slice_in_dim(self.partial, start, self.half, 0)

    def step(self, times=1):
        for _ in range(min(times, self.count - 1 - self.taken)):
            self.taken += 1
            up, down = (
                lax.ppermute(held, "gx", move).astype(wide)
                for held, move in zip(self.held, self.moves)
            )
            up = up + self.part(-1 - self.taken, 0).astype(wide)
            down = down + self.part(1 + self.taken, self.half).astype(wide)
            if self.taken < self.count - 1:
                up, down = up.astype(low), down.astype(low)
            self.held = (up, down)
        return self.held

    def finish(self):
        return jnp.concatenate(self.step(self.count), 0)


def flips(count, bit):
    return [(k, k ^ bit) for k in range(count)]


def halving_sum(partial, axis):
    count = lax.axis_size(axis)
    me = lax.axis_index(axis)
    held = partial.reshape(count, partial.shape[0] // count, partial.shape[1])
    bit = 1
    while bit < count:
        pairs = held.reshape(held.shape[0] // 2, 2, *held.shape[1:])
        mine = (me // bit) % 2
        kept = lax.dynamic_index_in_dim(pairs, mine, 1, keepdims=False)
        given = lax.dynamic_index_in_dim(pairs, 1 - mine, 1, keepdims=False)
        got = lax.ppermute(given, axis, flips(count, bit))
        held = (kept.astype(wide) + got.astype(wide)).astype(partial.dtype)
        bit *= 2
    return held[0]


def butterfly_sum(v, axis):
    count = lax.axis_size(axis)
    bit = 1
    while bit < count:
        v = v + lax.ppermute(v, axis, flips(count, bit))
        bit *= 2
    return v


def scatter_rows(partial):
    return lax.psum_scatter(partial, "gx", scatter_dimension=0, tiled=True)


def row_major(v):
    return with_layout_constraint(v, Layout((0, 1)))


def after(value, *others):
    return lax.optimization_barrier((value,) + others)[0]


def on_device(
    layer_input,
    norm_gain,
    gate_weight,
    value_weight,
    state_weight,
    step_weight,
    conv_value,
    conv_value_bias,
    conv_state,
    conv_state_bias,
    step_bias,
    decay_log,
    skip_scale,
    gated_gain,
    out_weight,
    segment_ids,
    cotangent,
):
    model_width = layer_input.shape[1]
    col_width = cotangent.shape[1]
    state_cols = state_weight.shape[1]
    col_start = lax.axis_index("gy") * col_width

    state_step_weight = jnp.concatenate([state_weight, step_weight], 1)
    full_state = lax.all_gather(state_step_weight, "gx", axis=0, tiled=True)
    full_gate = lax.all_gather(gate_weight, "gx", axis=0, tiled=True)
    upstream = lax.all_gather(cotangent, "gy", axis=1, tiled=True)
    value_gather = RingGather(value_weight)
    value_gather.step()

    tokens = after(layer_input, *value_gather.step()).astype(wide)
    scale_in = lax.rsqrt(jnp.mean(tokens * tokens, axis=1, keepdims=True) + epsilon)
    normed = (tokens * scale_in * norm_gain).astype(low)
    value_gather.step()
    value_gather.wait_for(normed)
    value_gather.step()

    state_step = dot(normed, full_state)
    mixer = Mixer(
        state_step[:, :state_cols],
        state_step[:, state_cols:],
        conv_state,
        conv_state_bias,
        step_bias,
        decay_log,
        segment_ids,
    )
    value_gather.step()
    value_gather.wait_for(mixer.g)
    full_value = value_gather.finish()
    out_gather = RingGather(after(out_weight.T, *value_gather.held))
    value_in = dot(normed, full_value)
    value_in = after(value_in, *out_gather.step())
    mixed = mixer.forward(value_in, conv_value, conv_value_bias, skip_scale)
    out_gather.step(2)
    out_gather.wait_for(mixed)
    full_out = out_gather.finish()
    full_value_state = jnp.concatenate([full_value, full_state], 1)
    gate_in = dot(normed, full_gate)
    gate_open = jax.nn.sigmoid(gate_in)
    gate_act = gate_in * gate_open
    gated = mixed * gate_act
    up_back = dot(upstream, full_out)

    sums_out = lax.psum(
        jnp.stack(
            [jnp.sum(gated * gated, axis=1), jnp.sum(gated * gated_gain * up_back, axis=1)]
        ),
        "gy",
    )
    scale_out = lax.rsqrt(sums_out[0] / INNER + epsilon)[:, None]
    grad_scale = sums_out[1][:, None]
    scaled = (gated * gated_gain).astype(low)

    scaled_out = (gated * gated_gain * scale_out).astype(low)
    out_ring = RingSum(row_major(contract_rows(upstream, scaled_out).astype(low)))

    grad_scaled = scale_out * after(up_back, *out_ring.held)
    grad_gated = grad_scaled * gated_gain - grad_scale * scale_out**3 * gated / INNER
    gate_gain_part = jnp.sum(grad_scaled * gated, axis=0)
    grad_gate_in = (
        grad_gated * mixed * gate_open * (1.0 + gate_in * (1.0 - gate_open))
    ).astype(low)
    grad_mixed = grad_gated * gate_act
    gate_partial = contract_rows(after(normed, *out_ring.step()), grad_gate_in)
    gate_ring = RingSum(row_major(gate_partial.astype(low)))

    first = (mixer.pairs + 2) // 3
    second = (first + mixer.pairs + 1) // 2
    part = mixer.backward_part(after(grad_mixed, *out_ring.step(), *gate_ring.held), 0, first)
    grad_mixed = after(grad_mixed, *out_ring.step(), *gate_ring.step(), part[0])
    part = mixer.backward_part(grad_mixed, first, second, part)
    grad_mixed = after(grad_mixed, *out_ring.step(), *gate_ring.step(), part[0])
    value_grad, value_sums, *totals = mixer.backward_part(grad_mixed, second, mixer.pairs, part)
    grad_value_in = value_grad[:, : gate_weight.shape[1]]
    value_partial = contract_rows(
        after(normed, *out_ring.step(), *gate_ring.step()), grad_value_in
    )
    value_ring = RingSum(row_major(value_partial.astype(low)))
    ends = mixer.backward_end(
        after(totals[0], *out_ring.step(), *gate_ring.step(), *value_ring.held), *totals[1:]
    )
    pulled = mixer.gradients(value_grad, value_sums, *ends)
    grad_state_in = jnp.concatenate([pulled[1], pulled[2]], 1)
    state_partial = row_major(contract_rows(normed, grad_state_in).astype(low))
    grad_state_step = scatter_rows(state_partial).astype(wide)

    held = value_ring.step()
    grad_normed_part = contract_cols(full_gate, after(grad_gate_in, state_partial, *held))
    grad_value_state_in = jnp.concatenate([grad_value_in, grad_state_in], 1)
    held = out_ring.step() + gate_ring.step()
    grad_value_state_in = after(grad_value_state_in, *held)
    grad_normed_part = grad_normed_part + contract_cols(full_value_state, grad_value_state_in)
    grad_normed_part = row_major(grad_normed_part.astype(low))
    held = value_ring.step()
    product_part = contract_cols(full_out, after(scaled, grad_normed_part, *held))
    product_part = row_major((product_part * scale_out[:, 0]).astype(low))
    grad_out = out_ring.finish()
    grad_gate = gate_ring.finish()
    grad_value = value_ring.finish()

    grad_normed = halving_sum(grad_normed_part, "gy").T.astype(wide)
    token_cols = lax.dynamic_slice_in_dim(layer_input, col_start, col_width, 1).astype(wide)
    gain_cols = lax.dynamic_slice_in_dim(norm_gain, col_start, col_width, 0)
    weighted = grad_normed * gain_cols
    inner_dot = lax.psum(jnp.sum(weighted * token_cols, axis=1), "gy")[:, None]
    grad_input = (
        cotangent.astype(wide)
        + scale_in * weighted
        - token_cols * scale_in**3 * inner_dot / model_width
    )
    grad_norm_gain = butterfly_sum(jnp.sum(grad_normed * token_cols * scale_in, axis=0), "gx")
    product = halving_sum(product_part, "gy").T
    layer_output = (token_cols + product.astype(wide)).astype(low)

    small = (gate_gain_part,) + pulled[3:]
    packed = jnp.concatenate([v.reshape(-1) for v in small])
    packed = butterfly_sum(after(packed, product_part), "gx")
    sums, start = [], 0
    for v in small:
        sums.append(packed[start : start + v.size].reshape(v.shape))
        start += v.size
    state_sums = butterfly_sum(
        jnp.concatenate([grad_state_step[:, :state_cols], sums[3], sums[4][None]], 0), "gy"
    )
    state_rows = state_weight.shape[0]
    return (
        layer_output,
        grad_input,
        grad_norm_gain,
        grad_gate,
        grad_value,
        state_sums[:state_rows],
        grad_state_step[:, state_cols:],
        sums[1],
        sums[2],
        state_sums[state_rows:-1],
        state_sums[-1],
        sums[5],
        sums[6],
        sums[7],
        sums[0],
        grad_out.T,
    )


def solution(mesh):
    return jax.shard_map(
        on_device,
        mesh=mesh,
        in_specs=(
            P("gx", None),
            P(),
            P("gx", "gy"),
            P("gx", "gy"),
            P("gx", None),
            P("gx", "gy"),
            P(None, "gy"),
            P("gy"),
            P(),
            P(),
            P("gy"),
            P("gy"),
            P("gy"),
            P("gy"),
            P("gy", "gx"),
            P("gx"),
            P("gx", "gy"),
        ),
        out_specs=(
            P("gx", "gy"),
            P("gx", "gy"),
            P("gy"),
            P("gx", "gy"),
            P("gx", "gy"),
            P("gx", None),
            P("gx", "gy"),
            P(None, "gy"),
            P("gy"),
            P(),
            P(),
            P("gy"),
            P("gy"),
            P("gy"),
            P("gy"),
            P("gy", "gx"),
        ),
        check_vma=False,
    )
```

```python
import functools

import jax
import jax.numpy as jnp
from jax import lax
from jax.experimental import pallas as pl
from jax.experimental.layout import Layout, with_layout_constraint
from jax.experimental.pallas import tpu as pltpu
from jax.sharding import PartitionSpec as P

INNER = 5120
SPAN = 128
LANES = 128
HALF = 64
LOG2E = 1.4426950408889634
VMEM_BYTES = 56 * 1024 * 1024

epsilon = 1e-05
highest = lax.Precision.HIGHEST
low = jnp.bfloat16
wide = jnp.float32


def dot(left, right, precision=None):
    return jnp.dot(left, right, preferred_element_type=wide, precision=precision)


def contract_rows(left, right, precision=None):
    return lax.dot_general(
        left, right, (((0,), (0,)), ((), ())), preferred_element_type=wide, precision=precision
    )


def contract_cols(left, right, precision=None):
    return lax.dot_general(
        left, right, (((1,), (1,)), ((), ())), preferred_element_type=wide, precision=precision
    )


def sigmoid(v):
    return 1.0 / (1.0 + jnp.exp(-v))


def softplus(v):
    return jnp.maximum(v, 0.0) + jnp.log1p(jnp.exp(-jnp.abs(v)))


def conv_in(v, taps, bias, masks):
    total = bias + taps[0:1] * v
    for k in range(1, 4):
        total = total + taps[k : k + 1] * (pltpu.roll(v, k, 0) * masks[k - 1])
    return total


def conv_back(grad, v, taps, masks):
    rows = grad.shape[0]
    back = taps[0:1] * grad
    sums = [jnp.sum(grad * v, axis=0, keepdims=True)]
    for k in range(1, 4):
        kept = grad * masks[k - 1]
        sums.append(jnp.sum(kept * pltpu.roll(v, k, 0), axis=0, keepdims=True))
        back = back + taps[k : k + 1] * pltpu.roll(kept, rows - k, 0)
    sums.append(jnp.sum(grad, axis=0, keepdims=True))
    return back, sums


def visible_block(seg_col, seg_row, row_is_query):
    shape = (SPAN, SPAN)
    first = lax.broadcasted_iota(jnp.int32, shape, 0)
    second = lax.broadcasted_iota(jnp.int32, shape, 1)
    ordered = (first >= second) if row_is_query else (first <= second)
    return ordered & (seg_col == seg_row)


def lower_triangle():
    shape = (SPAN, SPAN)
    return (
        lax.broadcasted_iota(jnp.int32, shape, 0) >= lax.broadcasted_iota(jnp.int32, shape, 1)
    ).astype(wide)


def prep_kernel(
    state_ref, step_ref, taps_ref, bias_ref, step_bias_ref, rate_ref, masks_ref, seg_col_ref,
    seg_row_ref, b_ref, c_ref, bt_ref, ct_ref, g_ref, gt_ref, dtx_ref, cumx_ref, cumt_ref,
):
    rows, states = b_ref.shape
    masks = [masks_ref[k] for k in range(3)]
    for part, (out, out_t) in enumerate(((b_ref, bt_ref), (c_ref, ct_ref))):
        cols = slice(part * states, (part + 1) * states)
        pre = conv_in(state_ref[:, cols], taps_ref[:, cols], bias_ref[:, cols], masks)
        act = pre * sigmoid(pre)
        out[...] = act.astype(low)
        out_t[...] = act.T.astype(low)
    step = softplus(step_ref[...] + step_bias_ref[...])
    triangle = lower_triangle()
    heads = lax.broadcasted_iota(jnp.int32, (LANES, dtx_ref.shape[1]), 0)
    channels = lax.broadcasted_iota(jnp.int32, (LANES, dtx_ref.shape[1]), 1)
    expand = (channels // HALF == heads).astype(wide)
    rate = step * (rate_ref[...] * LOG2E)
    for c in range(rows // SPAN):
        at = slice(c * SPAN, (c + 1) * SPAN)
        grams = dot(c_ref[at], bt_ref[:, at])
        g_ref[at] = jnp.where(visible_block(seg_col_ref[at], seg_row_ref[:, at], True), grams, 0.0)
        grams_t = dot(b_ref[at], ct_ref[:, at])
        gt_ref[at] = jnp.where(
            visible_block(seg_col_ref[at], seg_row_ref[:, at], False), grams_t, 0.0
        )
        total = dot(triangle, rate[at], highest)
        cumx_ref[at] = dot(total, expand, highest)
        dtx_ref[at] = dot(step[at], expand, highest)
        cumt_ref[:, at] = total.T


def decays(cumx_ref, cumt_ref, at, head, row_is_query):
    lane = head * HALF
    column = cumx_ref[at, lane : lane + 1]
    row = cumt_ref[0, head : head + 1, at]
    gap = (column - row) if row_is_query else (row - column)
    return jnp.exp2(jnp.minimum(gap, 0.0))


def split_heads(block):
    left = lax.broadcasted_iota(jnp.int32, block.shape, 1) < HALF
    zero = jnp.zeros_like(block)
    return jnp.concatenate([jnp.where(left, block, zero), jnp.where(left, zero, block)], 0)


def fwd_kernel(
    value_ref, taps_ref, bias_ref, skip_ref, dtx_ref, cumx_ref, cumt_ref, masks_ref, c_ref, bt_ref,
    g_ref, out_ref, x_scr,
):
    rows = value_ref.shape[0]
    masks = [masks_ref[k] for k in range(3)]
    pre = conv_in(value_ref[...], taps_ref[...], bias_ref[...], masks)
    x_scr[...] = pre * sigmoid(pre)
    state = jnp.zeros((c_ref.shape[1], LANES), wide)
    for c in range(rows // SPAN):
        at = slice(c * SPAN, (c + 1) * SPAN)
        x = x_scr[at]
        cum = cumx_ref[at]
        stepped = x * dtx_ref[at]
        mixing = jnp.concatenate(
            [decays(cumx_ref, cumt_ref, at, head, True) * g_ref[at] for head in (0, 1)], 1
        ).astype(low)
        y = dot(mixing, split_heads(stepped.astype(low)))
        if c > 0:
            y = y + dot(c_ref[at], state.astype(low)) * (jnp.exp2(cum) * masks_ref[3, at])
        out_ref[at] = y + skip_ref[...] * x
        if c + 1 < rows // SPAN:
            end = slice((c + 1) * SPAN - 1, (c + 1) * SPAN)
            last = cum[SPAN - 1 : SPAN]
            tail = jnp.exp2(last - cum) * masks_ref[4, at]
            fresh = dot(bt_ref[:, at], (stepped.astype(low) * tail).astype(low))
            state = (masks_ref[3, end] * jnp.exp2(last)) * state + fresh


def bwd_kernel(
    first, resumed, value_ref, mixed_ref, grad_ref, taps_ref, bias_ref, skip_ref, dtx_ref, cumx_ref, cumt_ref,
    masks_ref, b_ref, c_ref, bt_ref, ct_ref, gt_ref, *more,
):
    earlier, more = more[: 7 * resumed], more[7 * resumed :]
    value_out, sums_out, *totals, pre_scr, x_scr, dpre_scr, state_scr = more
    db_ref, dc_ref, dg_ref, z_ref, dt_ref = totals
    rows = value_ref.shape[0]
    blocks = rows // SPAN
    pair = pl.program_id(0) + first
    masks = [masks_ref[k] for k in range(3)]

    @pl.when(pl.program_id(0) == 0)
    def _():
        for place, ref in enumerate(totals):
            ref[...] = earlier[2 + place][...] if resumed else jnp.zeros_like(ref)

    pre = conv_in(value_ref[...], taps_ref[...], bias_ref[...], masks)
    pre_scr[...] = pre
    x_scr[...] = pre * sigmoid(pre)
    state = jnp.zeros((c_ref.shape[1], LANES), wide)
    for c in range(blocks):
        at = slice(c * SPAN, (c + 1) * SPAN)
        state_scr[c] = state
        if c + 1 < blocks:
            end = slice((c + 1) * SPAN - 1, (c + 1) * SPAN)
            cum = cumx_ref[at]
            last = cum[SPAN - 1 : SPAN]
            tail = jnp.exp2(last - cum) * masks_ref[4, at]
            stepped = (x_scr[at] * dtx_ref[at]).astype(low)
            fresh = dot(bt_ref[:, at], (stepped * tail).astype(low))
            state = (masks_ref[3, end] * jnp.exp2(last)) * state + fresh

    lanes = lax.broadcasted_iota(jnp.int32, (LANES, LANES), 0)
    heads = lax.broadcasted_iota(jnp.int32, (LANES, LANES), 1)
    gather = (lanes // HALF + 2 * pair == heads).astype(low)
    row_number = lax.broadcasted_iota(jnp.int32, (SPAN, LANES), 0)
    grad_skip = jnp.zeros((1, LANES), wide)
    grad_state = jnp.zeros((c_ref.shape[1], LANES), wide)
    for c in reversed(range(blocks)):
        at = slice(c * SPAN, (c + 1) * SPAN)
        end = slice((c + 1) * SPAN - 1, (c + 1) * SPAN)
        x = x_scr[at]
        dtx = dtx_ref[at]
        cum = cumx_ref[at]
        grad = grad_ref[at]
        grad_low = grad.astype(low)
        stepped = (x * dtx).astype(low)
        y = mixed_ref[at] - skip_ref[...] * x
        grad_mix = contract_cols(split_heads(stepped), grad_low)
        mixing = []
        grams = dg_ref[at]
        for head in (0, 1):
            decay = decays(cumx_ref, cumt_ref, at, head, False)
            mixing.append((decay * gt_ref[at]).astype(low))
            grams = grams + decay * grad_mix[head * SPAN : (head + 1) * SPAN]
        dg_ref[at] = grams
        grad_stepped = dot(jnp.concatenate(mixing, 1), split_heads(grad_low))
        last = cum[SPAN - 1 : SPAN]
        at_end = jnp.zeros((1, LANES), wide)
        carry = masks_ref[3, end] * jnp.exp2(last)
        if c + 1 < blocks:
            tail = jnp.exp2(last - cum) * masks_ref[4, at]
            grad_state_low = grad_state.astype(low)
            from_tail = dot(b_ref[at], grad_state_low) * tail
            grad_stepped = grad_stepped + from_tail
            db_ref[at] += contract_cols((stepped * tail).astype(low), grad_state_low)
            at_end = jnp.sum(stepped.astype(wide) * from_tail, axis=0, keepdims=True)
            at_end = at_end + carry * jnp.sum(state_scr[c] * grad_state, axis=0, keepdims=True)
        if c > 0:
            reach = (grad * (jnp.exp2(cum) * masks_ref[3, at])).astype(low)
            dc_ref[at] += contract_cols(reach, state_scr[c].astype(low))
            grad_state = carry * grad_state + dot(ct_ref[:, at], reach)
        z = grad_low.astype(wide) * y - stepped.astype(wide) * grad_stepped
        z = z + jnp.where(row_number == SPAN - 1, at_end, 0.0)
        z_high = z.astype(low)
        z_low = (z - z_high.astype(wide)).astype(low)
        z_ref[at] += dot(z_high, gather) + dot(z_low, gather)
        dt_ref[at] += dot((x * grad_stepped).astype(low), gather)
        grad_skip = grad_skip + jnp.sum(grad * x, axis=0, keepdims=True)
        pre_c = pre_scr[at]
        opened = sigmoid(pre_c)
        grad_x = grad_stepped * dtx + skip_ref[...] * grad
        dpre_scr[at] = grad_x * opened * (1.0 + pre_c * (1.0 - opened))

    back, sums = conv_back(dpre_scr[...], value_ref[...], taps_ref[...], masks)
    value_out[...] = back.astype(low)
    sums_out[...] = jnp.concatenate(sums + [grad_skip, jnp.zeros((2, LANES), wide)], 0)


def post_kernel(
    state_ref, step_ref, taps_ref, bias_ref, step_bias_ref, rate_ref, masks_ref, seg_col_ref,
    seg_row_ref, b_ref, c_ref, db_ref, dc_ref, dg_ref, z_ref, dt_ref,
    state_out, step_out, state_sums, step_sums, act_scr,
):
    rows, states = b_ref.shape
    masks = [masks_ref[k] for k in range(3)]
    triangle = lower_triangle()
    for c in range(rows // SPAN):
        at = slice(c * SPAN, (c + 1) * SPAN)
        seen = visible_block(seg_col_ref[at], seg_row_ref[:, at], False)
        grams = jnp.where(seen, dg_ref[at], 0.0)
        act_scr[0, at] = db_ref[at] + dot(grams.astype(low), c_ref[at])
        act_scr[1, at] = dc_ref[at] + dot(grams.T.astype(low), b_ref[at])
    for part in (0, 1):
        cols = slice(part * states, (part + 1) * states)
        v = state_ref[:, cols]
        pre = conv_in(v, taps_ref[:, cols], bias_ref[:, cols], masks)
        opened = sigmoid(pre)
        grad = act_scr[part] * opened * (1.0 + pre * (1.0 - opened))
        back, sums = conv_back(grad, v, taps_ref[:, cols], masks)
        state_out[:, cols] = back.astype(low)
        state_sums[:, cols] = jnp.concatenate(sums + [jnp.zeros((3, states), wide)], 0)
    pre = step_ref[...] + step_bias_ref[...]
    step = softplus(pre)
    rate_sum = jnp.zeros((1, LANES), wide)
    bias_sum = jnp.zeros((1, LANES), wide)
    for c in range(rows // SPAN):
        at = slice(c * SPAN, (c + 1) * SPAN)
        grad_rate = contract_rows(triangle, z_ref[at], highest)
        grad_step = (dt_ref[at] + rate_ref[...] * grad_rate) * sigmoid(pre[at])
        step_out[at] = grad_step.astype(low)
        rate_sum = rate_sum + jnp.sum(
            grad_rate * (rate_ref[...] * step[at]), axis=0, keepdims=True
        )
        bias_sum = bias_sum + jnp.sum(grad_step, axis=0, keepdims=True)
    step_sums[...] = jnp.concatenate([bias_sum, rate_sum, jnp.zeros((6, LANES), wide)], 0)


def call(
    kernel, outs, operands, grid=None, in_specs=None, out_specs=None, scratch=(), flops=0, aliases={}
):
    shapes = tuple(jax.ShapeDtypeStruct(shape, kind) for shape, kind in outs)
    moved = sum(a.size * a.dtype.itemsize for a in operands)
    moved += sum(s.size * s.dtype.itemsize for s in shapes)
    extra = {} if grid is None else dict(grid=grid, in_specs=in_specs, out_specs=out_specs)
    return pl.pallas_call(
        kernel,
        out_shape=shapes,
        scratch_shapes=list(scratch),
        compiler_params=pltpu.CompilerParams(vmem_limit_bytes=VMEM_BYTES),
        input_output_aliases=dict(aliases),
        cost_estimate=pl.CostEstimate(flops=flops, bytes_accessed=moved, transcendentals=0),
        **extra,
    )(*operands)


def column_block(rows, first=0):
    return pl.BlockSpec((rows, LANES), lambda i: (0, i + first))


def whole_block(shape):
    return pl.BlockSpec(shape, lambda i: (0,) * len(shape))


def lane_pad(v):
    return jnp.pad(v, ((0, 0), (0, LANES - v.shape[1])))


class Mixer:
    def __init__(
        self, state_in, step_in, conv_state, conv_state_bias, step_bias, decay_log, segments
    ):
        rows = state_in.shape[0]
        self.rows = rows
        self.head_count = step_bias.shape[0]
        self.pairs = (self.head_count + 1) // 2
        self.width = self.pairs * LANES
        self.states = conv_state.shape[1] // 2
        self.blocks = rows // SPAN
        before = [
            jnp.concatenate([jnp.full((k,), -1, jnp.int32), segments[: rows - k]]) == segments
            for k in (1, 2, 3)
        ]
        ends = segments.reshape(self.blocks, SPAN)[:, SPAN - 1]
        previous = jnp.concatenate([jnp.full((1,), -1, jnp.int32), ends[:-1]])
        carried = jnp.repeat(previous, SPAN) == segments
        tail = jnp.repeat(ends, SPAN) == segments
        flags = jnp.stack(before + [carried, tail]).astype(wide)
        self.masks = jnp.broadcast_to(flags[:, :, None], (5, rows, LANES))
        self.shared = (
            state_in,
            lane_pad(step_in),
            conv_state,
            conv_state_bias[None],
            lane_pad(step_bias[None]),
            lane_pad(-jnp.exp(decay_log)[None]),
            self.masks,
            segments[:, None],
            segments[None],
        )
        (
            self.b, self.c, self.bt, self.ct, self.g, self.gt, self.dtx, self.cumx, cumt,
        ) = call(
            prep_kernel,
            [((rows, self.states), low)] * 2
            + [((self.states, rows), low)] * 2
            + [((rows, SPAN), wide)] * 2
            + [((rows, self.width), wide)] * 2
            + [((LANES, rows), wide)],
            self.shared,
            flops=12 * rows * LANES * self.width,
        )
        self.cumt = cumt[: 2 * self.pairs].reshape(self.pairs, 2, rows)

    def widen(self, v):
        return jnp.pad(v, ((0, 0), (0, self.width - v.shape[1])))

    def forward(self, value_in, conv_value, conv_value_bias, skip_scale):
        rows, states = self.rows, self.states
        self.inner = value_in.shape[1]
        self.value = (
            self.widen(value_in),
            self.widen(conv_value),
            self.widen(conv_value_bias[None]),
            self.widen(jnp.repeat(skip_scale, HALF)[None]),
        )
        (mixed,) = call(
            fwd_kernel,
            [((rows, self.width), wide)],
            self.value + (self.dtx, self.cumx, self.cumt, self.masks, self.c, self.bt, self.g),
            grid=(self.pairs,),
            in_specs=[
                column_block(rows),
                column_block(4),
                column_block(1),
                column_block(1),
                column_block(rows),
                column_block(rows),
                pl.BlockSpec((1, 2, rows), lambda i: (i, 0, 0)),
                whole_block((5, rows, LANES)),
                whole_block((rows, states)),
                whole_block((states, rows)),
                whole_block((rows, SPAN)),
            ],
            out_specs=[column_block(rows)],
            scratch=[pltpu.VMEM((rows, LANES), wide)],
            flops=20 * rows * LANES * self.width,
        )
        self.mixed = mixed
        return mixed[:, : self.inner]

    def backward_part(self, grad_mixed, first, last, earlier=()):
        rows, states = self.rows, self.states
        operands = (
            (self.value[0], self.mixed, self.widen(grad_mixed))
            + self.value[1:]
            + (self.dtx, self.cumx, self.cumt, self.masks, self.b, self.c, self.bt, self.ct)
            + (self.gt,)
        )
        totals = [whole_block((rows, LANES))] * 5
        resumed = bool(earlier)
        return call(
            functools.partial(bwd_kernel, first, resumed),
            [((rows, self.width), low), ((8, self.width), wide)]
            + [((rows, LANES), wide)] * 5,
            operands + tuple(earlier),
            grid=(last - first,),
            in_specs=[
                column_block(rows, first),
                column_block(rows, first),
                column_block(rows, first),
                column_block(4, first),
                column_block(1, first),
                column_block(1, first),
                column_block(rows, first),
                column_block(rows, first),
                pl.BlockSpec((1, 2, rows), lambda i: (i + first, 0, 0)),
                whole_block((5, rows, LANES)),
                whole_block((rows, states)),
                whole_block((rows, states)),
                whole_block((states, rows)),
                whole_block((states, rows)),
                whole_block((rows, SPAN)),
            ]
            + ([pl.BlockSpec(memory_space=pl.ANY)] * 2 + totals if resumed else []),
            out_specs=[column_block(rows, first), column_block(8, first)] + totals,
            scratch=[pltpu.VMEM((rows, LANES), wide)] * 3
            + [pltpu.VMEM((self.blocks, states, LANES), wide)],
            flops=60 * rows * LANES * (last - first) * LANES,
            aliases={len(operands): 0, len(operands) + 1: 1} if resumed else {},
        )

    def backward_end(self, db, dc, dg, z, dt):
        rows, states = self.rows, self.states
        return call(
            post_kernel,
            [
                ((rows, 2 * states), low),
                ((rows, LANES), low),
                ((8, 2 * states), wide),
                ((8, LANES), wide),
            ],
            self.shared + (self.b, self.c, db, dc, dg, z, dt),
            scratch=[pltpu.VMEM((2, rows, states), wide)],
            flops=12 * rows * LANES * self.width,
        )

    def backward(self, grad_mixed):
        half = (self.pairs + 1) // 2
        part = self.backward_part(grad_mixed, 0, half)
        value_grad, sums, *totals = self.backward_part(grad_mixed, half, self.pairs, part)
        return self.gradients(value_grad, sums, *self.backward_end(*totals))

    def gradients(self, value_grad, sums, state_grad, step_grad, state_sums, step_sums):
        heads = self.head_count
        skip_grad = sums[5, : self.inner].reshape(heads, HALF).sum(axis=1)
        return (
            value_grad[:, : self.inner],
            state_grad,
            step_grad[:, :heads],
            sums[:4, : self.inner],
            sums[4, : self.inner],
            state_sums[:4],
            state_sums[4],
            step_sums[0, :heads],
            step_sums[1, :heads],
            skip_grad,
        )


def ring_place(index, count):
    return jnp.where(index % 2 == 0, index // 2, count - 1 - index // 2)


def ring_index(place, count):
    place = place % count
    return jnp.where(place < (count + 1) // 2, 2 * place, 2 * (count - 1 - place) + 1)


def ring_moves(count):
    order = list(range(0, count, 2)) + list(range(1, count, 2))[::-1]
    ahead = [(order[k], order[(k + 1) % count]) for k in range(count)]
    return ahead, [(target, source) for source, target in ahead]


class RingGather:
    def __init__(self, shard):
        self.count = lax.axis_size("gx")
        self.moves = ring_moves(self.count)
        me = lax.axis_index("gx")
        self.place = ring_place(me, self.count)
        self.rows, width = shard.shape
        self.half = self.rows // 2
        self.taken = 0
        self.held = (shard[: self.half], shard[self.half :])
        full = jnp.zeros((self.count * self.rows, width), shard.dtype)
        self.full = lax.dynamic_update_slice(full, shard, (me * self.rows, 0))

    def step(self, times=1):
        for _ in range(min(times, self.count - 1 - self.taken)):
            self.taken += 1
            arrived = tuple(
                lax.ppermute(held, "gx", move) for held, move in zip(self.held, self.moves)
            )
            self.held, self.full = lax.optimization_barrier((arrived, self.full))
            for piece, sign, offset in zip(self.held, (-1, 1), (0, self.half)):
                owner = ring_index(self.place + sign * self.taken, self.count)
                start = owner * self.rows + offset
                self.full = lax.dynamic_update_slice(self.full, piece, (start, 0))
        return self.held

    def finish(self):
        self.step(self.count)
        return self.full


class RingSum:
    def __init__(self, partial):
        self.count = lax.axis_size("gx")
        self.moves = ring_moves(self.count)
        self.place = ring_place(lax.axis_index("gx"), self.count)
        self.rows = partial.shape[0] // self.count
        self.half = self.rows // 2
        self.partial = partial
        self.taken = 0
        self.held = (self.part(-1, 0), self.part(1, self.half))

    def part(self, target, offset):
        start = ring_index(self.place + target, self.count) * self.rows + offset
        return lax.dynamic_slice_in_dim(self.partial, start, self.half, 0)

    def step(self, times=1):
        for _ in range(min(times, self.count - 1 - self.taken)):
            self.taken += 1
            up, down = (
                lax.ppermute(held, "gx", move).astype(wide)
                for held, move in zip(self.held, self.moves)
            )
            up = up + self.part(-1 - self.taken, 0).astype(wide)
            down = down + self.part(1 + self.taken, self.half).astype(wide)
            if self.taken < self.count - 1:
                up, down = up.astype(low), down.astype(low)
            self.held = (up, down)
        return self.held

    def finish(self):
        return jnp.concatenate(self.step(self.count), 0)


def flips(count, bit):
    return [(k, k ^ bit) for k in range(count)]


def butterfly_sum(v, axis):
    count = lax.axis_size(axis)
    bit = 1
    while bit < count:
        v = v + lax.ppermute(v, axis, flips(count, bit))
        bit *= 2
    return v


def scatter_rows(partial):
    return lax.psum_scatter(partial, "gx", scatter_dimension=0, tiled=True)


def row_major(v):
    return with_layout_constraint(v, Layout((0, 1)))


def together(*values):
    return lax.optimization_barrier(values)


def tie(value, *rings):
    value, held = lax.optimization_barrier((value, [ring.held for ring in rings]))
    for ring, pieces in zip(rings, held):
        ring.held = tuple(pieces)
    return value


def on_device(
    layer_input,
    norm_gain,
    gate_weight,
    value_weight,
    state_weight,
    step_weight,
    conv_value,
    conv_value_bias,
    conv_state,
    conv_state_bias,
    step_bias,
    decay_log,
    skip_scale,
    gated_gain,
    out_weight,
    segment_ids,
    cotangent,
):
    model_width = layer_input.shape[1]
    col_width = cotangent.shape[1]
    state_cols = state_weight.shape[1]
    col_start = lax.axis_index("gy") * col_width

    state_step_weight = jnp.concatenate([state_weight, step_weight], 1)
    full_state = lax.all_gather(state_step_weight, "gx", axis=0, tiled=True)
    upstream = lax.all_gather(cotangent, "gy", axis=1, tiled=True)
    value_gather = RingGather(value_weight)
    value_gather.step()
    tokens = tie(layer_input, value_gather).astype(wide)
    scale_in = lax.rsqrt(jnp.mean(tokens * tokens, axis=1, keepdims=True) + epsilon)
    normed = (tokens * scale_in * norm_gain).astype(low)
    value_gather.step()
    normed = tie(normed, value_gather)
    value_gather.step(value_gather.count)
    gate_shard = tie(gate_weight, value_gather)
    full_gate = lax.all_gather(gate_shard, "gx", axis=0, tiled=True)
    full_value = value_gather.finish()

    out_gather = RingGather(tie(out_weight.T, value_gather))
    out_gather.step()
    normed = tie(normed, out_gather)
    state_step = dot(normed, full_state)
    mixer = Mixer(
        state_step[:, :state_cols],
        state_step[:, state_cols:],
        conv_state,
        conv_state_bias,
        step_bias,
        decay_log,
        segment_ids,
    )
    out_gather.step()
    normed, mixer.g = together(normed, mixer.g)
    normed = tie(normed, out_gather)
    value_in = dot(normed, full_value)
    out_gather.step()
    value_in = tie(value_in, out_gather)
    mixed = mixer.forward(value_in, conv_value, conv_value_bias, skip_scale)
    out_gather.step()
    mixed = mixer.mixed = tie(mixer.mixed, out_gather)
    mixed = mixed[:, : mixer.inner]
    full_out = out_gather.finish()
    full_value_state = jnp.concatenate([full_value, full_state], 1)
    gate_in = dot(normed, full_gate)
    gate_open = jax.nn.sigmoid(gate_in)
    gate_act = gate_in * gate_open
    gated = mixed * gate_act
    up_back = dot(upstream, full_out)

    sums_out = lax.psum(
        jnp.stack(
            [jnp.sum(gated * gated, axis=1), jnp.sum(gated * gated_gain * up_back, axis=1)]
        ),
        "gy",
    )
    scale_out = lax.rsqrt(sums_out[0] / INNER + epsilon)[:, None]
    grad_scale = sums_out[1][:, None]
    scaled = (gated * gated_gain).astype(low)

    scaled_out = (gated * gated_gain * scale_out).astype(low)
    out_ring = RingSum(row_major(contract_rows(upstream, scaled_out).astype(low)))

    scaled = tie(scaled, out_ring)
    product_part = contract_cols(full_out, scaled)
    product_part = row_major((product_part * scale_out[:, 0]).astype(low))
    product = lax.psum_scatter(product_part, "gy", scatter_dimension=0, tiled=True)

    out_ring.step()
    up_back, product_part = together(up_back, product_part)
    grad_scaled = scale_out * tie(up_back, out_ring)
    grad_gated = grad_scaled * gated_gain - grad_scale * scale_out**3 * gated / INNER
    gate_gain_part = jnp.sum(grad_scaled * gated, axis=0)
    grad_gate_in = (
        grad_gated * mixed * gate_open * (1.0 + gate_in * (1.0 - gate_open))
    ).astype(low)
    grad_mixed = grad_gated * gate_act
    out_ring.step()
    normed = tie(normed, out_ring)
    gate_ring = RingSum(row_major(contract_rows(normed, grad_gate_in).astype(low)))

    half = (mixer.pairs + 1) // 2
    out_ring.step()
    grad_mixed = tie(grad_mixed, out_ring, gate_ring)
    part = mixer.backward_part(grad_mixed, 0, half)
    out_ring.step()
    gate_ring.step()
    grad_mixed = tie(grad_mixed, out_ring, gate_ring)
    value_grad, value_sums, *totals = mixer.backward_part(grad_mixed, half, mixer.pairs, part)
    grad_value_in = value_grad[:, : gate_weight.shape[1]]
    out_ring.step()
    gate_ring.step()
    normed = tie(normed, out_ring, gate_ring)
    value_ring = RingSum(row_major(contract_rows(normed, grad_value_in).astype(low)))
    out_ring.step()
    gate_ring.step()
    totals[0] = tie(totals[0], out_ring, gate_ring, value_ring)
    ends = mixer.backward_end(*totals)
    pulled = mixer.gradients(value_grad, value_sums, *ends)
    grad_state_in = jnp.concatenate([pulled[1], pulled[2]], 1)
    state_partial = row_major(contract_rows(normed, grad_state_in).astype(low))
    grad_state_step = scatter_rows(state_partial).astype(wide)

    value_ring.step()
    grad_gate_in = tie(grad_gate_in, value_ring)
    grad_normed_part = contract_cols(full_gate, grad_gate_in)
    grad_value_state_in = jnp.concatenate([grad_value_in, grad_state_in], 1)
    out_ring.step()
    gate_ring.step()
    grad_value_state_in = tie(grad_value_state_in, out_ring, gate_ring)
    grad_value_state_in, product = together(grad_value_state_in, product)
    grad_normed_part = grad_normed_part + contract_cols(full_value_state, grad_value_state_in)
    grad_normed_part = row_major(grad_normed_part.astype(low))
    grad_out = out_ring.finish()
    grad_gate = gate_ring.finish()
    grad_value = value_ring.finish()

    grad_normed = lax.psum_scatter(
        grad_normed_part, "gy", scatter_dimension=0, tiled=True
    ).T.astype(wide)
    token_cols = lax.dynamic_slice_in_dim(layer_input, col_start, col_width, 1).astype(wide)
    gain_cols = lax.dynamic_slice_in_dim(norm_gain, col_start, col_width, 0)
    weighted = grad_normed * gain_cols
    inner_dot = lax.psum(jnp.sum(weighted * token_cols, axis=1), "gy")[:, None]
    grad_input = (
        cotangent.astype(wide)
        + scale_in * weighted
        - token_cols * scale_in**3 * inner_dot / model_width
    )
    grad_norm_gain = butterfly_sum(jnp.sum(grad_normed * token_cols * scale_in, axis=0), "gx")
    layer_output = (token_cols + product.T.astype(wide)).astype(low)

    small = (gate_gain_part,) + pulled[3:]
    packed = jnp.concatenate([v.reshape(-1) for v in small])
    packed = butterfly_sum(packed, "gx")
    sums, start = [], 0
    for v in small:
        sums.append(packed[start : start + v.size].reshape(v.shape))
        start += v.size
    state_sums = butterfly_sum(
        jnp.concatenate([grad_state_step[:, :state_cols], sums[3], sums[4][None]], 0), "gy"
    )
    state_rows = state_weight.shape[0]
    return (
        layer_output,
        grad_input,
        grad_norm_gain,
        grad_gate,
        grad_value,
        state_sums[:state_rows],
        grad_state_step[:, state_cols:],
        sums[1],
        sums[2],
        state_sums[state_rows:-1],
        state_sums[-1],
        sums[5],
        sums[6],
        sums[7],
        sums[0],
        grad_out.T,
    )


def solution(mesh):
    return jax.shard_map(
        on_device,
        mesh=mesh,
        in_specs=(
            P("gx", None),
            P(),
            P("gx", "gy"),
            P("gx", "gy"),
            P("gx", None),
            P("gx", "gy"),
            P(None, "gy"),
            P("gy"),
            P(),
            P(),
            P("gy"),
            P("gy"),
            P("gy"),
            P("gy"),
            P("gy", "gx"),
            P("gx"),
            P("gx", "gy"),
        ),
        out_specs=(
            P("gx", "gy"),
            P("gx", "gy"),
            P("gy"),
            P("gx", "gy"),
            P("gx", "gy"),
            P("gx", None),
            P("gx", "gy"),
            P(None, "gy"),
            P("gy"),
            P(),
            P(),
            P("gy"),
            P("gy"),
            P("gy"),
            P("gy"),
            P("gy", "gx"),
        ),
        check_vma=False,
    )
```

```python
import functools

import jax
import jax.numpy as jnp
from jax import lax
from jax.experimental import pallas as pl
from jax.experimental.layout import Layout, with_layout_constraint
from jax.experimental.pallas import tpu as pltpu
from jax.sharding import PartitionSpec as P

INNER = 5120
SPAN = 128
LANES = 128
HALF = 64
LOG2E = 1.4426950408889634
VMEM_BYTES = 56 * 1024 * 1024

epsilon = 1e-05
highest = lax.Precision.HIGHEST
low = jnp.bfloat16
wide = jnp.float32


def dot(left, right, precision=None):
    return jnp.dot(left, right, preferred_element_type=wide, precision=precision)


def contract_rows(left, right, precision=None):
    return lax.dot_general(
        left, right, (((0,), (0,)), ((), ())), preferred_element_type=wide, precision=precision
    )


def contract_cols(left, right, precision=None):
    return lax.dot_general(
        left, right, (((1,), (1,)), ((), ())), preferred_element_type=wide, precision=precision
    )


def sigmoid(v):
    return 1.0 / (1.0 + jnp.exp(-v))


def softplus(v):
    return jnp.maximum(v, 0.0) + jnp.log1p(jnp.exp(-jnp.abs(v)))


def conv_in(v, taps, bias, masks):
    total = bias + taps[0:1] * v
    for k in range(1, 4):
        total = total + taps[k : k + 1] * (pltpu.roll(v, k, 0) * masks[k - 1])
    return total


def conv_back(grad, v, taps, masks):
    rows = grad.shape[0]
    back = taps[0:1] * grad
    sums = [jnp.sum(grad * v, axis=0, keepdims=True)]
    for k in range(1, 4):
        kept = grad * masks[k - 1]
        sums.append(jnp.sum(kept * pltpu.roll(v, k, 0), axis=0, keepdims=True))
        back = back + taps[k : k + 1] * pltpu.roll(kept, rows - k, 0)
    sums.append(jnp.sum(grad, axis=0, keepdims=True))
    return back, sums


def visible_block(seg_col, seg_row, row_is_query):
    shape = (SPAN, SPAN)
    first = lax.broadcasted_iota(jnp.int32, shape, 0)
    second = lax.broadcasted_iota(jnp.int32, shape, 1)
    ordered = (first >= second) if row_is_query else (first <= second)
    return ordered & (seg_col == seg_row)


def lower_triangle():
    shape = (SPAN, SPAN)
    return (
        lax.broadcasted_iota(jnp.int32, shape, 0) >= lax.broadcasted_iota(jnp.int32, shape, 1)
    ).astype(wide)


def prep_kernel(
    state_ref, step_ref, taps_ref, bias_ref, step_bias_ref, rate_ref, masks_ref, seg_col_ref,
    seg_row_ref, b_ref, c_ref, bt_ref, ct_ref, g_ref, gt_ref, dtx_ref, cumx_ref, cumt_ref,
):
    rows, states = b_ref.shape
    masks = [masks_ref[k] for k in range(3)]
    for part, (out, out_t) in enumerate(((b_ref, bt_ref), (c_ref, ct_ref))):
        cols = slice(part * states, (part + 1) * states)
        pre = conv_in(state_ref[:, cols], taps_ref[:, cols], bias_ref[:, cols], masks)
        act = pre * sigmoid(pre)
        out[...] = act.astype(low)
        out_t[...] = act.T.astype(low)
    step = softplus(step_ref[...] + step_bias_ref[...])
    triangle = lower_triangle()
    heads = lax.broadcasted_iota(jnp.int32, (LANES, dtx_ref.shape[1]), 0)
    channels = lax.broadcasted_iota(jnp.int32, (LANES, dtx_ref.shape[1]), 1)
    expand = (channels // HALF == heads).astype(wide)
    rate = step * (rate_ref[...] * LOG2E)
    for c in range(rows // SPAN):
        at = slice(c * SPAN, (c + 1) * SPAN)
        grams = dot(c_ref[at], bt_ref[:, at])
        g_ref[at] = jnp.where(visible_block(seg_col_ref[at], seg_row_ref[:, at], True), grams, 0.0)
        grams_t = dot(b_ref[at], ct_ref[:, at])
        gt_ref[at] = jnp.where(
            visible_block(seg_col_ref[at], seg_row_ref[:, at], False), grams_t, 0.0
        )
        total = dot(triangle, rate[at], highest)
        cumx_ref[at] = dot(total, expand, highest)
        dtx_ref[at] = dot(step[at], expand, highest)
        cumt_ref[:, at] = total.T


def decays(cumx_ref, cumt_ref, at, head, row_is_query):
    lane = head * HALF
    column = cumx_ref[at, lane : lane + 1]
    row = cumt_ref[0, head : head + 1, at]
    gap = (column - row) if row_is_query else (row - column)
    return jnp.exp2(jnp.minimum(gap, 0.0))


def split_heads(block):
    left = lax.broadcasted_iota(jnp.int32, block.shape, 1) < HALF
    zero = jnp.zeros_like(block)
    return jnp.concatenate([jnp.where(left, block, zero), jnp.where(left, zero, block)], 0)


def fwd_kernel(
    value_ref, taps_ref, bias_ref, skip_ref, dtx_ref, cumx_ref, cumt_ref, masks_ref, c_ref, bt_ref,
    g_ref, out_ref, x_scr,
):
    rows = value_ref.shape[0]
    masks = [masks_ref[k] for k in range(3)]
    pre = conv_in(value_ref[...], taps_ref[...], bias_ref[...], masks)
    x_scr[...] = pre * sigmoid(pre)
    state = jnp.zeros((c_ref.shape[1], LANES), wide)
    for c in range(rows // SPAN):
        at = slice(c * SPAN, (c + 1) * SPAN)
        x = x_scr[at]
        cum = cumx_ref[at]
        stepped = x * dtx_ref[at]
        mixing = jnp.concatenate(
            [decays(cumx_ref, cumt_ref, at, head, True) * g_ref[at] for head in (0, 1)], 1
        ).astype(low)
        y = dot(mixing, split_heads(stepped.astype(low)))
        if c > 0:
            y = y + dot(c_ref[at], state.astype(low)) * (jnp.exp2(cum) * masks_ref[3, at])
        out_ref[at] = y + skip_ref[...] * x
        if c + 1 < rows // SPAN:
            end = slice((c + 1) * SPAN - 1, (c + 1) * SPAN)
            last = cum[SPAN - 1 : SPAN]
            tail = jnp.exp2(last - cum) * masks_ref[4, at]
            fresh = dot(bt_ref[:, at], (stepped.astype(low) * tail).astype(low))
            state = (masks_ref[3, end] * jnp.exp2(last)) * state + fresh


def bwd_kernel(
    first, resumed, value_ref, mixed_ref, grad_ref, taps_ref, bias_ref, skip_ref, dtx_ref, cumx_ref, cumt_ref,
    masks_ref, b_ref, c_ref, bt_ref, ct_ref, gt_ref, *more,
):
    earlier, more = more[: 7 * resumed], more[7 * resumed :]
    value_out, sums_out, *totals, pre_scr, x_scr, dpre_scr, state_scr = more
    db_ref, dc_ref, dg_ref, z_ref, dt_ref = totals
    rows = value_ref.shape[0]
    blocks = rows // SPAN
    pair = pl.program_id(0) + first
    masks = [masks_ref[k] for k in range(3)]

    @pl.when(pl.program_id(0) == 0)
    def _():
        for place, ref in enumerate(totals):
            ref[...] = earlier[2 + place][...] if resumed else jnp.zeros_like(ref)

    pre = conv_in(value_ref[...], taps_ref[...], bias_ref[...], masks)
    pre_scr[...] = pre
    x_scr[...] = pre * sigmoid(pre)
    state = jnp.zeros((c_ref.shape[1], LANES), wide)
    for c in range(blocks):
        at = slice(c * SPAN, (c + 1) * SPAN)
        state_scr[c] = state
        if c + 1 < blocks:
            end = slice((c + 1) * SPAN - 1, (c + 1) * SPAN)
            cum = cumx_ref[at]
            last = cum[SPAN - 1 : SPAN]
            tail = jnp.exp2(last - cum) * masks_ref[4, at]
            stepped = (x_scr[at] * dtx_ref[at]).astype(low)
            fresh = dot(bt_ref[:, at], (stepped * tail).astype(low))
            state = (masks_ref[3, end] * jnp.exp2(last)) * state + fresh

    lanes = lax.broadcasted_iota(jnp.int32, (LANES, LANES), 0)
    heads = lax.broadcasted_iota(jnp.int32, (LANES, LANES), 1)
    gather = (lanes // HALF + 2 * pair == heads).astype(low)
    row_number = lax.broadcasted_iota(jnp.int32, (SPAN, LANES), 0)
    grad_skip = jnp.zeros((1, LANES), wide)
    grad_state = jnp.zeros((c_ref.shape[1], LANES), wide)
    for c in reversed(range(blocks)):
        at = slice(c * SPAN, (c + 1) * SPAN)
        end = slice((c + 1) * SPAN - 1, (c + 1) * SPAN)
        x = x_scr[at]
        dtx = dtx_ref[at]
        cum = cumx_ref[at]
        grad = grad_ref[at]
        grad_low = grad.astype(low)
        stepped = (x * dtx).astype(low)
        y = mixed_ref[at] - skip_ref[...] * x
        grad_mix = contract_cols(split_heads(stepped), grad_low)
        mixing = []
        grams = dg_ref[at]
        for head in (0, 1):
            decay = decays(cumx_ref, cumt_ref, at, head, False)
            mixing.append((decay * gt_ref[at]).astype(low))
            grams = grams + decay * grad_mix[head * SPAN : (head + 1) * SPAN]
        dg_ref[at] = grams
        grad_stepped = dot(jnp.concatenate(mixing, 1), split_heads(grad_low))
        last = cum[SPAN - 1 : SPAN]
        at_end = jnp.zeros((1, LANES), wide)
        carry = masks_ref[3, end] * jnp.exp2(last)
        if c + 1 < blocks:
            tail = jnp.exp2(last - cum) * masks_ref[4, at]
            grad_state_low = grad_state.astype(low)
            from_tail = dot(b_ref[at], grad_state_low) * tail
            grad_stepped = grad_stepped + from_tail
            db_ref[at] += contract_cols((stepped * tail).astype(low), grad_state_low)
            at_end = jnp.sum(stepped.astype(wide) * from_tail, axis=0, keepdims=True)
            at_end = at_end + carry * jnp.sum(state_scr[c] * grad_state, axis=0, keepdims=True)
        if c > 0:
            reach = (grad * (jnp.exp2(cum) * masks_ref[3, at])).astype(low)
            dc_ref[at] += contract_cols(reach, state_scr[c].astype(low))
            grad_state = carry * grad_state + dot(ct_ref[:, at], reach)
        z = grad_low.astype(wide) * y - stepped.astype(wide) * grad_stepped
        z = z + jnp.where(row_number == SPAN - 1, at_end, 0.0)
        z_high = z.astype(low)
        z_low = (z - z_high.astype(wide)).astype(low)
        z_ref[at] += dot(z_high, gather) + dot(z_low, gather)
        dt_ref[at] += dot((x * grad_stepped).astype(low), gather)
        grad_skip = grad_skip + jnp.sum(grad * x, axis=0, keepdims=True)
        pre_c = pre_scr[at]
        opened = sigmoid(pre_c)
        grad_x = grad_stepped * dtx + skip_ref[...] * grad
        dpre_scr[at] = grad_x * opened * (1.0 + pre_c * (1.0 - opened))

    back, sums = conv_back(dpre_scr[...], value_ref[...], taps_ref[...], masks)
    value_out[...] = back.astype(low)
    sums_out[...] = jnp.concatenate(sums + [grad_skip, jnp.zeros((2, LANES), wide)], 0)


def post_kernel(
    state_ref, step_ref, taps_ref, bias_ref, step_bias_ref, rate_ref, masks_ref, seg_col_ref,
    seg_row_ref, b_ref, c_ref, db_ref, dc_ref, dg_ref, z_ref, dt_ref,
    state_out, step_out, state_sums, step_sums, act_scr,
):
    rows, states = b_ref.shape
    masks = [masks_ref[k] for k in range(3)]
    triangle = lower_triangle()
    for c in range(rows // SPAN):
        at = slice(c * SPAN, (c + 1) * SPAN)
        seen = visible_block(seg_col_ref[at], seg_row_ref[:, at], False)
        grams = jnp.where(seen, dg_ref[at], 0.0)
        act_scr[0, at] = db_ref[at] + dot(grams.astype(low), c_ref[at])
        act_scr[1, at] = dc_ref[at] + dot(grams.T.astype(low), b_ref[at])
    for part in (0, 1):
        cols = slice(part * states, (part + 1) * states)
        v = state_ref[:, cols]
        pre = conv_in(v, taps_ref[:, cols], bias_ref[:, cols], masks)
        opened = sigmoid(pre)
        grad = act_scr[part] * opened * (1.0 + pre * (1.0 - opened))
        back, sums = conv_back(grad, v, taps_ref[:, cols], masks)
        state_out[:, cols] = back.astype(low)
        state_sums[:, cols] = jnp.concatenate(sums + [jnp.zeros((3, states), wide)], 0)
    pre = step_ref[...] + step_bias_ref[...]
    step = softplus(pre)
    rate_sum = jnp.zeros((1, LANES), wide)
    bias_sum = jnp.zeros((1, LANES), wide)
    for c in range(rows // SPAN):
        at = slice(c * SPAN, (c + 1) * SPAN)
        grad_rate = contract_rows(triangle, z_ref[at], highest)
        grad_step = (dt_ref[at] + rate_ref[...] * grad_rate) * sigmoid(pre[at])
        step_out[at] = grad_step.astype(low)
        rate_sum = rate_sum + jnp.sum(
            grad_rate * (rate_ref[...] * step[at]), axis=0, keepdims=True
        )
        bias_sum = bias_sum + jnp.sum(grad_step, axis=0, keepdims=True)
    step_sums[...] = jnp.concatenate([bias_sum, rate_sum, jnp.zeros((6, LANES), wide)], 0)


def call(
    kernel, outs, operands, grid=None, in_specs=None, out_specs=None, scratch=(), flops=0, aliases={}
):
    shapes = tuple(jax.ShapeDtypeStruct(shape, kind) for shape, kind in outs)
    moved = sum(a.size * a.dtype.itemsize for a in operands)
    moved += sum(s.size * s.dtype.itemsize for s in shapes)
    extra = {} if grid is None else dict(grid=grid, in_specs=in_specs, out_specs=out_specs)
    return pl.pallas_call(
        kernel,
        out_shape=shapes,
        scratch_shapes=list(scratch),
        compiler_params=pltpu.CompilerParams(vmem_limit_bytes=VMEM_BYTES),
        input_output_aliases=dict(aliases),
        cost_estimate=pl.CostEstimate(flops=flops, bytes_accessed=moved, transcendentals=0),
        **extra,
    )(*operands)


def column_block(rows, first=0):
    return pl.BlockSpec((rows, LANES), lambda i: (0, i + first))


def whole_block(shape):
    return pl.BlockSpec(shape, lambda i: (0,) * len(shape))


def lane_pad(v):
    return jnp.pad(v, ((0, 0), (0, LANES - v.shape[1])))


class Mixer:
    def __init__(
        self, state_in, step_in, conv_state, conv_state_bias, step_bias, decay_log, segments
    ):
        rows = state_in.shape[0]
        self.rows = rows
        self.head_count = step_bias.shape[0]
        self.pairs = (self.head_count + 1) // 2
        self.width = self.pairs * LANES
        self.states = conv_state.shape[1] // 2
        self.blocks = rows // SPAN
        before = [
            jnp.concatenate([jnp.full((k,), -1, jnp.int32), segments[: rows - k]]) == segments
            for k in (1, 2, 3)
        ]
        ends = segments.reshape(self.blocks, SPAN)[:, SPAN - 1]
        previous = jnp.concatenate([jnp.full((1,), -1, jnp.int32), ends[:-1]])
        carried = jnp.repeat(previous, SPAN) == segments
        tail = jnp.repeat(ends, SPAN) == segments
        flags = jnp.stack(before + [carried, tail]).astype(wide)
        self.masks = jnp.broadcast_to(flags[:, :, None], (5, rows, LANES))
        self.shared = (
            state_in,
            lane_pad(step_in),
            conv_state,
            conv_state_bias[None],
            lane_pad(step_bias[None]),
            lane_pad(-jnp.exp(decay_log)[None]),
            self.masks,
            segments[:, None],
            segments[None],
        )
        (
            self.b, self.c, self.bt, self.ct, self.g, self.gt, self.dtx, self.cumx, cumt,
        ) = call(
            prep_kernel,
            [((rows, self.states), low)] * 2
            + [((self.states, rows), low)] * 2
            + [((rows, SPAN), wide)] * 2
            + [((rows, self.width), wide)] * 2
            + [((LANES, rows), wide)],
            self.shared,
            flops=12 * rows * LANES * self.width,
        )
        self.cumt = cumt[: 2 * self.pairs].reshape(self.pairs, 2, rows)

    def widen(self, v):
        return jnp.pad(v, ((0, 0), (0, self.width - v.shape[1])))

    def forward(self, value_in, conv_value, conv_value_bias, skip_scale):
        rows, states = self.rows, self.states
        self.inner = value_in.shape[1]
        self.value = (
            self.widen(value_in),
            self.widen(conv_value),
            self.widen(conv_value_bias[None]),
            self.widen(jnp.repeat(skip_scale, HALF)[None]),
        )
        (mixed,) = call(
            fwd_kernel,
            [((rows, self.width), wide)],
            self.value + (self.dtx, self.cumx, self.cumt, self.masks, self.c, self.bt, self.g),
            grid=(self.pairs,),
            in_specs=[
                column_block(rows),
                column_block(4),
                column_block(1),
                column_block(1),
                column_block(rows),
                column_block(rows),
                pl.BlockSpec((1, 2, rows), lambda i: (i, 0, 0)),
                whole_block((5, rows, LANES)),
                whole_block((rows, states)),
                whole_block((states, rows)),
                whole_block((rows, SPAN)),
            ],
            out_specs=[column_block(rows)],
            scratch=[pltpu.VMEM((rows, LANES), wide)],
            flops=20 * rows * LANES * self.width,
        )
        self.mixed = mixed
        return mixed[:, : self.inner]

    def backward_part(self, grad_mixed, first, last, earlier=()):
        rows, states = self.rows, self.states
        operands = (
            (self.value[0], self.mixed, self.widen(grad_mixed))
            + self.value[1:]
            + (self.dtx, self.cumx, self.cumt, self.masks, self.b, self.c, self.bt, self.ct)
            + (self.gt,)
        )
        totals = [whole_block((rows, LANES))] * 5
        resumed = bool(earlier)
        return call(
            functools.partial(bwd_kernel, first, resumed),
            [((rows, self.width), low), ((8, self.width), wide)]
            + [((rows, LANES), wide)] * 5,
            operands + tuple(earlier),
            grid=(last - first,),
            in_specs=[
                column_block(rows, first),
                column_block(rows, first),
                column_block(rows, first),
                column_block(4, first),
                column_block(1, first),
                column_block(1, first),
                column_block(rows, first),
                column_block(rows, first),
                pl.BlockSpec((1, 2, rows), lambda i: (i + first, 0, 0)),
                whole_block((5, rows, LANES)),
                whole_block((rows, states)),
                whole_block((rows, states)),
                whole_block((states, rows)),
                whole_block((states, rows)),
                whole_block((rows, SPAN)),
            ]
            + ([pl.BlockSpec(memory_space=pl.ANY)] * 2 + totals if resumed else []),
            out_specs=[column_block(rows, first), column_block(8, first)] + totals,
            scratch=[pltpu.VMEM((rows, LANES), wide)] * 3
            + [pltpu.VMEM((self.blocks, states, LANES), wide)],
            flops=60 * rows * LANES * (last - first) * LANES,
            aliases={len(operands): 0, len(operands) + 1: 1} if resumed else {},
        )

    def backward_end(self, db, dc, dg, z, dt):
        rows, states = self.rows, self.states
        return call(
            post_kernel,
            [
                ((rows, 2 * states), low),
                ((rows, LANES), low),
                ((8, 2 * states), wide),
                ((8, LANES), wide),
            ],
            self.shared + (self.b, self.c, db, dc, dg, z, dt),
            scratch=[pltpu.VMEM((2, rows, states), wide)],
            flops=12 * rows * LANES * self.width,
        )

    def backward(self, grad_mixed):
        half = (self.pairs + 1) // 2
        part = self.backward_part(grad_mixed, 0, half)
        value_grad, sums, *totals = self.backward_part(grad_mixed, half, self.pairs, part)
        return self.gradients(value_grad, sums, *self.backward_end(*totals))

    def gradients(self, value_grad, sums, state_grad, step_grad, state_sums, step_sums):
        heads = self.head_count
        skip_grad = sums[5, : self.inner].reshape(heads, HALF).sum(axis=1)
        return (
            value_grad[:, : self.inner],
            state_grad,
            step_grad[:, :heads],
            sums[:4, : self.inner],
            sums[4, : self.inner],
            state_sums[:4],
            state_sums[4],
            step_sums[0, :heads],
            step_sums[1, :heads],
            skip_grad,
        )


def ring_place(index, count):
    return jnp.where(index % 2 == 0, index // 2, count - 1 - index // 2)


def ring_index(place, count):
    place = place % count
    return jnp.where(place < (count + 1) // 2, 2 * place, 2 * (count - 1 - place) + 1)


def ring_moves(count):
    order = list(range(0, count, 2)) + list(range(1, count, 2))[::-1]
    ahead = [(order[k], order[(k + 1) % count]) for k in range(count)]
    return ahead, [(target, source) for source, target in ahead]


class RingGather:
    def __init__(self, shard):
        self.count = lax.axis_size("gx")
        self.moves = ring_moves(self.count)
        me = lax.axis_index("gx")
        self.place = ring_place(me, self.count)
        self.rows, width = shard.shape
        self.half = self.rows // 2
        self.taken = 0
        self.held = (shard[: self.half], shard[self.half :])
        full = jnp.zeros((self.count * self.rows, width), shard.dtype)
        self.full = lax.dynamic_update_slice(full, shard, (me * self.rows, 0))

    def step(self, times=1):
        for _ in range(min(times, self.count - 1 - self.taken)):
            self.taken += 1
            arrived = tuple(
                lax.ppermute(held, "gx", move) for held, move in zip(self.held, self.moves)
            )
            self.held, self.full = lax.optimization_barrier((arrived, self.full))
            for piece, sign, offset in zip(self.held, (-1, 1), (0, self.half)):
                owner = ring_index(self.place + sign * self.taken, self.count)
                start = owner * self.rows + offset
                self.full = lax.dynamic_update_slice(self.full, piece, (start, 0))
        return self.held

    def finish(self):
        self.step(self.count)
        return self.full


class RingSum:
    def __init__(self, partial):
        self.count = lax.axis_size("gx")
        self.moves = ring_moves(self.count)
        self.place = ring_place(lax.axis_index("gx"), self.count)
        self.rows = partial.shape[0] // self.count
        self.half = self.rows // 2
        self.partial = partial
        self.taken = 0
        self.held = (self.part(-1, 0), self.part(1, self.half))

    def part(self, target, offset):
        start = ring_index(self.place + target, self.count) * self.rows + offset
        return lax.dynamic_slice_in_dim(self.partial, start, self.half, 0)

    def step(self, times=1):
        for _ in range(min(times, self.count - 1 - self.taken)):
            self.taken += 1
            up, down = (
                lax.ppermute(held, "gx", move).astype(wide)
                for held, move in zip(self.held, self.moves)
            )
            up = up + self.part(-1 - self.taken, 0).astype(wide)
            down = down + self.part(1 + self.taken, self.half).astype(wide)
            if self.taken < self.count - 1:
                up, down = up.astype(low), down.astype(low)
            self.held = (up, down)
        return self.held

    def finish(self):
        return jnp.concatenate(self.step(self.count), 0)


def flips(count, bit):
    return [(k, k ^ bit) for k in range(count)]


def halving_sum(partial, axis):
    count = lax.axis_size(axis)
    me = lax.axis_index(axis)
    held = partial.reshape(count, partial.shape[0] // count, partial.shape[1])
    bit = 1
    while bit < count:
        pairs = held.reshape(held.shape[0] // 2, 2, *held.shape[1:])
        mine = (me // bit) % 2
        kept = row_major(lax.dynamic_index_in_dim(pairs, mine, 1, keepdims=False))
        given = row_major(lax.dynamic_index_in_dim(pairs, 1 - mine, 1, keepdims=False))
        got = row_major(lax.ppermute(given, axis, flips(count, bit)))
        held = row_major((kept.astype(wide) + got.astype(wide)).astype(partial.dtype))
        bit *= 2
    return held[0]


def butterfly_sum(v, axis):
    count = lax.axis_size(axis)
    bit = 1
    while bit < count:
        v = v + lax.ppermute(v, axis, flips(count, bit))
        bit *= 2
    return v


def scatter_rows(partial):
    return lax.psum_scatter(partial, "gx", scatter_dimension=0, tiled=True)


def row_major(v):
    return with_layout_constraint(v, Layout(tuple(range(v.ndim))))


def together(*values):
    return lax.optimization_barrier(values)


def tie(value, *rings):
    value, held = lax.optimization_barrier((value, [ring.held for ring in rings]))
    for ring, pieces in zip(rings, held):
        ring.held = tuple(pieces)
    return value


def on_device(
    layer_input,
    norm_gain,
    gate_weight,
    value_weight,
    state_weight,
    step_weight,
    conv_value,
    conv_value_bias,
    conv_state,
    conv_state_bias,
    step_bias,
    decay_log,
    skip_scale,
    gated_gain,
    out_weight,
    segment_ids,
    cotangent,
):
    model_width = layer_input.shape[1]
    col_width = cotangent.shape[1]
    state_cols = state_weight.shape[1]
    col_start = lax.axis_index("gy") * col_width

    inner = gate_weight.shape[1]
    upstream = lax.all_gather(cotangent, "gy", axis=1, tiled=True)
    value_gather = RingGather(jnp.concatenate([value_weight, state_weight, step_weight], 1))
    value_gather.step()
    tokens = tie(layer_input, value_gather).astype(wide)
    scale_in = lax.rsqrt(jnp.mean(tokens * tokens, axis=1, keepdims=True) + epsilon)
    normed = (tokens * scale_in * norm_gain).astype(low)
    value_gather.step()
    normed = tie(normed, value_gather)
    value_gather.step(value_gather.count)
    gate_shard = tie(gate_weight, value_gather)
    gate_shard, upstream = together(gate_shard, upstream)
    full_gate = lax.all_gather(gate_shard, "gx", axis=0, tiled=True)
    full_value_state = value_gather.finish()

    out_gather = RingGather(tie(out_weight.T, value_gather))
    out_gather.step()
    normed = tie(normed, out_gather)
    state_step = dot(normed, full_value_state[:, inner:])
    mixer = Mixer(
        state_step[:, :state_cols],
        state_step[:, state_cols:],
        conv_state,
        conv_state_bias,
        step_bias,
        decay_log,
        segment_ids,
    )
    out_gather.step()
    normed, mixer.g = together(normed, mixer.g)
    normed = tie(normed, out_gather)
    value_in = dot(normed, full_value_state[:, :inner])
    out_gather.step()
    value_in = tie(value_in, out_gather)
    mixed = mixer.forward(value_in, conv_value, conv_value_bias, skip_scale)
    out_gather.step()
    mixed = mixer.mixed = tie(mixer.mixed, out_gather)
    mixed = mixed[:, : mixer.inner]
    full_out = out_gather.finish()
    gate_in = dot(normed, full_gate)
    gate_open = jax.nn.sigmoid(gate_in)
    gate_act = gate_in * gate_open
    gated = mixed * gate_act
    up_back = dot(upstream, full_out)

    sums_out = lax.psum(
        jnp.stack(
            [jnp.sum(gated * gated, axis=1), jnp.sum(gated * gated_gain * up_back, axis=1)]
        ),
        "gy",
    )
    scale_out = lax.rsqrt(sums_out[0] / INNER + epsilon)[:, None]
    grad_scale = sums_out[1][:, None]
    scaled = (gated * gated_gain).astype(low)

    scaled_out = (gated * gated_gain * scale_out).astype(low)
    out_partial = row_major(contract_rows(upstream, scaled_out).astype(low))
    up_back, out_partial = together(up_back, out_partial)
    grad_out = scatter_rows(out_partial)

    grad_scaled = scale_out * up_back
    grad_gated = grad_scaled * gated_gain - grad_scale * scale_out**3 * gated / INNER
    gate_gain_part = jnp.sum(grad_scaled * gated, axis=0)
    grad_gate_in = (
        grad_gated * mixed * gate_open * (1.0 + gate_in * (1.0 - gate_open))
    ).astype(low)
    grad_mixed = grad_gated * gate_act
    gate_ring = RingSum(row_major(contract_rows(normed, grad_gate_in).astype(low)))

    gate_ring.step()
    scaled = tie(scaled, gate_ring)
    product_part = contract_cols(full_out, scaled)
    product_part = row_major((product_part * scale_out[:, 0]).astype(low))
    grad_mixed, product_part = together(grad_mixed, product_part)
    product = halving_sum(product_part, "gy")

    half = (mixer.pairs + 1) // 2
    gate_ring.step()
    grad_mixed = tie(grad_mixed, gate_ring)
    part = mixer.backward_part(grad_mixed, 0, half)
    gate_ring.step()
    grad_mixed = tie(grad_mixed, gate_ring)
    value_grad, value_sums, *totals = mixer.backward_part(grad_mixed, half, mixer.pairs, part)
    grad_value_in = value_grad[:, :inner]
    gate_ring.step()
    normed = tie(normed, gate_ring)
    value_ring = RingSum(row_major(contract_rows(normed, grad_value_in).astype(low)))
    gate_ring.step()
    totals[0] = tie(totals[0], gate_ring, value_ring)
    totals[0], product = together(totals[0], product)
    ends = mixer.backward_end(*totals)
    pulled = mixer.gradients(value_grad, value_sums, *ends)
    grad_state_in = jnp.concatenate([pulled[1], pulled[2]], 1)
    state_partial = row_major(contract_rows(normed, grad_state_in).astype(low))
    grad_state_step = scatter_rows(state_partial).astype(wide)

    value_ring.step()
    gate_ring.step()
    grad_gate_in = tie(grad_gate_in, gate_ring, value_ring)
    grad_normed_part = contract_cols(full_gate, grad_gate_in)
    grad_value_state_in = jnp.concatenate([grad_value_in, grad_state_in], 1)
    value_ring.step()
    gate_ring.step()
    grad_value_state_in = tie(grad_value_state_in, gate_ring, value_ring)
    grad_normed_part = grad_normed_part + contract_cols(full_value_state, grad_value_state_in)
    grad_normed_part = row_major(grad_normed_part.astype(low))
    value_ring.step()
    grad_out = tie(grad_out, value_ring)
    grad_gate = gate_ring.finish()
    grad_value = value_ring.finish()

    grad_normed = lax.psum_scatter(
        grad_normed_part, "gy", scatter_dimension=0, tiled=True
    ).T.astype(wide)
    token_cols = lax.dynamic_slice_in_dim(layer_input, col_start, col_width, 1).astype(wide)
    gain_cols = lax.dynamic_slice_in_dim(norm_gain, col_start, col_width, 0)
    weighted = grad_normed * gain_cols
    inner_dot = lax.psum(jnp.sum(weighted * token_cols, axis=1), "gy")[:, None]
    grad_input = (
        cotangent.astype(wide)
        + scale_in * weighted
        - token_cols * scale_in**3 * inner_dot / model_width
    )
    grad_norm_gain = butterfly_sum(jnp.sum(grad_normed * token_cols * scale_in, axis=0), "gx")
    layer_output = (token_cols + product.T.astype(wide)).astype(low)

    small = (gate_gain_part,) + pulled[3:]
    packed = jnp.concatenate([v.reshape(-1) for v in small])
    packed = butterfly_sum(packed, "gx")
    sums, start = [], 0
    for v in small:
        sums.append(packed[start : start + v.size].reshape(v.shape))
        start += v.size
    state_sums = butterfly_sum(
        jnp.concatenate([grad_state_step[:, :state_cols], sums[3], sums[4][None]], 0), "gy"
    )
    state_rows = state_weight.shape[0]
    return (
        layer_output,
        grad_input,
        grad_norm_gain,
        grad_gate,
        grad_value,
        state_sums[:state_rows],
        grad_state_step[:, state_cols:],
        sums[1],
        sums[2],
        state_sums[state_rows:-1],
        state_sums[-1],
        sums[5],
        sums[6],
        sums[7],
        sums[0],
        grad_out.T.astype(wide),
    )


def solution(mesh):
    return jax.shard_map(
        on_device,
        mesh=mesh,
        in_specs=(
            P("gx", None),
            P(),
            P("gx", "gy"),
            P("gx", "gy"),
            P("gx", None),
            P("gx", "gy"),
            P(None, "gy"),
            P("gy"),
            P(),
            P(),
            P("gy"),
            P("gy"),
            P("gy"),
            P("gy"),
            P("gy", "gx"),
            P("gx"),
            P("gx", "gy"),
        ),
        out_specs=(
            P("gx", "gy"),
            P("gx", "gy"),
            P("gy"),
            P("gx", "gy"),
            P("gx", "gy"),
            P("gx", None),
            P("gx", "gy"),
            P(None, "gy"),
            P("gy"),
            P(),
            P(),
            P("gy"),
            P("gy"),
            P("gy"),
            P("gy"),
            P("gy", "gx"),
        ),
        check_vma=False,
    )
```

```python
import functools

import jax
import jax.numpy as jnp
from jax import lax
from jax.experimental import pallas as pl
from jax.experimental.layout import Layout, with_layout_constraint
from jax.experimental.pallas import tpu as pltpu
from jax.sharding import PartitionSpec as P

INNER = 5120
SPAN = 128
LANES = 128
HALF = 64
LOG2E = 1.4426950408889634
VMEM_BYTES = 56 * 1024 * 1024

epsilon = 1e-05
highest = lax.Precision.HIGHEST
low = jnp.bfloat16
wide = jnp.float32


def dot(left, right, precision=None):
    return jnp.dot(left, right, preferred_element_type=wide, precision=precision)


def contract_rows(left, right, precision=None):
    return lax.dot_general(
        left, right, (((0,), (0,)), ((), ())), preferred_element_type=wide, precision=precision
    )


def contract_cols(left, right, precision=None):
    return lax.dot_general(
        left, right, (((1,), (1,)), ((), ())), preferred_element_type=wide, precision=precision
    )


def sigmoid(v):
    return 1.0 / (1.0 + jnp.exp(-v))


def softplus(v):
    return jnp.maximum(v, 0.0) + jnp.log1p(jnp.exp(-jnp.abs(v)))


def conv_in(v, taps, bias, masks):
    total = bias + taps[0:1] * v
    for k in range(1, 4):
        total = total + taps[k : k + 1] * (pltpu.roll(v, k, 0) * masks[k - 1])
    return total


def conv_back(grad, v, taps, masks):
    rows = grad.shape[0]
    back = taps[0:1] * grad
    sums = [jnp.sum(grad * v, axis=0, keepdims=True)]
    for k in range(1, 4):
        kept = grad * masks[k - 1]
        sums.append(jnp.sum(kept * pltpu.roll(v, k, 0), axis=0, keepdims=True))
        back = back + taps[k : k + 1] * pltpu.roll(kept, rows - k, 0)
    sums.append(jnp.sum(grad, axis=0, keepdims=True))
    return back, sums


def visible_block(seg_col, seg_row, row_is_query):
    shape = (SPAN, SPAN)
    first = lax.broadcasted_iota(jnp.int32, shape, 0)
    second = lax.broadcasted_iota(jnp.int32, shape, 1)
    ordered = (first >= second) if row_is_query else (first <= second)
    return ordered & (seg_col == seg_row)


def lower_triangle():
    shape = (SPAN, SPAN)
    return (
        lax.broadcasted_iota(jnp.int32, shape, 0) >= lax.broadcasted_iota(jnp.int32, shape, 1)
    ).astype(wide)


def prep_kernel(
    state_ref, step_ref, taps_ref, bias_ref, step_bias_ref, rate_ref, masks_ref, seg_col_ref,
    seg_row_ref, b_ref, c_ref, bt_ref, ct_ref, g_ref, gt_ref, dtx_ref, cumx_ref, cumt_ref,
):
    rows, states = b_ref.shape
    masks = [masks_ref[k] for k in range(3)]
    for part, (out, out_t) in enumerate(((b_ref, bt_ref), (c_ref, ct_ref))):
        cols = slice(part * states, (part + 1) * states)
        pre = conv_in(state_ref[:, cols], taps_ref[:, cols], bias_ref[:, cols], masks)
        act = pre * sigmoid(pre)
        out[...] = act.astype(low)
        out_t[...] = act.T.astype(low)
    step = softplus(step_ref[...] + step_bias_ref[...])
    triangle = lower_triangle()
    heads = lax.broadcasted_iota(jnp.int32, (LANES, dtx_ref.shape[1]), 0)
    channels = lax.broadcasted_iota(jnp.int32, (LANES, dtx_ref.shape[1]), 1)
    expand = (channels // HALF == heads).astype(wide)
    rate = step * (rate_ref[...] * LOG2E)
    for c in range(rows // SPAN):
        at = slice(c * SPAN, (c + 1) * SPAN)
        grams = dot(c_ref[at], bt_ref[:, at])
        g_ref[at] = jnp.where(visible_block(seg_col_ref[at], seg_row_ref[:, at], True), grams, 0.0)
        grams_t = dot(b_ref[at], ct_ref[:, at])
        gt_ref[at] = jnp.where(
            visible_block(seg_col_ref[at], seg_row_ref[:, at], False), grams_t, 0.0
        )
        total = dot(triangle, rate[at], highest)
        cumx_ref[at] = dot(total, expand, highest)
        dtx_ref[at] = dot(step[at], expand, highest)
        cumt_ref[:, at] = total.T


def decays(cumx_ref, cumt_ref, at, head, row_is_query):
    lane = head * HALF
    column = cumx_ref[at, lane : lane + 1]
    row = cumt_ref[0, head : head + 1, at]
    gap = (column - row) if row_is_query else (row - column)
    return jnp.exp2(jnp.minimum(gap, 0.0))


def split_heads(block):
    left = lax.broadcasted_iota(jnp.int32, block.shape, 1) < HALF
    zero = jnp.zeros_like(block)
    return jnp.concatenate([jnp.where(left, block, zero), jnp.where(left, zero, block)], 0)


def fwd_kernel(
    value_ref, taps_ref, bias_ref, skip_ref, dtx_ref, cumx_ref, cumt_ref, masks_ref, c_ref, bt_ref,
    g_ref, out_ref, x_scr,
):
    rows = value_ref.shape[0]
    masks = [masks_ref[k] for k in range(3)]
    pre = conv_in(value_ref[...], taps_ref[...], bias_ref[...], masks)
    x_scr[...] = pre * sigmoid(pre)
    state = jnp.zeros((c_ref.shape[1], LANES), wide)
    for c in range(rows // SPAN):
        at = slice(c * SPAN, (c + 1) * SPAN)
        x = x_scr[at]
        cum = cumx_ref[at]
        stepped = x * dtx_ref[at]
        mixing = jnp.concatenate(
            [decays(cumx_ref, cumt_ref, at, head, True) * g_ref[at] for head in (0, 1)], 1
        ).astype(low)
        y = dot(mixing, split_heads(stepped.astype(low)))
        if c > 0:
            y = y + dot(c_ref[at], state.astype(low)) * (jnp.exp2(cum) * masks_ref[3, at])
        out_ref[at] = y + skip_ref[...] * x
        if c + 1 < rows // SPAN:
            end = slice((c + 1) * SPAN - 1, (c + 1) * SPAN)
            last = cum[SPAN - 1 : SPAN]
            tail = jnp.exp2(last - cum) * masks_ref[4, at]
            fresh = dot(bt_ref[:, at], (stepped.astype(low) * tail).astype(low))
            state = (masks_ref[3, end] * jnp.exp2(last)) * state + fresh


def bwd_kernel(
    first, resumed, value_ref, mixed_ref, grad_ref, taps_ref, bias_ref, skip_ref, dtx_ref, cumx_ref, cumt_ref,
    masks_ref, b_ref, c_ref, bt_ref, ct_ref, gt_ref, *more,
):
    earlier, more = more[: 7 * resumed], more[7 * resumed :]
    value_out, sums_out, *totals, pre_scr, x_scr, dpre_scr, state_scr = more
    db_ref, dc_ref, dg_ref, z_ref, dt_ref = totals
    rows = value_ref.shape[0]
    blocks = rows // SPAN
    pair = pl.program_id(0) + first
    masks = [masks_ref[k] for k in range(3)]

    @pl.when(pl.program_id(0) == 0)
    def _():
        for place, ref in enumerate(totals):
            ref[...] = earlier[2 + place][...] if resumed else jnp.zeros_like(ref)

    pre = conv_in(value_ref[...], taps_ref[...], bias_ref[...], masks)
    pre_scr[...] = pre
    x_scr[...] = pre * sigmoid(pre)
    state = jnp.zeros((c_ref.shape[1], LANES), wide)
    for c in range(blocks):
        at = slice(c * SPAN, (c + 1) * SPAN)
        state_scr[c] = state
        if c + 1 < blocks:
            end = slice((c + 1) * SPAN - 1, (c + 1) * SPAN)
            cum = cumx_ref[at]
            last = cum[SPAN - 1 : SPAN]
            tail = jnp.exp2(last - cum) * masks_ref[4, at]
            stepped = (x_scr[at] * dtx_ref[at]).astype(low)
            fresh = dot(bt_ref[:, at], (stepped * tail).astype(low))
            state = (masks_ref[3, end] * jnp.exp2(last)) * state + fresh

    lanes = lax.broadcasted_iota(jnp.int32, (LANES, LANES), 0)
    heads = lax.broadcasted_iota(jnp.int32, (LANES, LANES), 1)
    gather = (lanes // HALF + 2 * pair == heads).astype(low)
    row_number = lax.broadcasted_iota(jnp.int32, (SPAN, LANES), 0)
    grad_skip = jnp.zeros((1, LANES), wide)
    grad_state = jnp.zeros((c_ref.shape[1], LANES), wide)
    for c in reversed(range(blocks)):
        at = slice(c * SPAN, (c + 1) * SPAN)
        end = slice((c + 1) * SPAN - 1, (c + 1) * SPAN)
        x = x_scr[at]
        dtx = dtx_ref[at]
        cum = cumx_ref[at]
        grad = grad_ref[at]
        grad_low = grad.astype(low)
        stepped = (x * dtx).astype(low)
        y = mixed_ref[at] - skip_ref[...] * x
        grad_mix = contract_cols(split_heads(stepped), grad_low)
        mixing = []
        grams = dg_ref[at]
        for head in (0, 1):
            decay = decays(cumx_ref, cumt_ref, at, head, False)
            mixing.append((decay * gt_ref[at]).astype(low))
            grams = grams + decay * grad_mix[head * SPAN : (head + 1) * SPAN]
        dg_ref[at] = grams
        grad_stepped = dot(jnp.concatenate(mixing, 1), split_heads(grad_low))
        last = cum[SPAN - 1 : SPAN]
        at_end = jnp.zeros((1, LANES), wide)
        carry = masks_ref[3, end] * jnp.exp2(last)
        if c + 1 < blocks:
            tail = jnp.exp2(last - cum) * masks_ref[4, at]
            grad_state_low = grad_state.astype(low)
            from_tail = dot(b_ref[at], grad_state_low) * tail
            grad_stepped = grad_stepped + from_tail
            db_ref[at] += contract_cols((stepped * tail).astype(low), grad_state_low)
            at_end = jnp.sum(stepped.astype(wide) * from_tail, axis=0, keepdims=True)
            at_end = at_end + carry * jnp.sum(state_scr[c] * grad_state, axis=0, keepdims=True)
        if c > 0:
            reach = (grad * (jnp.exp2(cum) * masks_ref[3, at])).astype(low)
            dc_ref[at] += contract_cols(reach, state_scr[c].astype(low))
            grad_state = carry * grad_state + dot(ct_ref[:, at], reach)
        z = grad_low.astype(wide) * y - stepped.astype(wide) * grad_stepped
        z = z + jnp.where(row_number == SPAN - 1, at_end, 0.0)
        z_high = z.astype(low)
        z_low = (z - z_high.astype(wide)).astype(low)
        z_ref[at] += dot(z_high, gather) + dot(z_low, gather)
        dt_ref[at] += dot((x * grad_stepped).astype(low), gather)
        grad_skip = grad_skip + jnp.sum(grad * x, axis=0, keepdims=True)
        pre_c = pre_scr[at]
        opened = sigmoid(pre_c)
        grad_x = grad_stepped * dtx + skip_ref[...] * grad
        dpre_scr[at] = grad_x * opened * (1.0 + pre_c * (1.0 - opened))

    back, sums = conv_back(dpre_scr[...], value_ref[...], taps_ref[...], masks)
    value_out[...] = back.astype(low)
    sums_out[...] = jnp.concatenate(sums + [grad_skip, jnp.zeros((2, LANES), wide)], 0)


def post_kernel(
    state_ref, step_ref, taps_ref, bias_ref, step_bias_ref, rate_ref, masks_ref, seg_col_ref,
    seg_row_ref, b_ref, c_ref, db_ref, dc_ref, dg_ref, z_ref, dt_ref,
    state_out, step_out, state_sums, step_sums, act_scr,
):
    rows, states = b_ref.shape
    masks = [masks_ref[k] for k in range(3)]
    triangle = lower_triangle()
    for c in range(rows // SPAN):
        at = slice(c * SPAN, (c + 1) * SPAN)
        seen = visible_block(seg_col_ref[at], seg_row_ref[:, at], False)
        grams = jnp.where(seen, dg_ref[at], 0.0)
        act_scr[0, at] = db_ref[at] + dot(grams.astype(low), c_ref[at])
        act_scr[1, at] = dc_ref[at] + dot(grams.T.astype(low), b_ref[at])
    for part in (0, 1):
        cols = slice(part * states, (part + 1) * states)
        v = state_ref[:, cols]
        pre = conv_in(v, taps_ref[:, cols], bias_ref[:, cols], masks)
        opened = sigmoid(pre)
        grad = act_scr[part] * opened * (1.0 + pre * (1.0 - opened))
        back, sums = conv_back(grad, v, taps_ref[:, cols], masks)
        state_out[:, cols] = back.astype(low)
        state_sums[:, cols] = jnp.concatenate(sums + [jnp.zeros((3, states), wide)], 0)
    pre = step_ref[...] + step_bias_ref[...]
    step = softplus(pre)
    rate_sum = jnp.zeros((1, LANES), wide)
    bias_sum = jnp.zeros((1, LANES), wide)
    for c in range(rows // SPAN):
        at = slice(c * SPAN, (c + 1) * SPAN)
        grad_rate = contract_rows(triangle, z_ref[at], highest)
        grad_step = (dt_ref[at] + rate_ref[...] * grad_rate) * sigmoid(pre[at])
        step_out[at] = grad_step.astype(low)
        rate_sum = rate_sum + jnp.sum(
            grad_rate * (rate_ref[...] * step[at]), axis=0, keepdims=True
        )
        bias_sum = bias_sum + jnp.sum(grad_step, axis=0, keepdims=True)
    step_sums[...] = jnp.concatenate([bias_sum, rate_sum, jnp.zeros((6, LANES), wide)], 0)


def call(
    kernel, outs, operands, grid=None, in_specs=None, out_specs=None, scratch=(), flops=0, aliases={}
):
    shapes = tuple(jax.ShapeDtypeStruct(shape, kind) for shape, kind in outs)
    moved = sum(a.size * a.dtype.itemsize for a in operands)
    moved += sum(s.size * s.dtype.itemsize for s in shapes)
    extra = {} if grid is None else dict(grid=grid, in_specs=in_specs, out_specs=out_specs)
    return pl.pallas_call(
        kernel,
        out_shape=shapes,
        scratch_shapes=list(scratch),
        compiler_params=pltpu.CompilerParams(vmem_limit_bytes=VMEM_BYTES),
        input_output_aliases=dict(aliases),
        cost_estimate=pl.CostEstimate(flops=flops, bytes_accessed=moved, transcendentals=0),
        **extra,
    )(*operands)


def column_block(rows, first=0):
    return pl.BlockSpec((rows, LANES), lambda i: (0, i + first))


def whole_block(shape):
    return pl.BlockSpec(shape, lambda i: (0,) * len(shape))


def lane_pad(v):
    return jnp.pad(v, ((0, 0), (0, LANES - v.shape[1])))


class Mixer:
    def __init__(
        self, state_in, step_in, conv_state, conv_state_bias, step_bias, decay_log, segments
    ):
        rows = state_in.shape[0]
        self.rows = rows
        self.head_count = step_bias.shape[0]
        self.pairs = (self.head_count + 1) // 2
        self.width = self.pairs * LANES
        self.states = conv_state.shape[1] // 2
        self.blocks = rows // SPAN
        before = [
            jnp.concatenate([jnp.full((k,), -1, jnp.int32), segments[: rows - k]]) == segments
            for k in (1, 2, 3)
        ]
        ends = segments.reshape(self.blocks, SPAN)[:, SPAN - 1]
        previous = jnp.concatenate([jnp.full((1,), -1, jnp.int32), ends[:-1]])
        carried = jnp.repeat(previous, SPAN) == segments
        tail = jnp.repeat(ends, SPAN) == segments
        flags = jnp.stack(before + [carried, tail]).astype(wide)
        self.masks = jnp.broadcast_to(flags[:, :, None], (5, rows, LANES))
        self.shared = (
            state_in,
            lane_pad(step_in),
            conv_state,
            conv_state_bias[None],
            lane_pad(step_bias[None]),
            lane_pad(-jnp.exp(decay_log)[None]),
            self.masks,
            segments[:, None],
            segments[None],
        )
        (
            self.b, self.c, self.bt, self.ct, self.g, self.gt, self.dtx, self.cumx, cumt,
        ) = call(
            prep_kernel,
            [((rows, self.states), low)] * 2
            + [((self.states, rows), low)] * 2
            + [((rows, SPAN), wide)] * 2
            + [((rows, self.width), wide)] * 2
            + [((LANES, rows), wide)],
            self.shared,
            flops=12 * rows * LANES * self.width,
        )
        self.cumt = cumt[: 2 * self.pairs].reshape(self.pairs, 2, rows)

    def widen(self, v):
        return jnp.pad(v, ((0, 0), (0, self.width - v.shape[1])))

    def forward(self, value_in, conv_value, conv_value_bias, skip_scale):
        rows, states = self.rows, self.states
        self.inner = value_in.shape[1]
        self.value = (
            self.widen(value_in),
            self.widen(conv_value),
            self.widen(conv_value_bias[None]),
            self.widen(jnp.repeat(skip_scale, HALF)[None]),
        )
        (mixed,) = call(
            fwd_kernel,
            [((rows, self.width), wide)],
            self.value + (self.dtx, self.cumx, self.cumt, self.masks, self.c, self.bt, self.g),
            grid=(self.pairs,),
            in_specs=[
                column_block(rows),
                column_block(4),
                column_block(1),
                column_block(1),
                column_block(rows),
                column_block(rows),
                pl.BlockSpec((1, 2, rows), lambda i: (i, 0, 0)),
                whole_block((5, rows, LANES)),
                whole_block((rows, states)),
                whole_block((states, rows)),
                whole_block((rows, SPAN)),
            ],
            out_specs=[column_block(rows)],
            scratch=[pltpu.VMEM((rows, LANES), wide)],
            flops=20 * rows * LANES * self.width,
        )
        self.mixed = mixed
        return mixed[:, : self.inner]

    def backward_part(self, grad_mixed, first, last, earlier=()):
        rows, states = self.rows, self.states
        operands = (
            (self.value[0], self.mixed, self.widen(grad_mixed))
            + self.value[1:]
            + (self.dtx, self.cumx, self.cumt, self.masks, self.b, self.c, self.bt, self.ct)
            + (self.gt,)
        )
        totals = [whole_block((rows, LANES))] * 5
        resumed = bool(earlier)
        return call(
            functools.partial(bwd_kernel, first, resumed),
            [((rows, self.width), low), ((8, self.width), wide)]
            + [((rows, LANES), wide)] * 5,
            operands + tuple(earlier),
            grid=(last - first,),
            in_specs=[
                column_block(rows, first),
                column_block(rows, first),
                column_block(rows, first),
                column_block(4, first),
                column_block(1, first),
                column_block(1, first),
                column_block(rows, first),
                column_block(rows, first),
                pl.BlockSpec((1, 2, rows), lambda i: (i + first, 0, 0)),
                whole_block((5, rows, LANES)),
                whole_block((rows, states)),
                whole_block((rows, states)),
                whole_block((states, rows)),
                whole_block((states, rows)),
                whole_block((rows, SPAN)),
            ]
            + ([pl.BlockSpec(memory_space=pl.ANY)] * 2 + totals if resumed else []),
            out_specs=[column_block(rows, first), column_block(8, first)] + totals,
            scratch=[pltpu.VMEM((rows, LANES), wide)] * 3
            + [pltpu.VMEM((self.blocks, states, LANES), wide)],
            flops=60 * rows * LANES * (last - first) * LANES,
            aliases={len(operands): 0, len(operands) + 1: 1} if resumed else {},
        )

    def backward_end(self, db, dc, dg, z, dt):
        rows, states = self.rows, self.states
        return call(
            post_kernel,
            [
                ((rows, 2 * states), low),
                ((rows, LANES), low),
                ((8, 2 * states), wide),
                ((8, LANES), wide),
            ],
            self.shared + (self.b, self.c, db, dc, dg, z, dt),
            scratch=[pltpu.VMEM((2, rows, states), wide)],
            flops=12 * rows * LANES * self.width,
        )

    def backward(self, grad_mixed):
        half = (self.pairs + 1) // 2
        part = self.backward_part(grad_mixed, 0, half)
        value_grad, sums, *totals = self.backward_part(grad_mixed, half, self.pairs, part)
        return self.gradients(value_grad, sums, *self.backward_end(*totals))

    def gradients(self, value_grad, sums, state_grad, step_grad, state_sums, step_sums):
        heads = self.head_count
        skip_grad = sums[5, : self.inner].reshape(heads, HALF).sum(axis=1)
        return (
            value_grad[:, : self.inner],
            state_grad,
            step_grad[:, :heads],
            sums[:4, : self.inner],
            sums[4, : self.inner],
            state_sums[:4],
            state_sums[4],
            step_sums[0, :heads],
            step_sums[1, :heads],
            skip_grad,
        )


def ring_place(index, count):
    return jnp.where(index % 2 == 0, index // 2, count - 1 - index // 2)


def ring_index(place, count):
    place = place % count
    return jnp.where(place < (count + 1) // 2, 2 * place, 2 * (count - 1 - place) + 1)


def ring_moves(count):
    order = list(range(0, count, 2)) + list(range(1, count, 2))[::-1]
    ahead = [(order[k], order[(k + 1) % count]) for k in range(count)]
    return ahead, [(target, source) for source, target in ahead]


class RingGather:
    def __init__(self, shard):
        self.count = lax.axis_size("gx")
        self.moves = ring_moves(self.count)
        me = lax.axis_index("gx")
        self.place = ring_place(me, self.count)
        self.rows, width = shard.shape
        self.half = self.rows // 2
        self.taken = 0
        self.held = (shard[: self.half], shard[self.half :])
        self.waiting = []
        full = jnp.zeros((self.count * self.rows, width), shard.dtype)
        self.full = lax.dynamic_update_slice(full, shard, (me * self.rows, 0))

    def step(self, times=1, place=True):
        for _ in range(min(times, self.count - 1 - self.taken)):
            self.taken += 1
            self.held = tuple(
                lax.ppermute(held, "gx", move) for held, move in zip(self.held, self.moves)
            )
            for piece, sign, offset in zip(self.held, (-1, 1), (0, self.half)):
                owner = ring_index(self.place + sign * self.taken, self.count)
                self.waiting.append((piece, owner * self.rows + offset))
            if place:
                if len(self.waiting) > 2:
                    self.held, self.full = lax.optimization_barrier((self.held, self.full))
                for piece, start in self.waiting:
                    self.full = lax.dynamic_update_slice(self.full, piece, (start, 0))
                self.waiting = []
        return self.held

    def finish(self):
        self.step(self.count)
        return self.full


class RingSum:
    def __init__(self, partial):
        self.count = lax.axis_size("gx")
        self.moves = ring_moves(self.count)
        self.place = ring_place(lax.axis_index("gx"), self.count)
        self.rows = partial.shape[0] // self.count
        self.half = self.rows // 2
        self.partial = partial
        self.taken = 0
        self.held = (self.part(-1, 0), self.part(1, self.half))

    def part(self, target, offset):
        start = ring_index(self.place + target, self.count) * self.rows + offset
        return lax.dynamic_slice_in_dim(self.partial, start, self.half, 0)

    def step(self, times=1):
        for _ in range(min(times, self.count - 1 - self.taken)):
            self.taken += 1
            up, down = (
                lax.ppermute(held, "gx", move).astype(wide)
                for held, move in zip(self.held, self.moves)
            )
            up = up + self.part(-1 - self.taken, 0).astype(wide)
            down = down + self.part(1 + self.taken, self.half).astype(wide)
            if self.taken < self.count - 1:
                up, down = up.astype(low), down.astype(low)
            self.held = (up, down)
        return self.held

    def finish(self):
        return jnp.concatenate(self.step(self.count), 0)


def flips(count, bit):
    return [(k, k ^ bit) for k in range(count)]


def butterfly_sum(v, axis):
    count = lax.axis_size(axis)
    bit = 1
    while bit < count:
        v = v + lax.ppermute(v, axis, flips(count, bit))
        bit *= 2
    return v


def scatter_rows(partial):
    return lax.psum_scatter(partial, "gx", scatter_dimension=0, tiled=True)


def row_major(v):
    return with_layout_constraint(v, Layout((0, 1)))


def together(*values):
    return lax.optimization_barrier(values)


def tie(value, *rings):
    value, held = lax.optimization_barrier((value, [ring.held for ring in rings]))
    for ring, pieces in zip(rings, held):
        ring.held = tuple(pieces)
    return value


def on_device(
    layer_input,
    norm_gain,
    gate_weight,
    value_weight,
    state_weight,
    step_weight,
    conv_value,
    conv_value_bias,
    conv_state,
    conv_state_bias,
    step_bias,
    decay_log,
    skip_scale,
    gated_gain,
    out_weight,
    segment_ids,
    cotangent,
):
    model_width = layer_input.shape[1]
    col_width = cotangent.shape[1]
    state_cols = state_weight.shape[1]
    col_start = lax.axis_index("gy") * col_width

    inner = gate_weight.shape[1]
    upstream = lax.all_gather(cotangent, "gy", axis=1, tiled=True)
    value_gather = RingGather(jnp.concatenate([value_weight, state_weight, step_weight], 1))
    value_gather.step()
    tokens = tie(layer_input, value_gather).astype(wide)
    scale_in = lax.rsqrt(jnp.mean(tokens * tokens, axis=1, keepdims=True) + epsilon)
    normed = (tokens * scale_in * norm_gain).astype(low)
    value_gather.step()
    normed = tie(normed, value_gather)
    full_value_state = value_gather.finish()

    gate_gather = RingGather(tie(gate_weight, value_gather))
    gate_gather.step(place=False)
    normed = tie(normed, gate_gather)
    state_step = dot(normed, full_value_state[:, inner:])
    mixer = Mixer(
        state_step[:, :state_cols],
        state_step[:, state_cols:],
        conv_state,
        conv_state_bias,
        step_bias,
        decay_log,
        segment_ids,
    )
    gate_gather.step(place=False)
    normed, mixer.g = together(normed, mixer.g)
    normed = tie(normed, gate_gather)
    value_in = dot(normed, full_value_state[:, :inner])
    gate_gather.step(place=False)
    value_in = tie(value_in, gate_gather)
    mixed = mixer.forward(value_in, conv_value, conv_value_bias, skip_scale)
    gate_gather.step(place=False)
    mixed = mixer.mixed = tie(mixer.mixed, gate_gather)
    mixed = mixed[:, : mixer.inner]
    full_gate = gate_gather.finish()
    out_gather = RingGather(tie(out_weight.T, gate_gather))
    out_gather.step(place=False)
    normed = tie(normed, out_gather)
    gate_in = dot(normed, full_gate)
    out_gather.step(place=False)
    gate_in = tie(gate_in, out_gather)
    full_out = out_gather.finish()
    up_back = dot(upstream, full_out)
    gate_open = jax.nn.sigmoid(gate_in)
    gate_act = gate_in * gate_open
    gated = mixed * gate_act

    sums_out = lax.psum(
        jnp.stack(
            [jnp.sum(gated * gated, axis=1), jnp.sum(gated * gated_gain * up_back, axis=1)]
        ),
        "gy",
    )
    scale_out = lax.rsqrt(sums_out[0] / INNER + epsilon)[:, None]
    grad_scale = sums_out[1][:, None]
    scaled = (gated * gated_gain).astype(low)

    scaled_out = (gated * gated_gain * scale_out).astype(low)
    out_ring = RingSum(row_major(contract_rows(upstream, scaled_out).astype(low)))

    scaled = tie(scaled, out_ring)
    product_part = contract_cols(full_out, scaled)
    product_part = row_major((product_part * scale_out[:, 0]).astype(low))
    product = lax.psum_scatter(product_part, "gy", scatter_dimension=0, tiled=True)

    out_ring.step()
    up_back, product_part = together(up_back, product_part)
    grad_scaled = scale_out * tie(up_back, out_ring)
    grad_gated = grad_scaled * gated_gain - grad_scale * scale_out**3 * gated / INNER
    gate_gain_part = jnp.sum(grad_scaled * gated, axis=0)
    grad_gate_in = (
        grad_gated * mixed * gate_open * (1.0 + gate_in * (1.0 - gate_open))
    ).astype(low)
    grad_mixed = grad_gated * gate_act
    out_ring.step()
    normed = tie(normed, out_ring)
    gate_ring = RingSum(row_major(contract_rows(normed, grad_gate_in).astype(low)))

    half = (mixer.pairs + 1) // 2
    out_ring.step()
    grad_mixed = tie(grad_mixed, out_ring, gate_ring)
    part = mixer.backward_part(grad_mixed, 0, half)
    out_ring.step()
    gate_ring.step()
    grad_mixed = tie(grad_mixed, out_ring, gate_ring)
    value_grad, value_sums, *totals = mixer.backward_part(grad_mixed, half, mixer.pairs, part)
    grad_value_in = value_grad[:, : gate_weight.shape[1]]
    out_ring.step()
    gate_ring.step()
    normed = tie(normed, out_ring, gate_ring)
    value_ring = RingSum(row_major(contract_rows(normed, grad_value_in).astype(low)))
    out_ring.step()
    gate_ring.step()
    totals[0] = tie(totals[0], out_ring, gate_ring, value_ring)
    ends = mixer.backward_end(*totals)
    pulled = mixer.gradients(value_grad, value_sums, *ends)
    grad_state_in = jnp.concatenate([pulled[1], pulled[2]], 1)
    state_partial = row_major(contract_rows(normed, grad_state_in).astype(low))
    grad_state_step = scatter_rows(state_partial).astype(wide)

    value_ring.step()
    grad_gate_in = tie(grad_gate_in, value_ring)
    grad_normed_part = contract_cols(full_gate, grad_gate_in)
    grad_value_state_in = jnp.concatenate([grad_value_in, grad_state_in], 1)
    out_ring.step()
    gate_ring.step()
    grad_value_state_in = tie(grad_value_state_in, out_ring, gate_ring)
    grad_value_state_in, product = together(grad_value_state_in, product)
    grad_normed_part = grad_normed_part + contract_cols(full_value_state, grad_value_state_in)
    grad_normed_part = row_major(grad_normed_part.astype(low))
    grad_out = out_ring.finish()
    grad_gate = gate_ring.finish()
    grad_value = value_ring.finish()

    grad_normed = lax.psum_scatter(
        grad_normed_part, "gy", scatter_dimension=0, tiled=True
    ).T.astype(wide)
    token_cols = lax.dynamic_slice_in_dim(layer_input, col_start, col_width, 1).astype(wide)
    gain_cols = lax.dynamic_slice_in_dim(norm_gain, col_start, col_width, 0)
    weighted = grad_normed * gain_cols
    inner_dot = lax.psum(jnp.sum(weighted * token_cols, axis=1), "gy")[:, None]
    grad_input = (
        cotangent.astype(wide)
        + scale_in * weighted
        - token_cols * scale_in**3 * inner_dot / model_width
    )
    grad_norm_gain = butterfly_sum(jnp.sum(grad_normed * token_cols * scale_in, axis=0), "gx")
    layer_output = (token_cols + product.T.astype(wide)).astype(low)

    small = (gate_gain_part,) + pulled[3:]
    packed = jnp.concatenate([v.reshape(-1) for v in small])
    packed = butterfly_sum(packed, "gx")
    sums, start = [], 0
    for v in small:
        sums.append(packed[start : start + v.size].reshape(v.shape))
        start += v.size
    state_sums = butterfly_sum(
        jnp.concatenate([grad_state_step[:, :state_cols], sums[3], sums[4][None]], 0), "gy"
    )
    state_rows = state_weight.shape[0]
    return (
        layer_output,
        grad_input,
        grad_norm_gain,
        grad_gate,
        grad_value,
        state_sums[:state_rows],
        grad_state_step[:, state_cols:],
        sums[1],
        sums[2],
        state_sums[state_rows:-1],
        state_sums[-1],
        sums[5],
        sums[6],
        sums[7],
        sums[0],
        grad_out.T,
    )


def solution(mesh):
    return jax.shard_map(
        on_device,
        mesh=mesh,
        in_specs=(
            P("gx", None),
            P(),
            P("gx", "gy"),
            P("gx", "gy"),
            P("gx", None),
            P("gx", "gy"),
            P(None, "gy"),
            P("gy"),
            P(),
            P(),
            P("gy"),
            P("gy"),
            P("gy"),
            P("gy"),
            P("gy", "gx"),
            P("gx"),
            P("gx", "gy"),
        ),
        out_specs=(
            P("gx", "gy"),
            P("gx", "gy"),
            P("gy"),
            P("gx", "gy"),
            P("gx", "gy"),
            P("gx", None),
            P("gx", "gy"),
            P(None, "gy"),
            P("gy"),
            P(),
            P(),
            P("gy"),
            P("gy"),
            P("gy"),
            P("gy"),
            P("gy", "gx"),
        ),
        check_vma=False,
    )
```

```python
import functools

import jax
import jax.numpy as jnp
from jax import lax
from jax.experimental import pallas as pl
from jax.experimental.layout import Layout, with_layout_constraint
from jax.experimental.pallas import tpu as pltpu
from jax.sharding import PartitionSpec as P

INNER = 5120
SPAN = 128
LANES = 128
HALF = 64
LOG2E = 1.4426950408889634
VMEM_BYTES = 56 * 1024 * 1024

epsilon = 1e-05
highest = lax.Precision.HIGHEST
low = jnp.bfloat16
wide = jnp.float32


def dot(left, right, precision=None):
    return jnp.dot(left, right, preferred_element_type=wide, precision=precision)


def contract_rows(left, right, precision=None):
    return lax.dot_general(
        left, right, (((0,), (0,)), ((), ())), preferred_element_type=wide, precision=precision
    )


def contract_cols(left, right, precision=None):
    return lax.dot_general(
        left, right, (((1,), (1,)), ((), ())), preferred_element_type=wide, precision=precision
    )


def sigmoid(v):
    return 1.0 / (1.0 + jnp.exp(-v))


def softplus(v):
    return jnp.maximum(v, 0.0) + jnp.log1p(jnp.exp(-jnp.abs(v)))


def conv_in(v, taps, bias, masks):
    total = bias + taps[0:1] * v
    for k in range(1, 4):
        total = total + taps[k : k + 1] * (pltpu.roll(v, k, 0) * masks[k - 1])
    return total


def conv_back(grad, v, taps, masks):
    rows = grad.shape[0]
    back = taps[0:1] * grad
    sums = [jnp.sum(grad * v, axis=0, keepdims=True)]
    for k in range(1, 4):
        kept = grad * masks[k - 1]
        sums.append(jnp.sum(kept * pltpu.roll(v, k, 0), axis=0, keepdims=True))
        back = back + taps[k : k + 1] * pltpu.roll(kept, rows - k, 0)
    sums.append(jnp.sum(grad, axis=0, keepdims=True))
    return back, sums


def visible_block(seg_col, seg_row, row_is_query):
    shape = (SPAN, SPAN)
    first = lax.broadcasted_iota(jnp.int32, shape, 0)
    second = lax.broadcasted_iota(jnp.int32, shape, 1)
    ordered = (first >= second) if row_is_query else (first <= second)
    return ordered & (seg_col == seg_row)


def lower_triangle():
    shape = (SPAN, SPAN)
    return (
        lax.broadcasted_iota(jnp.int32, shape, 0) >= lax.broadcasted_iota(jnp.int32, shape, 1)
    ).astype(wide)


def prep_kernel(
    state_ref, step_ref, taps_ref, bias_ref, step_bias_ref, rate_ref, masks_ref, seg_col_ref,
    seg_row_ref, b_ref, c_ref, bt_ref, ct_ref, g_ref, gt_ref, dtx_ref, cumx_ref, cumt_ref,
):
    rows, states = b_ref.shape
    masks = [masks_ref[k] for k in range(3)]
    for part, (out, out_t) in enumerate(((b_ref, bt_ref), (c_ref, ct_ref))):
        cols = slice(part * states, (part + 1) * states)
        pre = conv_in(state_ref[:, cols], taps_ref[:, cols], bias_ref[:, cols], masks)
        act = pre * sigmoid(pre)
        out[...] = act.astype(low)
        out_t[...] = act.T.astype(low)
    step = softplus(step_ref[...] + step_bias_ref[...])
    triangle = lower_triangle()
    heads = lax.broadcasted_iota(jnp.int32, (LANES, dtx_ref.shape[1]), 0)
    channels = lax.broadcasted_iota(jnp.int32, (LANES, dtx_ref.shape[1]), 1)
    expand = (channels // HALF == heads).astype(wide)
    rate = step * (rate_ref[...] * LOG2E)
    for c in range(rows // SPAN):
        at = slice(c * SPAN, (c + 1) * SPAN)
        grams = dot(c_ref[at], bt_ref[:, at])
        g_ref[at] = jnp.where(visible_block(seg_col_ref[at], seg_row_ref[:, at], True), grams, 0.0)
        grams_t = dot(b_ref[at], ct_ref[:, at])
        gt_ref[at] = jnp.where(
            visible_block(seg_col_ref[at], seg_row_ref[:, at], False), grams_t, 0.0
        )
        total = dot(triangle, rate[at], highest)
        cumx_ref[at] = dot(total, expand, highest)
        dtx_ref[at] = dot(step[at], expand, highest)
        cumt_ref[:, at] = total.T


def decays(cumx_ref, cumt_ref, at, head, row_is_query):
    lane = head * HALF
    column = cumx_ref[at, lane : lane + 1]
    row = cumt_ref[0, head : head + 1, at]
    gap = (column - row) if row_is_query else (row - column)
    return jnp.exp2(jnp.minimum(gap, 0.0))


def split_heads(block):
    left = lax.broadcasted_iota(jnp.int32, block.shape, 1) < HALF
    zero = jnp.zeros_like(block)
    return jnp.concatenate([jnp.where(left, block, zero), jnp.where(left, zero, block)], 0)


def fwd_kernel(
    value_ref, taps_ref, bias_ref, skip_ref, dtx_ref, cumx_ref, cumt_ref, masks_ref, c_ref, bt_ref,
    g_ref, out_ref, x_scr,
):
    rows = value_ref.shape[0]
    masks = [masks_ref[k] for k in range(3)]
    pre = conv_in(value_ref[...], taps_ref[...], bias_ref[...], masks)
    x_scr[...] = pre * sigmoid(pre)
    state = jnp.zeros((c_ref.shape[1], LANES), wide)
    for c in range(rows // SPAN):
        at = slice(c * SPAN, (c + 1) * SPAN)
        x = x_scr[at]
        cum = cumx_ref[at]
        stepped = x * dtx_ref[at]
        mixing = jnp.concatenate(
            [decays(cumx_ref, cumt_ref, at, head, True) * g_ref[at] for head in (0, 1)], 1
        ).astype(low)
        y = dot(mixing, split_heads(stepped.astype(low)))
        if c > 0:
            y = y + dot(c_ref[at], state.astype(low)) * (jnp.exp2(cum) * masks_ref[3, at])
        out_ref[at] = y + skip_ref[...] * x
        if c + 1 < rows // SPAN:
            end = slice((c + 1) * SPAN - 1, (c + 1) * SPAN)
            last = cum[SPAN - 1 : SPAN]
            tail = jnp.exp2(last - cum) * masks_ref[4, at]
            fresh = dot(bt_ref[:, at], (stepped.astype(low) * tail).astype(low))
            state = (masks_ref[3, end] * jnp.exp2(last)) * state + fresh


def bwd_kernel(
    first, resumed, value_ref, mixed_ref, grad_ref, taps_ref, bias_ref, skip_ref, dtx_ref, cumx_ref, cumt_ref,
    masks_ref, b_ref, c_ref, bt_ref, ct_ref, gt_ref, *more,
):
    earlier, more = more[: 7 * resumed], more[7 * resumed :]
    value_out, sums_out, *totals, pre_scr, x_scr, dpre_scr, state_scr = more
    db_ref, dc_ref, dg_ref, z_ref, dt_ref = totals
    rows = value_ref.shape[0]
    blocks = rows // SPAN
    pair = pl.program_id(0) + first
    masks = [masks_ref[k] for k in range(3)]

    @pl.when(pl.program_id(0) == 0)
    def _():
        for place, ref in enumerate(totals):
            ref[...] = earlier[2 + place][...] if resumed else jnp.zeros_like(ref)

    pre = conv_in(value_ref[...], taps_ref[...], bias_ref[...], masks)
    pre_scr[...] = pre
    x_scr[...] = pre * sigmoid(pre)
    state = jnp.zeros((c_ref.shape[1], LANES), wide)
    for c in range(blocks):
        at = slice(c * SPAN, (c + 1) * SPAN)
        state_scr[c] = state
        if c + 1 < blocks:
            end = slice((c + 1) * SPAN - 1, (c + 1) * SPAN)
            cum = cumx_ref[at]
            last = cum[SPAN - 1 : SPAN]
            tail = jnp.exp2(last - cum) * masks_ref[4, at]
            stepped = (x_scr[at] * dtx_ref[at]).astype(low)
            fresh = dot(bt_ref[:, at], (stepped * tail).astype(low))
            state = (masks_ref[3, end] * jnp.exp2(last)) * state + fresh

    lanes = lax.broadcasted_iota(jnp.int32, (LANES, LANES), 0)
    heads = lax.broadcasted_iota(jnp.int32, (LANES, LANES), 1)
    gather = (lanes // HALF + 2 * pair == heads).astype(low)
    row_number = lax.broadcasted_iota(jnp.int32, (SPAN, LANES), 0)
    grad_skip = jnp.zeros((1, LANES), wide)
    grad_state = jnp.zeros((c_ref.shape[1], LANES), wide)
    for c in reversed(range(blocks)):
        at = slice(c * SPAN, (c + 1) * SPAN)
        end = slice((c + 1) * SPAN - 1, (c + 1) * SPAN)
        x = x_scr[at]
        dtx = dtx_ref[at]
        cum = cumx_ref[at]
        grad = grad_ref[at]
        grad_low = grad.astype(low)
        stepped = (x * dtx).astype(low)
        y = mixed_ref[at] - skip_ref[...] * x
        grad_mix = contract_cols(split_heads(stepped), grad_low)
        mixing = []
        grams = dg_ref[at]
        for head in (0, 1):
            decay = decays(cumx_ref, cumt_ref, at, head, False)
            mixing.append((decay * gt_ref[at]).astype(low))
            grams = grams + decay * grad_mix[head * SPAN : (head + 1) * SPAN]
        dg_ref[at] = grams
        grad_stepped = dot(jnp.concatenate(mixing, 1), split_heads(grad_low))
        last = cum[SPAN - 1 : SPAN]
        at_end = jnp.zeros((1, LANES), wide)
        carry = masks_ref[3, end] * jnp.exp2(last)
        if c + 1 < blocks:
            tail = jnp.exp2(last - cum) * masks_ref[4, at]
            grad_state_low = grad_state.astype(low)
            from_tail = dot(b_ref[at], grad_state_low) * tail
            grad_stepped = grad_stepped + from_tail
            db_ref[at] += contract_cols((stepped * tail).astype(low), grad_state_low)
            at_end = jnp.sum(stepped.astype(wide) * from_tail, axis=0, keepdims=True)
            at_end = at_end + carry * jnp.sum(state_scr[c] * grad_state, axis=0, keepdims=True)
        if c > 0:
            reach = (grad * (jnp.exp2(cum) * masks_ref[3, at])).astype(low)
            dc_ref[at] += contract_cols(reach, state_scr[c].astype(low))
            grad_state = carry * grad_state + dot(ct_ref[:, at], reach)
        z = grad_low.astype(wide) * y - stepped.astype(wide) * grad_stepped
        z = z + jnp.where(row_number == SPAN - 1, at_end, 0.0)
        z_high = z.astype(low)
        z_low = (z - z_high.astype(wide)).astype(low)
        z_ref[at] += dot(z_high, gather) + dot(z_low, gather)
        dt_ref[at] += dot((x * grad_stepped).astype(low), gather)
        grad_skip = grad_skip + jnp.sum(grad * x, axis=0, keepdims=True)
        pre_c = pre_scr[at]
        opened = sigmoid(pre_c)
        grad_x = grad_stepped * dtx + skip_ref[...] * grad
        dpre_scr[at] = grad_x * opened * (1.0 + pre_c * (1.0 - opened))

    back, sums = conv_back(dpre_scr[...], value_ref[...], taps_ref[...], masks)
    value_out[...] = back.astype(low)
    sums_out[...] = jnp.concatenate(sums + [grad_skip, jnp.zeros((2, LANES), wide)], 0)


def post_kernel(
    state_ref, step_ref, taps_ref, bias_ref, step_bias_ref, rate_ref, masks_ref, seg_col_ref,
    seg_row_ref, b_ref, c_ref, db_ref, dc_ref, dg_ref, z_ref, dt_ref,
    state_out, step_out, state_sums, step_sums, act_scr,
):
    rows, states = b_ref.shape
    masks = [masks_ref[k] for k in range(3)]
    triangle = lower_triangle()
    for c in range(rows // SPAN):
        at = slice(c * SPAN, (c + 1) * SPAN)
        seen = visible_block(seg_col_ref[at], seg_row_ref[:, at], False)
        grams = jnp.where(seen, dg_ref[at], 0.0)
        act_scr[0, at] = db_ref[at] + dot(grams.astype(low), c_ref[at])
        act_scr[1, at] = dc_ref[at] + dot(grams.T.astype(low), b_ref[at])
    for part in (0, 1):
        cols = slice(part * states, (part + 1) * states)
        v = state_ref[:, cols]
        pre = conv_in(v, taps_ref[:, cols], bias_ref[:, cols], masks)
        opened = sigmoid(pre)
        grad = act_scr[part] * opened * (1.0 + pre * (1.0 - opened))
        back, sums = conv_back(grad, v, taps_ref[:, cols], masks)
        state_out[:, cols] = back.astype(low)
        state_sums[:, cols] = jnp.concatenate(sums + [jnp.zeros((3, states), wide)], 0)
    pre = step_ref[...] + step_bias_ref[...]
    step = softplus(pre)
    rate_sum = jnp.zeros((1, LANES), wide)
    bias_sum = jnp.zeros((1, LANES), wide)
    for c in range(rows // SPAN):
        at = slice(c * SPAN, (c + 1) * SPAN)
        grad_rate = contract_rows(triangle, z_ref[at], highest)
        grad_step = (dt_ref[at] + rate_ref[...] * grad_rate) * sigmoid(pre[at])
        step_out[at] = grad_step.astype(low)
        rate_sum = rate_sum + jnp.sum(
            grad_rate * (rate_ref[...] * step[at]), axis=0, keepdims=True
        )
        bias_sum = bias_sum + jnp.sum(grad_step, axis=0, keepdims=True)
    step_sums[...] = jnp.concatenate([bias_sum, rate_sum, jnp.zeros((6, LANES), wide)], 0)


def call(
    kernel, outs, operands, grid=None, in_specs=None, out_specs=None, scratch=(), flops=0, aliases={}
):
    shapes = tuple(jax.ShapeDtypeStruct(shape, kind) for shape, kind in outs)
    moved = sum(a.size * a.dtype.itemsize for a in operands)
    moved += sum(s.size * s.dtype.itemsize for s in shapes)
    extra = {} if grid is None else dict(grid=grid, in_specs=in_specs, out_specs=out_specs)
    return pl.pallas_call(
        kernel,
        out_shape=shapes,
        scratch_shapes=list(scratch),
        compiler_params=pltpu.CompilerParams(vmem_limit_bytes=VMEM_BYTES),
        input_output_aliases=dict(aliases),
        cost_estimate=pl.CostEstimate(flops=flops, bytes_accessed=moved, transcendentals=0),
        **extra,
    )(*operands)


def column_block(rows, first=0):
    return pl.BlockSpec((rows, LANES), lambda i: (0, i + first))


def whole_block(shape):
    return pl.BlockSpec(shape, lambda i: (0,) * len(shape))


def lane_pad(v):
    return jnp.pad(v, ((0, 0), (0, LANES - v.shape[1])))


class Mixer:
    def __init__(
        self, state_in, step_in, conv_state, conv_state_bias, step_bias, decay_log, segments
    ):
        rows = state_in.shape[0]
        self.rows = rows
        self.head_count = step_bias.shape[0]
        self.pairs = (self.head_count + 1) // 2
        self.width = self.pairs * LANES
        self.states = conv_state.shape[1] // 2
        self.blocks = rows // SPAN
        before = [
            jnp.concatenate([jnp.full((k,), -1, jnp.int32), segments[: rows - k]]) == segments
            for k in (1, 2, 3)
        ]
        ends = segments.reshape(self.blocks, SPAN)[:, SPAN - 1]
        previous = jnp.concatenate([jnp.full((1,), -1, jnp.int32), ends[:-1]])
        carried = jnp.repeat(previous, SPAN) == segments
        tail = jnp.repeat(ends, SPAN) == segments
        flags = jnp.stack(before + [carried, tail]).astype(wide)
        self.masks = jnp.broadcast_to(flags[:, :, None], (5, rows, LANES))
        self.shared = (
            state_in,
            lane_pad(step_in),
            conv_state,
            conv_state_bias[None],
            lane_pad(step_bias[None]),
            lane_pad(-jnp.exp(decay_log)[None]),
            self.masks,
            segments[:, None],
            segments[None],
        )
        (
            self.b, self.c, self.bt, self.ct, self.g, self.gt, self.dtx, self.cumx, cumt,
        ) = call(
            prep_kernel,
            [((rows, self.states), low)] * 2
            + [((self.states, rows), low)] * 2
            + [((rows, SPAN), wide)] * 2
            + [((rows, self.width), wide)] * 2
            + [((LANES, rows), wide)],
            self.shared,
            flops=12 * rows * LANES * self.width,
        )
        self.cumt = cumt[: 2 * self.pairs].reshape(self.pairs, 2, rows)

    def widen(self, v):
        return jnp.pad(v, ((0, 0), (0, self.width - v.shape[1])))

    def forward(self, value_in, conv_value, conv_value_bias, skip_scale):
        rows, states = self.rows, self.states
        self.inner = value_in.shape[1]
        self.value = (
            self.widen(value_in),
            self.widen(conv_value),
            self.widen(conv_value_bias[None]),
            self.widen(jnp.repeat(skip_scale, HALF)[None]),
        )
        (mixed,) = call(
            fwd_kernel,
            [((rows, self.width), wide)],
            self.value + (self.dtx, self.cumx, self.cumt, self.masks, self.c, self.bt, self.g),
            grid=(self.pairs,),
            in_specs=[
                column_block(rows),
                column_block(4),
                column_block(1),
                column_block(1),
                column_block(rows),
                column_block(rows),
                pl.BlockSpec((1, 2, rows), lambda i: (i, 0, 0)),
                whole_block((5, rows, LANES)),
                whole_block((rows, states)),
                whole_block((states, rows)),
                whole_block((rows, SPAN)),
            ],
            out_specs=[column_block(rows)],
            scratch=[pltpu.VMEM((rows, LANES), wide)],
            flops=20 * rows * LANES * self.width,
        )
        self.mixed = mixed
        return mixed[:, : self.inner]

    def backward_part(self, grad_mixed, first, last, earlier=()):
        rows, states = self.rows, self.states
        operands = (
            (self.value[0], self.mixed, self.widen(grad_mixed))
            + self.value[1:]
            + (self.dtx, self.cumx, self.cumt, self.masks, self.b, self.c, self.bt, self.ct)
            + (self.gt,)
        )
        totals = [whole_block((rows, LANES))] * 5
        resumed = bool(earlier)
        return call(
            functools.partial(bwd_kernel, first, resumed),
            [((rows, self.width), low), ((8, self.width), wide)]
            + [((rows, LANES), wide)] * 5,
            operands + tuple(earlier),
            grid=(last - first,),
            in_specs=[
                column_block(rows, first),
                column_block(rows, first),
                column_block(rows, first),
                column_block(4, first),
                column_block(1, first),
                column_block(1, first),
                column_block(rows, first),
                column_block(rows, first),
                pl.BlockSpec((1, 2, rows), lambda i: (i + first, 0, 0)),
                whole_block((5, rows, LANES)),
                whole_block((rows, states)),
                whole_block((rows, states)),
                whole_block((states, rows)),
                whole_block((states, rows)),
                whole_block((rows, SPAN)),
            ]
            + ([pl.BlockSpec(memory_space=pl.ANY)] * 2 + totals if resumed else []),
            out_specs=[column_block(rows, first), column_block(8, first)] + totals,
            scratch=[pltpu.VMEM((rows, LANES), wide)] * 3
            + [pltpu.VMEM((self.blocks, states, LANES), wide)],
            flops=60 * rows * LANES * (last - first) * LANES,
            aliases={len(operands): 0, len(operands) + 1: 1} if resumed else {},
        )

    def backward_end(self, db, dc, dg, z, dt):
        rows, states = self.rows, self.states
        return call(
            post_kernel,
            [
                ((rows, 2 * states), low),
                ((rows, LANES), low),
                ((8, 2 * states), wide),
                ((8, LANES), wide),
            ],
            self.shared + (self.b, self.c, db, dc, dg, z, dt),
            scratch=[pltpu.VMEM((2, rows, states), wide)],
            flops=12 * rows * LANES * self.width,
        )

    def backward(self, grad_mixed):
        half = (self.pairs + 1) // 2
        part = self.backward_part(grad_mixed, 0, half)
        value_grad, sums, *totals = self.backward_part(grad_mixed, half, self.pairs, part)
        return self.gradients(value_grad, sums, *self.backward_end(*totals))

    def gradients(self, value_grad, sums, state_grad, step_grad, state_sums, step_sums):
        heads = self.head_count
        skip_grad = sums[5, : self.inner].reshape(heads, HALF).sum(axis=1)
        return (
            value_grad[:, : self.inner],
            state_grad,
            step_grad[:, :heads],
            sums[:4, : self.inner],
            sums[4, : self.inner],
            state_sums[:4],
            state_sums[4],
            step_sums[0, :heads],
            step_sums[1, :heads],
            skip_grad,
        )


def ring_place(index, count):
    return jnp.where(index % 2 == 0, index // 2, count - 1 - index // 2)


def ring_index(place, count):
    place = place % count
    return jnp.where(place < (count + 1) // 2, 2 * place, 2 * (count - 1 - place) + 1)


def ring_moves(count):
    order = list(range(0, count, 2)) + list(range(1, count, 2))[::-1]
    ahead = [(order[k], order[(k + 1) % count]) for k in range(count)]
    return ahead, [(target, source) for source, target in ahead]


class RingGather:
    def __init__(self, shard):
        self.count = lax.axis_size("gx")
        self.moves = ring_moves(self.count)
        me = lax.axis_index("gx")
        self.place = ring_place(me, self.count)
        self.rows, width = shard.shape
        self.half = self.rows // 2
        self.taken = 0
        self.held = (shard[: self.half], shard[self.half :])
        self.waiting = []
        full = jnp.zeros((self.count * self.rows, width), shard.dtype)
        self.full = lax.dynamic_update_slice(full, shard, (me * self.rows, 0))

    def step(self, times=1, place=True):
        for _ in range(min(times, self.count - 1 - self.taken)):
            self.taken += 1
            self.held = tuple(
                lax.ppermute(held, "gx", move) for held, move in zip(self.held, self.moves)
            )
            for piece, sign, offset in zip(self.held, (-1, 1), (0, self.half)):
                owner = ring_index(self.place + sign * self.taken, self.count)
                self.waiting.append((piece, owner * self.rows + offset))
            if place:
                if len(self.waiting) > 2:
                    self.held, self.full = lax.optimization_barrier((self.held, self.full))
                for piece, start in self.waiting:
                    self.full = lax.dynamic_update_slice(self.full, piece, (start, 0))
                self.waiting = []
        return self.held

    def finish(self):
        self.step(self.count)
        return self.full


class RingSum:
    def __init__(self, partial):
        self.count = lax.axis_size("gx")
        self.moves = ring_moves(self.count)
        self.place = ring_place(lax.axis_index("gx"), self.count)
        self.rows = partial.shape[0] // self.count
        self.half = self.rows // 2
        self.partial = partial
        self.taken = 0
        self.held = (self.part(-1, 0), self.part(1, self.half))

    def part(self, target, offset):
        start = ring_index(self.place + target, self.count) * self.rows + offset
        return lax.dynamic_slice_in_dim(self.partial, start, self.half, 0)

    def step(self, times=1):
        for _ in range(min(times, self.count - 1 - self.taken)):
            self.taken += 1
            up, down = (
                lax.ppermute(held, "gx", move).astype(wide)
                for held, move in zip(self.held, self.moves)
            )
            up = up + self.part(-1 - self.taken, 0).astype(wide)
            down = down + self.part(1 + self.taken, self.half).astype(wide)
            if self.taken < self.count - 1:
                up, down = up.astype(low), down.astype(low)
            self.held = (up, down)
        return self.held

    def finish(self):
        return jnp.concatenate(self.step(self.count), 0)


def flips(count, bit):
    return [(k, k ^ bit) for k in range(count)]


def butterfly_sum(v, axis):
    count = lax.axis_size(axis)
    bit = 1
    while bit < count:
        v = v + lax.ppermute(v, axis, flips(count, bit))
        bit *= 2
    return v


def scatter_rows(partial):
    return lax.psum_scatter(partial, "gx", scatter_dimension=0, tiled=True)


def row_major(v):
    return with_layout_constraint(v, Layout((0, 1)))


def together(*values):
    return lax.optimization_barrier(values)


def tie(value, *rings):
    value, held = lax.optimization_barrier((value, [ring.held for ring in rings]))
    for ring, pieces in zip(rings, held):
        ring.held = tuple(pieces)
    return value


def on_device(
    layer_input,
    norm_gain,
    gate_weight,
    value_weight,
    state_weight,
    step_weight,
    conv_value,
    conv_value_bias,
    conv_state,
    conv_state_bias,
    step_bias,
    decay_log,
    skip_scale,
    gated_gain,
    out_weight,
    segment_ids,
    cotangent,
):
    model_width = layer_input.shape[1]
    col_width = cotangent.shape[1]
    state_cols = state_weight.shape[1]
    col_start = lax.axis_index("gy") * col_width

    inner = gate_weight.shape[1]
    upstream = lax.all_gather(cotangent, "gy", axis=1, tiled=True)
    value_gather = RingGather(jnp.concatenate([value_weight, state_weight, step_weight], 1))
    value_gather.step()
    tokens = tie(layer_input, value_gather).astype(wide)
    scale_in = lax.rsqrt(jnp.mean(tokens * tokens, axis=1, keepdims=True) + epsilon)
    normed = (tokens * scale_in * norm_gain).astype(low)
    value_gather.step()
    normed = tie(normed, value_gather)
    full_value_state = value_gather.finish()

    gate_gather = RingGather(tie(gate_weight, value_gather))
    gate_gather.step(place=False)
    normed = tie(normed, gate_gather)
    state_step = dot(normed, full_value_state[:, inner:])
    mixer = Mixer(
        state_step[:, :state_cols],
        state_step[:, state_cols:],
        conv_state,
        conv_state_bias,
        step_bias,
        decay_log,
        segment_ids,
    )
    gate_gather.step(place=False)
    normed, mixer.g = together(normed, mixer.g)
    normed = tie(normed, gate_gather)
    value_in = dot(normed, full_value_state[:, :inner])
    gate_gather.step(place=False)
    value_in = tie(value_in, gate_gather)
    mixed = mixer.forward(value_in, conv_value, conv_value_bias, skip_scale)
    gate_gather.step(place=False)
    mixed = mixer.mixed = tie(mixer.mixed, gate_gather)
    mixed = mixed[:, : mixer.inner]
    full_gate = gate_gather.finish()
    out_gather = RingGather(tie(out_weight.T, gate_gather))
    out_gather.step(place=False)
    normed = tie(normed, out_gather)
    gate_in = dot(normed, full_gate)
    out_gather.step(place=False)
    gate_in = tie(gate_in, out_gather)
    full_out = out_gather.finish()
    up_back = dot(upstream, full_out)
    gate_open = jax.nn.sigmoid(gate_in)
    gate_act = gate_in * gate_open
    gated = mixed * gate_act

    sums_out = lax.psum(
        jnp.stack(
            [jnp.sum(gated * gated, axis=1), jnp.sum(gated * gated_gain * up_back, axis=1)]
        ),
        "gy",
    )
    scale_out = lax.rsqrt(sums_out[0] / INNER + epsilon)[:, None]
    grad_scale = sums_out[1][:, None]
    scaled = (gated * gated_gain).astype(low)

    scaled_out = (gated * gated_gain * scale_out).astype(low)
    out_ring = RingSum(row_major(contract_rows(upstream, scaled_out).astype(low)))

    scaled = tie(scaled, out_ring)
    product_part = contract_cols(full_out, scaled)
    product_part = row_major((product_part * scale_out[:, 0]).astype(low))
    product = lax.psum_scatter(product_part, "gy", scatter_dimension=0, tiled=True)

    out_ring.step()
    up_back, product_part = together(up_back, product_part)
    grad_scaled = scale_out * tie(up_back, out_ring)
    grad_gated = grad_scaled * gated_gain - grad_scale * scale_out**3 * gated / INNER
    gate_gain_part = jnp.sum(grad_scaled * gated, axis=0)
    grad_gate_in = (
        grad_gated * mixed * gate_open * (1.0 + gate_in * (1.0 - gate_open))
    ).astype(low)
    grad_mixed = grad_gated * gate_act
    out_ring.step()
    normed = tie(normed, out_ring)
    gate_ring = RingSum(row_major(contract_rows(normed, grad_gate_in).astype(low)))

    first = (mixer.pairs + 2) // 3
    second = (first + mixer.pairs + 1) // 2
    out_ring.step()
    grad_mixed = tie(grad_mixed, out_ring, gate_ring)
    part = mixer.backward_part(grad_mixed, 0, first)
    out_ring.step()
    gate_ring.step()
    grad_mixed = tie(grad_mixed, out_ring, gate_ring)
    part = mixer.backward_part(grad_mixed, first, second, part)
    out_ring.step()
    gate_ring.step()
    grad_mixed = tie(grad_mixed, out_ring, gate_ring)
    value_grad, value_sums, *totals = mixer.backward_part(grad_mixed, second, mixer.pairs, part)
    grad_value_in = value_grad[:, : gate_weight.shape[1]]
    out_ring.step()
    gate_ring.step()
    normed = tie(normed, out_ring, gate_ring)
    value_ring = RingSum(row_major(contract_rows(normed, grad_value_in).astype(low)))
    out_ring.step()
    gate_ring.step()
    totals[0] = tie(totals[0], out_ring, gate_ring, value_ring)
    ends = mixer.backward_end(*totals)
    pulled = mixer.gradients(value_grad, value_sums, *ends)
    grad_state_in = jnp.concatenate([pulled[1], pulled[2]], 1)
    state_partial = row_major(contract_rows(normed, grad_state_in).astype(low))
    grad_state_step = scatter_rows(state_partial).astype(wide)

    value_ring.step()
    grad_gate_in = tie(grad_gate_in, value_ring)
    grad_normed_part = contract_cols(full_gate, grad_gate_in)
    grad_value_state_in = jnp.concatenate([grad_value_in, grad_state_in], 1)
    out_ring.step()
    gate_ring.step()
    grad_value_state_in = tie(grad_value_state_in, out_ring, gate_ring)
    grad_value_state_in, product = together(grad_value_state_in, product)
    grad_normed_part = grad_normed_part + contract_cols(full_value_state, grad_value_state_in)
    grad_normed_part = row_major(grad_normed_part.astype(low))
    grad_out = out_ring.finish()
    grad_gate = gate_ring.finish()
    grad_value = value_ring.finish()

    grad_normed = lax.psum_scatter(
        grad_normed_part, "gy", scatter_dimension=0, tiled=True
    ).T.astype(wide)
    token_cols = lax.dynamic_slice_in_dim(layer_input, col_start, col_width, 1).astype(wide)
    gain_cols = lax.dynamic_slice_in_dim(norm_gain, col_start, col_width, 0)
    weighted = grad_normed * gain_cols
    inner_dot = lax.psum(jnp.sum(weighted * token_cols, axis=1), "gy")[:, None]
    grad_input = (
        cotangent.astype(wide)
        + scale_in * weighted
        - token_cols * scale_in**3 * inner_dot / model_width
    )
    grad_norm_gain = butterfly_sum(jnp.sum(grad_normed * token_cols * scale_in, axis=0), "gx")
    layer_output = (token_cols + product.T.astype(wide)).astype(low)

    small = (gate_gain_part,) + pulled[3:]
    packed = jnp.concatenate([v.reshape(-1) for v in small])
    packed = butterfly_sum(packed, "gx")
    sums, start = [], 0
    for v in small:
        sums.append(packed[start : start + v.size].reshape(v.shape))
        start += v.size
    state_sums = butterfly_sum(
        jnp.concatenate([grad_state_step[:, :state_cols], sums[3], sums[4][None]], 0), "gy"
    )
    state_rows = state_weight.shape[0]
    return (
        layer_output,
        grad_input,
        grad_norm_gain,
        grad_gate,
        grad_value,
        state_sums[:state_rows],
        grad_state_step[:, state_cols:],
        sums[1],
        sums[2],
        state_sums[state_rows:-1],
        state_sums[-1],
        sums[5],
        sums[6],
        sums[7],
        sums[0],
        grad_out.T,
    )


def solution(mesh):
    return jax.shard_map(
        on_device,
        mesh=mesh,
        in_specs=(
            P("gx", None),
            P(),
            P("gx", "gy"),
            P("gx", "gy"),
            P("gx", None),
            P("gx", "gy"),
            P(None, "gy"),
            P("gy"),
            P(),
            P(),
            P("gy"),
            P("gy"),
            P("gy"),
            P("gy"),
            P("gy", "gx"),
            P("gx"),
            P("gx", "gy"),
        ),
        out_specs=(
            P("gx", "gy"),
            P("gx", "gy"),
            P("gy"),
            P("gx", "gy"),
            P("gx", "gy"),
            P("gx", None),
            P("gx", "gy"),
            P(None, "gy"),
            P("gy"),
            P(),
            P(),
            P("gy"),
            P("gy"),
            P("gy"),
            P("gy"),
            P("gy", "gx"),
        ),
        check_vma=False,
    )
```
